32 devices in a mesh: grp: 4 (over x, core), ep: 8 (over z, y).
Axes of the slice: x: 2, y: 2, z: 4, core: 2. Of those that a mesh axis runs over, the one named last changes fastest.
Arguments:
- queries: bfloat16 [3, 128, 128, 576], P(None, ('grp', 'ep')), may hold values from -10 to 10, as said below
- cache: bfloat16 [128, 128, 576], P(('grp', 'ep')), may hold values from -5 to 5, as said below
- new_entries: bfloat16 [3, 128, 576], P(None, ('grp', 'ep')), may hold values from -5 to 5
- lengths: int32 [128], P(('grp', 'ep')), may hold values from 2 to 125, as said below
- moe_input: bfloat16 [3, 128, 3584], P(None, ('grp', 'ep')), may hold values from -6 to 6
- expert_ids: int32 [3, 4, 32, 8], P(None, None, 'ep'), may hold values from 0 to 7, all different within a row; in each aligned block of 4 rows (0 to 3, 4 to 7, ..., all dimensions but the last counted through in order) at most 4 rows name the same one
- route_gains: float32 [3, 4, 32, 8], P(None, None, 'ep'), may hold values from 0.1 to 1
- w_gate: bfloat16 [8, 3584, 2048], P('ep', None, 'grp'), may hold values from -0.09375 to 0.09375
- w_up: bfloat16 [8, 3584, 2048], P('ep', None, 'grp'), may hold values from -0.09375 to 0.09375
- w_down: bfloat16 [8, 2048, 3584], P('ep', 'grp'), may hold values from -0.125 to 0.125
- plan: int32 [4, 8, 2, 2], P(None, 'ep'), may hold values from 0 to 3, as said below
Outputs:
- contexts: bfloat16 [3, 128, 128, 512], P(None, ('grp', 'ep'))
- migrated_cache: bfloat16 [128, 128, 576], P(('grp', 'ep'))
- moe_output: bfloat16 [3, 128, 3584], P(None, ('grp', 'ep'))
The draws below stay inside these ranges and needn't reach their ends.
Inputs may be any that keep to these rules, and one draw needn't show every extreme that they name: `queries`: queries lie in this range. `cache`: cache entries lie in this range. `lengths`: some trace has exactly 125 filled rows. `expert_ids`: within the 4 tokens of one device in one step, no expert is named by more than 4 tokens. plan[g, e, k] = (slot, grp index d): device (g, e) sends the trace in that slot to device (d, e). A device's 2 slots differ; its destinations differ from each other and from g. For each k, every device of an ep index is the destination of exactly one device's entry k, and the trace lands in the slot that the destination lists in its own entry k.
All inputs are finite; a program needn't handle non-finite values.
Results may differ from the reference program's by a relative error of at most 0.019.
Values may be sent and summed in bfloat16 or wider, within the bound.
No kernel may reach another device: no remote copies, remote signals or barrier semaphores. Data moves between devices by JAX's collectives and lax.ppermute only.
A program may use at most 128 MiB of HBM per device.

```python
import math
import jax
import jax.numpy as jnp
import numpy as np
from jax import lax

D = 3584
HEADS = 128
LAT = 512
MOE_HID = 2048
TOPK = 8
STEPS = 3
MIG = 2
TR_DEV = 4
CAP = 128
KVDIM = 576
EXPERTS = 8
HID_DEV = 512
CAP_E = 4
TRACES = 128
MAXLEN = 125
N_GRP = 4
N_EP = 8


def draw_queries(key, part):
    array_shape = (STEPS, TRACES, HEADS, KVDIM)
    values = jnp.clip(jax.random.normal(key, array_shape, jnp.float32), -5.0, 5.0)
    return values.astype(jnp.bfloat16)


def draw_cache(key, part):
    array_shape = (TRACES, CAP, KVDIM)
    values = jnp.clip(jax.random.normal(key, array_shape, jnp.float32), -5.0, 5.0)
    return values.astype(jnp.bfloat16)


def draw_lengths(key, part):
    key_kind, key_long, key_short, key_top = jax.random.split(key, 4)
    long_trace = jax.random.randint(key_kind, (TRACES,), 0, 4) == 0
    long_length = jax.random.randint(key_long, (TRACES,), 2, MAXLEN + 1)
    short_length = jax.random.randint(key_short, (TRACES,), 2, MAXLEN // 4 + 3)
    longest = jax.random.randint(key_top, (), 0, TRACES)
    result = jnp.where(long_trace, long_length, short_length)
    result = jnp.where(jnp.arange(TRACES) == longest, MAXLEN, result)
    return result.astype(jnp.int32)


def draw_plan(key, part):
    key_offset, key_slots = jax.random.split(key)
    offset_keys = jax.random.split(key_offset, N_EP)
    offsets = jax.vmap(lambda one_key: jax.random.permutation(one_key, N_GRP - 1)[:MIG] + 1)(offset_keys)
    slot_keys = jax.random.split(key_slots, N_GRP * N_EP)
    slots_out = jax.vmap(lambda one_key: jax.random.permutation(one_key, TR_DEV)[:MIG])(slot_keys).reshape(N_GRP, N_EP, MIG)
    destination = (jnp.arange(N_GRP)[:, None, None] + offsets[None, :, :]) % N_GRP
    return jnp.stack([slots_out, destination], axis=3).astype(jnp.int32)


def steps_of(rng, shape, shards, low, largest):
    gain = 1.0
    for position, blocks in shards:
        heights = jax.random.uniform(jax.random.fold_in(jax.random.fold_in(rng, 6), position), (blocks,), jnp.float32, low / len(shards), largest / len(shards))
        gain = gain * jnp.repeat(jnp.exp(heights), shape[position] // blocks).reshape((-1,) + (1,) * (len(shape) - 1 - position))
    return gain


def assign_block(own_key, own, number, rows, count, top, bound, slope):
    sequence = jax.random.permutation(own_key, count)
    packed, common = load_shares(count, rows * top, bound, slope, True), load_shares(count, rows * top, bound, slope, False)
    places = jnp.arange(count)

    def named(tallies, rotation):
        used = int((tallies > 0).sum())
        fixed = max(1, used // 4)
        moved = fixed + (places - fixed + rotation * (used - fixed)) % max(1, count - fixed)
        return jnp.zeros((count,), jnp.int32).at[sequence[jnp.where(places < fixed, places, moved)]].set(jnp.asarray(tallies, jnp.int32))

    tallies = jnp.where(number % 4 == 0, named(packed, number // 4), named(common, number - number // 4 - 1))
    mixed = jax.random.permutation(jax.random.fold_in(own, 3), count)
    giver, taker = mixed[0:count // 2 * 2:2], mixed[1:count // 2 * 2:2]
    room = jnp.minimum(tallies[giver] - 1, bound - tallies[taker]) // 2
    room = jnp.where((giver == sequence[0]) | (taker == sequence[0]) | (tallies[taker] == 0), 0, jnp.maximum(room, 0))
    moved = jax.random.randint(jax.random.fold_in(own, 4), (count // 2,), 0, 1 << 20) % (room + 1)
    tallies = tallies.at[giver].add(-moved).at[taker].add(moved)
    labels = jnp.searchsorted(jnp.cumsum(tallies), jnp.arange(rows * top), side="right").astype(jnp.int32)
    table = labels.reshape(top, rows).T
    table = table[jax.random.permutation(jax.random.fold_in(own, 1), rows)]
    rotation = jax.random.randint(jax.random.fold_in(own, 2), (rows, 1), 0, top)
    return jnp.take_along_axis(table, (jnp.arange(top)[None, :] + rotation) % top, axis=1)


def load_shares(amount, total, limit, skew, full):
    weights = [(1 << 20) // math.isqrt(grade ** skew) + 1 for grade in range(1, amount + 1)]
    largest = limit if full else min(limit, max(-(-total // amount), total * weights[0] // sum(weights)))
    least = 1 if total - largest >= amount - 1 else 0
    counts, rest = [largest] + [least] * (amount - 1), total - largest - least * (amount - 1)
    while rest > 0:
        candidates = [i for i in range(1, amount) if counts[i] < largest] or [i for i in range(1, amount) if counts[i] < limit]
        pool, left = sum([weights[i] for i in candidates]), rest
        for i in candidates:
            addition = min(limit - counts[i], max(1, left * weights[i] // pool), rest)
            counts[i] = counts[i] + addition
            rest = rest - addition
    return np.array(counts)


def gaussian(stream_key, extent, scale, most, shards=(), kind=jnp.bfloat16):
    values = scale * jax.random.normal(stream_key, extent, jnp.float32)
    if shards:
        values = values * steps_of(stream_key, extent, shards, -0.22, 0.18)
    return jnp.clip(values, -most, most).astype(kind)


def setup_inputs(seed: int = 0) -> dict:
    arg_keys = jax.random.split(jax.random.key(seed), 12)
    queries = draw_queries(jax.random.fold_in(arg_keys[11], 71), 0)
    cache = draw_cache(jax.random.fold_in(arg_keys[11], 71), 0)
    new_entries = gaussian(arg_keys[2], (STEPS, TRACES, KVDIM), 1.0, 5.0, ((1, 32),))
    lengths = draw_lengths(jax.random.fold_in(arg_keys[11], 71), 0)
    moe_input = gaussian(arg_keys[4], (STEPS, TRACES, D), 1.0, 6.0, ((1, 32),))
    expert_ids_keys = jax.random.split(jax.random.fold_in(arg_keys[5], 1), STEPS * N_GRP * (N_EP * TR_DEV) // TR_DEV)
    expert_ids_turns = jax.random.permutation(jax.random.fold_in(arg_keys[5], 3), STEPS * N_GRP * (N_EP * TR_DEV) // TR_DEV)
    expert_ids = jax.vmap(lambda own, number: assign_block(jax.random.fold_in(arg_keys[5], 2), own, number, TR_DEV, EXPERTS, TOPK, CAP_E, 2))(expert_ids_keys, expert_ids_turns).reshape((STEPS, N_GRP, N_EP * TR_DEV, TOPK))
    route_gains = jnp.clip(jnp.exp(math.log(1.0) - 2.3025851 * jax.random.uniform(arg_keys[6], (STEPS, N_GRP, N_EP * TR_DEV, TOPK), jnp.float32) ** steps_of(arg_keys[6], (STEPS, N_GRP, N_EP * TR_DEV, TOPK), ((2, 8),), -0.2, 0.2)), 0.1, 1.0)
    w_gate = gaussian(arg_keys[7], (EXPERTS, D, MOE_HID), D ** -0.5, 0.09375, ((0, 8), (2, 4)))
    w_up = gaussian(arg_keys[8], (EXPERTS, D, MOE_HID), D ** -0.5, 0.09375, ((0, 8), (2, 4)))
    w_down = gaussian(arg_keys[9], (EXPERTS, MOE_HID, D), MOE_HID ** -0.5, 0.125, ((0, 8), (1, 4)))
    plan = draw_plan(jax.random.fold_in(arg_keys[11], 71), 0)
    return dict(queries=queries, cache=cache, new_entries=new_entries, lengths=lengths, moe_input=moe_input, expert_ids=expert_ids, route_gains=route_gains, w_gate=w_gate, w_up=w_up, w_down=w_down, plan=plan)


SCORE_SCALE = 192.0 ** -0.5


def attend_trace(trace_index, queries, cache, new_entries, lengths):
    trace_cache = cache[trace_index]
    trace_length = lengths[trace_index]
    positions = jnp.arange(trace_cache.shape[0], dtype=jnp.int32)
    outputs = []
    for step_index in range(queries.shape[0]):
        filled = trace_length + step_index
        trace_cache = jnp.where((positions == filled)[:, None], new_entries[step_index, trace_index][None, :], trace_cache)
        scores = jnp.einsum("hd,cd->hc", queries[step_index, trace_index].astype(jnp.float32), trace_cache.astype(jnp.float32)) * SCORE_SCALE
        scores = jnp.where((positions <= filled)[None, :], scores, -jnp.inf)
        top_score = jnp.max(scores, axis=1, keepdims=True)
        exp_scores = jnp.exp(scores - top_score)
        weights = (exp_scores / jnp.sum(exp_scores, axis=1, keepdims=True)).astype(jnp.bfloat16)
        context = jnp.dot(weights, trace_cache[:, :LAT], preferred_element_type=jnp.float32)
        outputs.append(context.astype(jnp.bfloat16))
    return jnp.stack(outputs), trace_cache


def expert_layer(tokens, route_ids, route_gains, w_gate, w_up, w_down):
    most_rows = N_GRP * N_EP * CAP_E

    def per_expert(running, inputs):
        expert_index, gate_weight, up_weight, down_weight = inputs
        matched = route_ids == expert_index
        row_weight = jnp.sum(jnp.where(matched, route_gains, 0.0), axis=1)
        chosen = jnp.any(matched, axis=1)
        row_order = jnp.argsort(jnp.where(chosen, 0, 1).astype(jnp.int32), stable=True)[:most_rows].astype(jnp.int32)
        token_rows = tokens[row_order]
        gate_out = jnp.dot(token_rows, gate_weight, preferred_element_type=jnp.float32)
        up_out = jnp.dot(token_rows, up_weight, preferred_element_type=jnp.float32)
        hidden = (jax.nn.silu(gate_out) * up_out).astype(jnp.bfloat16)
        blocks = hidden.reshape(most_rows, N_GRP, HID_DEV).astype(jnp.float32)
        down_blocks = down_weight.reshape(N_GRP, HID_DEV, D).astype(jnp.float32)
        partial_sums = jnp.einsum("rbh,bhd->rbd", blocks, down_blocks, precision=lax.Precision.HIGHEST)
        partial_sums = lax.optimization_barrier(partial_sums.astype(jnp.bfloat16)).astype(jnp.float32)
        expert_out = jnp.sum(partial_sums, axis=1)
        running = running.at[row_order].add(row_weight[row_order][:, None] * expert_out)
        return running, None

    start_sum = jnp.zeros((tokens.shape[0], D), jnp.float32)
    expert_list = jnp.arange(EXPERTS, dtype=jnp.int32)
    running, unused = lax.scan(per_expert, start_sum, (expert_list, w_gate, w_up, w_down))
    return running.astype(jnp.bfloat16)


def reference(queries, cache, new_entries, lengths, moe_input, expert_ids, route_gains, w_gate, w_up, w_down, plan):
    trace_list = jnp.arange(TRACES, dtype=jnp.int32)
    contexts, grown_cache = lax.map(lambda trace_index: attend_trace(trace_index, queries, cache, new_entries, lengths), trace_list)
    contexts = jnp.transpose(contexts, (1, 0, 2, 3))
    grid_group = jnp.arange(N_GRP, dtype=jnp.int32)[:, None, None]
    grid_expert = jnp.arange(N_EP, dtype=jnp.int32)[None, :, None]
    grid_entry = jnp.arange(MIG, dtype=jnp.int32)[None, None, :]
    dest_group = plan[:, :, :, 1]
    source_index = (grid_group * N_EP + grid_expert) * TR_DEV + plan[:, :, :, 0]
    dest_slot = plan[dest_group, grid_expert, grid_entry, 0]
    dest_index = (dest_group * N_EP + grid_expert) * TR_DEV + dest_slot
    migrated_cache = grown_cache.at[dest_index.reshape(-1).astype(jnp.int32)].set(grown_cache[source_index.reshape(-1).astype(jnp.int32)])
    moe_steps = []
    for step_index in range(STEPS):
        step_ids = expert_ids[step_index].reshape(TRACES, TOPK)
        step_gains = route_gains[step_index].reshape(TRACES, TOPK)
        moe_steps.append(expert_layer(moe_input[step_index], step_ids, step_gains, w_gate, w_up, w_down))
    moe_output = jnp.stack(moe_steps)
    return contexts, migrated_cache, moe_output
```

```python
from functools import partial

import jax
import jax.numpy as jnp
from jax import lax
from jax.experimental import pallas as pl
from jax.experimental.pallas import tpu as pltpu
from jax.sharding import PartitionSpec as P

ROPE = 64


SCORE_SCALE = 192.0 ** (-0.5)


BOTH = ("grp", "ep")


GAIN_LANES = 128


STEP_CHUNKS = ((0, 1), (1, 3))


def across(values, grp_flip, ep_flip):
    groups, columns = lax.axis_size("grp"), lax.axis_size("ep")
    pairs = [
        (g * columns + e, (g ^ grp_flip) * columns + (e ^ ep_flip))
        for g in range(groups)
        for e in range(columns)
    ]
    return lax.ppermute(values, BOTH, pairs)


def attention_kernel(
    lengths_ref, source_ref, queries_ref, cache_ref, entries_ref, *rest
):
    received_refs, (contexts_ref, migrated_ref) = rest[:-2], rest[-2:]
    trace = pl.program_id(0)
    filled = lengths_ref[trace]
    step_count, _, heads, width = queries_ref.shape
    latent = contexts_ref.shape[3]
    capacity = cache_ref.shape[1]
    keys = cache_ref[0].astype(jnp.float32)
    row_index = lax.broadcasted_iota(jnp.int32, keys.shape, 0)
    for step_index in range(step_count):
        entry_rows = entries_ref[step_index].astype(jnp.float32)
        entry_index = lax.broadcasted_iota(jnp.int32, entry_rows.shape, 0)
        entry = jnp.sum(jnp.where(entry_index == trace, entry_rows, 0.0), axis=0, keepdims=True)
        keys = jnp.where(row_index == filled + step_index, entry, keys)
    keys = keys.astype(jnp.bfloat16)
    source = source_ref[trace]

    @pl.when(source == 0)
    def _():
        migrated_ref[0] = keys

    for number, received_ref in enumerate(received_refs):

        @pl.when(source == number + 1)
        def _(received_ref=received_ref):
            migrated_ref[0] = received_ref[...]

    flat_queries = queries_ref[...].reshape(step_count * heads, width)
    scores = (
        lax.dot_general(
            flat_queries, keys, (((1,), (1,)), ((), ())), preferred_element_type=jnp.float32
        )
        * SCORE_SCALE
    )
    step_of_row = lax.broadcasted_iota(jnp.int32, (step_count, heads, capacity), 0).reshape(
        step_count * heads, capacity
    )
    position = lax.broadcasted_iota(jnp.int32, scores.shape, 1)
    scores = jnp.where(position <= filled + step_of_row, scores, -jnp.inf)
    exp_scores = jnp.exp(scores - jnp.max(scores, axis=1, keepdims=True))
    weights = (exp_scores / jnp.sum(exp_scores, axis=1, keepdims=True)).astype(jnp.bfloat16)
    context = jnp.dot(weights, keys[:, :latent], preferred_element_type=jnp.float32)
    contexts_ref[...] = context.astype(jnp.bfloat16).reshape(contexts_ref.shape)


def attention(queries, cache, new_entries, lengths, source, received):
    step_count, traces, heads, width = queries.shape
    capacity = cache.shape[1]
    latent = width - ROPE
    whole = lambda shape: pl.BlockSpec(shape, lambda t, *_: (0,) * len(shape))
    return pl.pallas_call(
        attention_kernel,
        grid_spec=pltpu.PrefetchScalarGridSpec(
            num_scalar_prefetch=2,
            grid=(traces,),
            in_specs=[
                pl.BlockSpec((step_count, 1, heads, width), lambda t, *_: (0, t, 0, 0)),
                pl.BlockSpec((1, capacity, width), lambda t, *_: (t, 0, 0)),
                whole(new_entries.shape),
            ]
            + [whole((capacity, width))] * len(received),
            out_specs=[
                pl.BlockSpec((step_count, 1, heads, latent), lambda t, *_: (0, t, 0, 0)),
                pl.BlockSpec((1, capacity, width), lambda t, *_: (t, 0, 0)),
            ],
        ),
        out_shape=[
            jax.ShapeDtypeStruct((step_count, traces, heads, latent), jnp.bfloat16),
            jax.ShapeDtypeStruct(cache.shape, jnp.bfloat16),
        ],
        cost_estimate=pl.CostEstimate(
            flops=2 * step_count * traces * heads * capacity * (width + latent),
            bytes_accessed=2 * (queries.size * 2 + cache.size * 2),
            transcendentals=step_count * traces * heads * capacity,
        ),
        name="attention",
    )(lengths, source, queries, cache, new_entries, *received)


def migrate(cache, new_entries, lengths, plan):
    traces, capacity, _ = cache.shape
    groups = lax.axis_size("grp")
    group_index = lax.axis_index("grp")
    column_plan = plan[:, 0]
    own_plan = lax.dynamic_index_in_dim(column_plan, group_index, 0, keepdims=False)
    slot_list = jnp.arange(traces, dtype=jnp.int32)
    positions = jnp.arange(capacity, dtype=jnp.int32)
    source = jnp.zeros((traces,), jnp.int32)
    received = []
    for flip in range(1, groups):
        partner = group_index ^ flip
        slot = jnp.sum(jnp.where(own_plan[:, 1] == partner, own_plan[:, 0], 0))
        rows = lax.dynamic_index_in_dim(cache, slot, 0, keepdims=False)
        filled = lax.dynamic_index_in_dim(lengths, slot, 0, keepdims=False)
        entries = lax.dynamic_index_in_dim(new_entries, slot, 1, keepdims=False)
        for step_index in range(new_entries.shape[0]):
            rows = jnp.where(
                (positions == filled + step_index)[:, None], entries[step_index][None, :], rows
            )
        received.append(across(rows, flip, 0))
        partner_plan = lax.dynamic_index_in_dim(column_plan, partner, 0, keepdims=False)
        lands = (partner_plan[:, 1] == group_index)[None, :] & (
            own_plan[:, 0][None, :] == slot_list[:, None]
        )
        source = jnp.where(jnp.any(lands, axis=1), flip, source)
    return received, source


def expert_kernel(tile, column_ref, *refs):
    pieces = refs[:-12]
    gate_hbm, up_hbm, down_hbm, own_ref, other_ref = refs[-12:-7]
    gate_ref, up_ref, down_ref, gate_sum, up_sum, hidden_ref, semaphores = refs[-7:]
    width, hidden_width = gate_ref.shape
    tiles = width // tile
    piece_rows = pieces[0].shape[0]
    half = own_ref.shape[0]
    copies = []
    for index in range(tiles):
        rows = pl.ds(index * tile, tile)
        copies.append(
            (
                pltpu.make_async_copy(gate_hbm.at[0, rows], gate_ref.at[rows], semaphores.at[0, index]),
                pltpu.make_async_copy(up_hbm.at[0, rows], up_ref.at[rows], semaphores.at[1, index]),
            )
        )
    down_copies = []
    for index in range(tiles):
        columns = pl.ds(index * tile, tile)
        down_copies.append(
            pltpu.make_async_copy(
                down_hbm.at[0, :, columns], down_ref.at[:, columns], semaphores.at[2, index]
            )
        )
    for pair in copies:
        for copy in pair:
            copy.start()
    for copy in down_copies:
        copy.start()
    gain_parts = jnp.concatenate([piece[:, width:] for piece in pieces], axis=0).astype(jnp.float32)
    lane = lax.broadcasted_iota(jnp.int32, gain_parts.shape, 1)
    first_lane = column_ref[0] * 3
    gain = jnp.sum(
        jnp.where((lane >= first_lane) & (lane < first_lane + 3), gain_parts, 0.0),
        axis=1,
        keepdims=True,
    )
    for index in range(tiles):
        rows = slice(index * tile, (index + 1) * tile)
        tokens = jnp.concatenate([piece[:, rows] for piece in pieces], axis=0)
        for copy, weight_ref, sum_ref in zip(copies[index], (gate_ref, up_ref), (gate_sum, up_sum)):
            copy.wait()
            product = jnp.dot(tokens, weight_ref[rows, :], preferred_element_type=jnp.float32)
            if index == 0:
                sum_ref[...] = product
            else:
                sum_ref[...] += product
    gate_out = gate_sum[...]
    hidden = gate_out / (1.0 + jnp.exp(-gate_out)) * up_sum[...] * gain
    hidden_ref[...] = hidden.astype(jnp.bfloat16)
    for index in range(tiles):
        columns = slice(index * tile, (index + 1) * tile)
        down_copies[index].wait()
        for number, out_ref in enumerate((own_ref, other_ref)):
            out_ref[:, columns] = jnp.dot(
                hidden_ref[number * half : (number + 1) * half, :],
                down_ref[:, columns],
                preferred_element_type=jnp.float32,
            ).astype(jnp.bfloat16)


def expert(pieces, w_gate, w_up, w_down):
    _, width, hidden_width = w_gate.shape
    token_count = sum(piece.shape[0] for piece in pieces)
    tile = width // 4 if width % 512 == 0 else width
    vmem = pl.BlockSpec(memory_space=pltpu.VMEM)
    half = jax.ShapeDtypeStruct((token_count // 2, width), jnp.bfloat16)
    column = lax.axis_index("ep").astype(jnp.int32).reshape(1)
    return pl.pallas_call(
        partial(expert_kernel, tile),
        in_specs=[pl.BlockSpec(memory_space=pltpu.SMEM)]
        + [vmem] * len(pieces)
        + [pl.BlockSpec(memory_space=pl.ANY)] * 3,
        out_specs=[vmem, vmem],
        out_shape=[half, half],
        scratch_shapes=[
            pltpu.VMEM((width, hidden_width), jnp.bfloat16),
            pltpu.VMEM((width, hidden_width), jnp.bfloat16),
            pltpu.VMEM((hidden_width, width), jnp.bfloat16),
            pltpu.VMEM((token_count, hidden_width), jnp.float32),
            pltpu.VMEM((token_count, hidden_width), jnp.float32),
            pltpu.VMEM((token_count, hidden_width), jnp.bfloat16),
            pltpu.SemaphoreType.DMA((3, width // tile)),
        ],
        compiler_params=pltpu.CompilerParams(vmem_limit_bytes=40 * 1024 * 1024),
        cost_estimate=pl.CostEstimate(
            flops=6 * token_count * width * hidden_width,
            bytes_accessed=6 * width * hidden_width + 4 * token_count * width,
            transcendentals=token_count * hidden_width,
        ),
        name="expert",
    )(column, *pieces, w_gate, w_up, w_down)


def add_up(terms):
    total = terms[0].astype(jnp.float32)
    for term in terms[1:]:
        total = total + term.astype(jnp.float32)
    return total.astype(jnp.bfloat16)


def token_rows(moe_input, expert_ids, route_gains, experts):
    group_index = lax.axis_index("grp")
    own_ids = lax.dynamic_index_in_dim(expert_ids, group_index, 1, keepdims=False)
    own_gains = lax.dynamic_index_in_dim(route_gains, group_index, 1, keepdims=False)
    chosen = own_ids[..., None] == jnp.arange(experts, dtype=jnp.int32)
    gains = jnp.sum(jnp.where(chosen, own_gains[..., None], 0.0), axis=2)
    high = gains.astype(jnp.bfloat16)
    rest = gains - high.astype(jnp.float32)
    middle = rest.astype(jnp.bfloat16)
    low = (rest - middle.astype(jnp.float32)).astype(jnp.bfloat16)
    parts = jnp.stack([high, middle, low], axis=-1).reshape(gains.shape[:2] + (3 * experts,))
    parts = jnp.pad(parts, ((0, 0), (0, 0), (0, GAIN_LANES - 3 * experts)))
    return jnp.concatenate([moe_input, parts], axis=2)


def dense_experts(moe_input, expert_ids, route_gains, w_gate, w_up, w_down):
    groups, experts = lax.axis_size("grp"), lax.axis_size("ep")
    far_flips = [(0, 2 * z) for z in range(1, experts // 2)]
    far_flips = far_flips[::-1]
    near_flips = [(2 * x, y) for x in range(groups // 2) for y in range(2)][1:]
    near_flips = near_flips[::-1]
    tokens = token_rows(moe_input, expert_ids, route_gains, experts)
    trace_count, width = moe_input.shape[1:]
    out_chunks = []
    for first, last in STEP_CHUNKS:
        rows = tokens[first:last].reshape((last - first) * trace_count, -1)
        line = jnp.concatenate([rows] + [across(rows, *flip) for flip in far_flips], axis=0)
        plane = [line] + [across(line, *flip) for flip in near_flips]
        pieces = plane + [across(piece, 1, 0) for piece in plane]
        own, other = expert(pieces, w_gate, w_up, w_down)
        other = across(other, 1, 0)
        count = line.shape[0]
        sums = [
            add_up([half[i * count : (i + 1) * count] for half in (own, other)])
            for i in range(len(plane))
        ]
        sums = add_up(
            [sums[0]] + [across(part, *flip) for part, flip in zip(sums[1:], near_flips)]
        )
        count = rows.shape[0]
        parts = [sums[i * count : (i + 1) * count] for i in range(len(far_flips) + 1)]
        total = add_up(
            [parts[0]] + [across(part, *flip) for part, flip in zip(parts[1:], far_flips)]
        )
        out_chunks.append(total.reshape(last - first, trace_count, width))
    return jnp.concatenate(out_chunks, axis=0)


def slot_tables(route_ids, route_gains, expert_count, slot_count):
    token_count, top_count = route_ids.shape
    flat_ids = route_ids.reshape(-1)
    row_list = jnp.arange(flat_ids.shape[0], dtype=jnp.int32)
    same_expert = flat_ids[:, None] == flat_ids[None, :]
    earlier = row_list[None, :] < row_list[:, None]
    slot_rank = jnp.sum(jnp.where(same_expert & earlier, 1, 0), axis=1).astype(jnp.int32)
    slot_index = flat_ids * slot_count + slot_rank
    slot_hot = (
        slot_index[:, None] == jnp.arange(expert_count * slot_count, dtype=jnp.int32)[None, :]
    ).astype(jnp.float32)
    token_hot = (
        (row_list // top_count)[:, None] == jnp.arange(token_count, dtype=jnp.int32)[None, :]
    ).astype(jnp.float32)
    dispatch = jnp.dot(slot_hot.T, token_hot, precision=lax.Precision.HIGHEST)
    combine = jnp.dot(
        token_hot.T, slot_hot * route_gains.reshape(-1)[:, None], precision=lax.Precision.HIGHEST
    )
    return (dispatch, combine)


def expert_rows(token_rows, gate_slice, up_slice, down_slice):
    gate_out = jnp.dot(token_rows, gate_slice, preferred_element_type=jnp.float32)
    up_out = jnp.dot(token_rows, up_slice, preferred_element_type=jnp.float32)
    hidden = (jax.nn.silu(gate_out) * up_out).astype(jnp.bfloat16)
    return jnp.dot(hidden, down_slice, preferred_element_type=jnp.float32).astype(jnp.bfloat16)


def routed_experts(moe_input, expert_ids, route_gains, w_gate, w_up, w_down):
    groups, experts = lax.axis_size("grp"), lax.axis_size("ep")
    trace_count, model_width = moe_input.shape[1:]
    top_count = expert_ids.shape[3]
    slot_count = max(2, trace_count * top_count // experts)
    tables = partial(slot_tables, expert_count=experts, slot_count=slot_count)
    moe_list = []
    for step_index in range(moe_input.shape[0]):
        column_ids = expert_ids[step_index]
        column_gains = route_gains[step_index]
        dispatch_all, combine_all = jax.vmap(tables)(column_ids, column_gains)
        column_tokens = lax.all_gather(moe_input[step_index][None], "grp", axis=0, tiled=True)
        packed = jnp.einsum(
            "gsj,gjd->sgd",
            dispatch_all.astype(jnp.bfloat16),
            column_tokens,
            preferred_element_type=jnp.float32,
        )
        packed = packed.astype(jnp.bfloat16).reshape(experts, slot_count * groups, model_width)
        exchanged = lax.all_to_all(packed, "ep", split_axis=0, concat_axis=0, tiled=True)
        flat_rows = exchanged.reshape(-1, exchanged.shape[-1])
        partial_out = expert_rows(flat_rows, w_gate[0], w_up[0], w_down[0]).reshape(exchanged.shape)
        returned = lax.all_to_all(partial_out, "ep", split_axis=0, concat_axis=0, tiled=True)
        returned = returned.reshape(experts * slot_count, groups, model_width).astype(jnp.float32)
        token_terms = jnp.einsum(
            "gjs,sgd->gjd", combine_all, returned, precision=lax.Precision.HIGHEST
        )
        summed = lax.psum_scatter(
            token_terms.astype(jnp.bfloat16), "grp", scatter_dimension=0, tiled=True
        ).astype(jnp.float32)
        moe_list.append(summed[0].astype(jnp.bfloat16))
    return jnp.stack(moe_list)


def body(
    queries,
    cache,
    new_entries,
    lengths,
    moe_input,
    expert_ids,
    route_gains,
    w_gate,
    w_up,
    w_down,
    plan,
):
    received, source = migrate(cache, new_entries, lengths, plan)
    contexts, migrated_cache = attention(queries, cache, new_entries, lengths, source, received)
    every_expert = expert_ids.shape[3] == lax.axis_size("ep")
    experts_of = dense_experts if every_expert else routed_experts
    moe_output = experts_of(moe_input, expert_ids, route_gains, w_gate, w_up, w_down)
    return (contexts, migrated_cache, moe_output)


def solution(mesh):
    return jax.shard_map(
        body,
        mesh=mesh,
        in_specs=(
            P(None, ("grp", "ep"), None, None),
            P(("grp", "ep"), None, None),
            P(None, ("grp", "ep"), None),
            P(("grp", "ep")),
            P(None, ("grp", "ep"), None),
            P(None, None, "ep", None),
            P(None, None, "ep", None),
            P("ep", None, "grp"),
            P("ep", None, "grp"),
            P("ep", "grp", None),
            P(None, "ep", None, None),
        ),
        out_specs=(
            P(None, ("grp", "ep"), None, None),
            P(("grp", "ep"), None, None),
            P(None, ("grp", "ep"), None),
        ),
        check_vma=False,
    )
```

```python
from functools import partial

import jax
import jax.numpy as jnp
from jax import lax
from jax.experimental import pallas as pl
from jax.experimental.pallas import tpu as pltpu
from jax.sharding import PartitionSpec as P

ROPE = 64


SCORE_SCALE = 192.0 ** (-0.5)


BOTH = ("grp", "ep")


GAIN_LANES = 128


STEP_CHUNKS = ((0, 1), (1, 3))


def across(values, grp_flip, ep_flip):
    groups, columns = lax.axis_size("grp"), lax.axis_size("ep")
    pairs = [
        (g * columns + e, (g ^ grp_flip) * columns + (e ^ ep_flip))
        for g in range(groups)
        for e in range(columns)
    ]
    return lax.ppermute(values, BOTH, pairs)


def plan_entry(plan_ref, group, entry, field):
    return plan_ref[(group * 2 + entry) * 2 + field]


def insert_entries(keys, entries, filled, trace):
    column_index = lax.broadcasted_iota(jnp.int32, keys.shape, 1)
    keys = keys.astype(jnp.float32)
    for step_index in range(entries.shape[0]):
        rows = entries[step_index].astype(jnp.float32)
        row_index = lax.broadcasted_iota(jnp.int32, rows.shape, 0)
        entry = jnp.sum(jnp.where(row_index == trace, rows, 0.0), axis=0, keepdims=True)
        column = jnp.transpose(entry)
        keys = jnp.where(column_index == filled + step_index, column, keys)
    return keys.astype(jnp.bfloat16)


def outgoing_kernel(lengths_ref, plan_ref, group_ref, cache_ref, entries_ref, out_ref):
    slot = outgoing_slot(pl.program_id(0), plan_ref, group_ref)
    out_ref[0] = insert_entries(cache_ref[0], entries_ref[...], lengths_ref[slot], slot)


def outgoing_slot(number, plan_ref, group_ref):
    group = group_ref[0]
    partner = group ^ (number + 1)
    slot = jnp.int32(0)
    for entry in range(2):
        goes = plan_entry(plan_ref, group, entry, 1) == partner
        slot = jnp.where(goes, plan_entry(plan_ref, group, entry, 0), slot)
    return slot


def outgoing(cache, new_entries, lengths, plan, group):
    _, width, capacity = cache.shape
    others = lax.axis_size("grp") - 1
    return pl.pallas_call(
        outgoing_kernel,
        grid_spec=pltpu.PrefetchScalarGridSpec(
            num_scalar_prefetch=3,
            grid=(others,),
            in_specs=[
                pl.BlockSpec(
                    (1, width, capacity),
                    lambda m, lengths_ref, plan_ref, group_ref: (
                        outgoing_slot(m, plan_ref, group_ref),
                        0,
                        0,
                    ),
                ),
                pl.BlockSpec(new_entries.shape, lambda m, *_: (0, 0, 0)),
            ],
            out_specs=pl.BlockSpec((1, width, capacity), lambda m, *_: (m, 0, 0)),
        ),
        out_shape=jax.ShapeDtypeStruct((others, width, capacity), cache.dtype),
        cost_estimate=pl.CostEstimate(
            flops=0, bytes_accessed=4 * others * width * capacity, transcendentals=0
        ),
        name="outgoing",
    )(lengths, plan, group, cache, new_entries)


def attention_kernel(
    lengths_ref, plan_ref, group_ref, queries_ref, cache_ref, entries_ref, *rest
):
    received_refs, (contexts_ref, migrated_ref) = rest[:-2], rest[-2:]
    trace = pl.program_id(0)
    filled = lengths_ref[trace]
    step_count, _, width, heads = queries_ref.shape
    latent = contexts_ref.shape[3]
    capacity = cache_ref.shape[2]
    keys = insert_entries(cache_ref[0], entries_ref[...], filled, trace)
    group = group_ref[0]
    source = jnp.int32(0)
    for number in range(len(received_refs)):
        partner = group ^ (number + 1)
        for entry in range(2):
            lands = (plan_entry(plan_ref, partner, entry, 1) == group) & (
                plan_entry(plan_ref, group, entry, 0) == trace
            )
            source = jnp.where(lands, number + 1, source)

    @pl.when(source == 0)
    def _():
        migrated_ref[0] = keys

    for number, received_ref in enumerate(received_refs):

        @pl.when(source == number + 1)
        def _(received_ref=received_ref):
            migrated_ref[0] = received_ref[...]

    key_rows = jnp.transpose(keys)
    flat_queries = jnp.concatenate([queries_ref[s, 0] for s in range(step_count)], axis=1)
    scores = jnp.dot(key_rows, flat_queries, preferred_element_type=jnp.float32) * SCORE_SCALE
    position = lax.broadcasted_iota(jnp.int32, scores.shape, 0)
    step_of_column = lax.broadcasted_iota(jnp.int32, scores.shape, 1) // heads
    scores = jnp.where(position <= filled + step_of_column, scores, -jnp.inf)
    exp_scores = jnp.exp(scores - jnp.max(scores, axis=0, keepdims=True))
    weights = (exp_scores / jnp.sum(exp_scores, axis=0, keepdims=True)).astype(jnp.bfloat16)
    context = lax.dot_general(
        weights,
        key_rows[:, :latent],
        (((0,), (0,)), ((), ())),
        preferred_element_type=jnp.float32,
    )
    contexts_ref[...] = context.astype(jnp.bfloat16).reshape(contexts_ref.shape)


def attention(queries, cache, new_entries, lengths, plan, group, received):
    step_count, traces, width, heads = queries.shape
    capacity = cache.shape[2]
    latent = width - ROPE
    whole = lambda shape: pl.BlockSpec(shape, lambda t, *_: (0,) * len(shape))
    return pl.pallas_call(
        attention_kernel,
        grid_spec=pltpu.PrefetchScalarGridSpec(
            num_scalar_prefetch=3,
            grid=(traces,),
            in_specs=[
                pl.BlockSpec((step_count, 1, width, heads), lambda t, *_: (0, t, 0, 0)),
                pl.BlockSpec((1, width, capacity), lambda t, *_: (t, 0, 0)),
                whole(new_entries.shape),
            ]
            + [whole((width, capacity))] * len(received),
            out_specs=[
                pl.BlockSpec((step_count, 1, heads, latent), lambda t, *_: (0, t, 0, 0)),
                pl.BlockSpec((1, width, capacity), lambda t, *_: (t, 0, 0)),
            ],
        ),
        out_shape=[
            jax.ShapeDtypeStruct((step_count, traces, heads, latent), jnp.bfloat16),
            jax.ShapeDtypeStruct(cache.shape, jnp.bfloat16),
        ],
        cost_estimate=pl.CostEstimate(
            flops=2 * step_count * traces * heads * capacity * (width + latent),
            bytes_accessed=2 * (queries.size * 2 + cache.size * 2),
            transcendentals=step_count * traces * heads * capacity,
        ),
        name="attention",
    )(lengths, plan, group, queries, cache, new_entries, *received)


def expert_kernel(tile, column_ref, *refs):
    pieces = refs[:-12]
    gate_hbm, up_hbm, down_hbm, own_ref, other_ref = refs[-12:-7]
    gate_ref, up_ref, down_ref, gate_sum, up_sum, hidden_ref, semaphores = refs[-7:]
    width, hidden_width = gate_ref.shape
    tiles = width // tile
    piece_rows = pieces[0].shape[0]
    half = own_ref.shape[0]
    copies = []
    for index in range(tiles):
        rows = pl.ds(index * tile, tile)
        copies.append(
            (
                pltpu.make_async_copy(gate_hbm.at[0, rows], gate_ref.at[rows], semaphores.at[0, index]),
                pltpu.make_async_copy(up_hbm.at[0, rows], up_ref.at[rows], semaphores.at[1, index]),
            )
        )
    down_copies = []
    for index in range(tiles):
        columns = pl.ds(index * tile, tile)
        down_copies.append(
            pltpu.make_async_copy(
                down_hbm.at[0, :, columns], down_ref.at[:, columns], semaphores.at[2, index]
            )
        )
    for pair in copies:
        for copy in pair:
            copy.start()
    for copy in down_copies:
        copy.start()
    gain_parts = jnp.concatenate([piece[:, width:] for piece in pieces], axis=0).astype(jnp.float32)
    lane = lax.broadcasted_iota(jnp.int32, gain_parts.shape, 1)
    first_lane = column_ref[0] * 3
    gain = jnp.sum(
        jnp.where((lane >= first_lane) & (lane < first_lane + 3), gain_parts, 0.0),
        axis=1,
        keepdims=True,
    )
    for index in range(tiles):
        rows = slice(index * tile, (index + 1) * tile)
        tokens = jnp.concatenate([piece[:, rows] for piece in pieces], axis=0)
        for copy, weight_ref, sum_ref in zip(copies[index], (gate_ref, up_ref), (gate_sum, up_sum)):
            copy.wait()
            product = jnp.dot(tokens, weight_ref[rows, :], preferred_element_type=jnp.float32)
            if index == 0:
                sum_ref[...] = product
            else:
                sum_ref[...] += product
    gate_out = gate_sum[...]
    hidden = gate_out / (1.0 + jnp.exp(-gate_out)) * up_sum[...] * gain
    hidden_ref[...] = hidden.astype(jnp.bfloat16)
    for index in range(tiles):
        columns = slice(index * tile, (index + 1) * tile)
        down_copies[index].wait()
        for number, out_ref in enumerate((own_ref, other_ref)):
            out_ref[:, columns] = jnp.dot(
                hidden_ref[number * half : (number + 1) * half, :],
                down_ref[:, columns],
                preferred_element_type=jnp.float32,
            ).astype(jnp.bfloat16)


def expert(pieces, w_gate, w_up, w_down):
    _, width, hidden_width = w_gate.shape
    token_count = sum(piece.shape[0] for piece in pieces)
    tile = width // 4 if width % 512 == 0 else width
    vmem = pl.BlockSpec(memory_space=pltpu.VMEM)
    half = jax.ShapeDtypeStruct((token_count // 2, width), jnp.bfloat16)
    column = lax.axis_index("ep").astype(jnp.int32).reshape(1)
    return pl.pallas_call(
        partial(expert_kernel, tile),
        in_specs=[pl.BlockSpec(memory_space=pltpu.SMEM)]
        + [vmem] * len(pieces)
        + [pl.BlockSpec(memory_space=pl.ANY)] * 3,
        out_specs=[vmem, vmem],
        out_shape=[half, half],
        scratch_shapes=[
            pltpu.VMEM((width, hidden_width), jnp.bfloat16),
            pltpu.VMEM((width, hidden_width), jnp.bfloat16),
            pltpu.VMEM((hidden_width, width), jnp.bfloat16),
            pltpu.VMEM((token_count, hidden_width), jnp.float32),
            pltpu.VMEM((token_count, hidden_width), jnp.float32),
            pltpu.VMEM((token_count, hidden_width), jnp.bfloat16),
            pltpu.SemaphoreType.DMA((3, width // tile)),
        ],
        compiler_params=pltpu.CompilerParams(vmem_limit_bytes=56 * 1024 * 1024),
        cost_estimate=pl.CostEstimate(
            flops=6 * token_count * width * hidden_width,
            bytes_accessed=6 * width * hidden_width + 4 * token_count * width,
            transcendentals=token_count * hidden_width,
        ),
        name="expert",
    )(column, *pieces, w_gate, w_up, w_down)


def add_up(terms):
    total = terms[0].astype(jnp.float32)
    for term in terms[1:]:
        total = total + term.astype(jnp.float32)
    return total.astype(jnp.bfloat16)


def token_rows_kernel(chunks, group_ref, ids_ref, gains_ref, tokens_ref, *out_refs):
    width = tokens_ref.shape[2]
    experts = ids_ref.shape[3]
    group = group_ref[0]
    for out_ref, (first, last) in zip(out_refs, chunks):
        for step_index in range(first, last):
            ids, gains = ids_ref[step_index, group], gains_ref[step_index, group]
            lane = lax.broadcasted_iota(jnp.int32, (ids.shape[0], GAIN_LANES), 1)
            dense = jnp.zeros(lane.shape, jnp.float32)
            for choice in range(ids.shape[1]):
                place = ids[:, choice : choice + 1]
                named = (lane >= 3 * place) & (lane < 3 * place + 3)
                dense = dense + jnp.where(named, gains[:, choice : choice + 1], 0.0)
            high = dense.astype(jnp.bfloat16).astype(jnp.float32)
            rest = dense - high
            middle = rest.astype(jnp.bfloat16).astype(jnp.float32)
            part = lane % 3
            parts = jnp.where(part == 0, high, jnp.where(part == 1, middle, rest - middle))
            out_ref[step_index - first, :, :width] = tokens_ref[step_index]
            out_ref[step_index - first, :, width:] = parts.astype(jnp.bfloat16)


def token_rows(moe_input, expert_ids, route_gains, group):
    _, trace_count, width = moe_input.shape
    vmem = pl.BlockSpec(memory_space=pltpu.VMEM)
    return pl.pallas_call(
        partial(token_rows_kernel, STEP_CHUNKS),
        in_specs=[pl.BlockSpec(memory_space=pltpu.SMEM), vmem, vmem, vmem],
        out_specs=[vmem] * len(STEP_CHUNKS),
        out_shape=[
            jax.ShapeDtypeStruct((last - first, trace_count, width + GAIN_LANES), moe_input.dtype)
            for first, last in STEP_CHUNKS
        ],
        name="token_rows",
    )(group, expert_ids, route_gains, moe_input)


def dense_experts(moe_input, expert_ids, route_gains, w_gate, w_up, w_down):
    groups, experts = lax.axis_size("grp"), lax.axis_size("ep")
    far_flips = [(0, 2 * z) for z in range(1, experts // 2)]
    far_flips = far_flips[::-1]
    near_flips = [(2 * x, y) for x in range(groups // 2) for y in range(2)][1:]
    near_flips = near_flips[::-1]
    tokens = token_rows(moe_input, expert_ids, route_gains, lax.axis_index("grp").reshape(1))
    trace_count, width = moe_input.shape[1:]
    out_chunks = []
    for rows in tokens:
        line = jnp.concatenate([rows] + [across(rows, *flip) for flip in far_flips], axis=0)
        line = line.reshape(-1, line.shape[-1])
        plane = [line] + [across(line, *flip) for flip in near_flips]
        pieces = plane + [across(piece, 1, 0) for piece in plane]
        own, other = expert(pieces, w_gate, w_up, w_down)
        other = across(other, 1, 0)
        count = line.shape[0]
        sums = [
            add_up([half[i * count : (i + 1) * count] for half in (own, other)])
            for i in range(len(plane))
        ]
        sums = add_up(
            [sums[0]] + [across(part, *flip) for part, flip in zip(sums[1:], near_flips)]
        )
        count = rows.shape[0] * trace_count
        parts = [sums[i * count : (i + 1) * count] for i in range(len(far_flips) + 1)]
        total = add_up(
            [parts[0]] + [across(part, *flip) for part, flip in zip(parts[1:], far_flips)]
        )
        out_chunks.append(total.reshape(-1, trace_count, width))
    return jnp.concatenate(out_chunks, axis=0)


def slot_tables(route_ids, route_gains, expert_count, slot_count):
    token_count, top_count = route_ids.shape
    flat_ids = route_ids.reshape(-1)
    row_list = jnp.arange(flat_ids.shape[0], dtype=jnp.int32)
    same_expert = flat_ids[:, None] == flat_ids[None, :]
    earlier = row_list[None, :] < row_list[:, None]
    slot_rank = jnp.sum(jnp.where(same_expert & earlier, 1, 0), axis=1).astype(jnp.int32)
    slot_index = flat_ids * slot_count + slot_rank
    slot_hot = (
        slot_index[:, None] == jnp.arange(expert_count * slot_count, dtype=jnp.int32)[None, :]
    ).astype(jnp.float32)
    token_hot = (
        (row_list // top_count)[:, None] == jnp.arange(token_count, dtype=jnp.int32)[None, :]
    ).astype(jnp.float32)
    dispatch = jnp.dot(slot_hot.T, token_hot, precision=lax.Precision.HIGHEST)
    combine = jnp.dot(
        token_hot.T, slot_hot * route_gains.reshape(-1)[:, None], precision=lax.Precision.HIGHEST
    )
    return (dispatch, combine)


def expert_rows(token_rows, gate_slice, up_slice, down_slice):
    gate_out = jnp.dot(token_rows, gate_slice, preferred_element_type=jnp.float32)
    up_out = jnp.dot(token_rows, up_slice, preferred_element_type=jnp.float32)
    hidden = (jax.nn.silu(gate_out) * up_out).astype(jnp.bfloat16)
    return jnp.dot(hidden, down_slice, preferred_element_type=jnp.float32).astype(jnp.bfloat16)


def routed_experts(moe_input, expert_ids, route_gains, w_gate, w_up, w_down):
    groups, experts = lax.axis_size("grp"), lax.axis_size("ep")
    trace_count, model_width = moe_input.shape[1:]
    top_count = expert_ids.shape[3]
    slot_count = max(2, trace_count * top_count // experts)
    tables = partial(slot_tables, expert_count=experts, slot_count=slot_count)
    moe_list = []
    for step_index in range(moe_input.shape[0]):
        column_ids = expert_ids[step_index]
        column_gains = route_gains[step_index]
        dispatch_all, combine_all = jax.vmap(tables)(column_ids, column_gains)
        column_tokens = lax.all_gather(moe_input[step_index][None], "grp", axis=0, tiled=True)
        packed = jnp.einsum(
            "gsj,gjd->sgd",
            dispatch_all.astype(jnp.bfloat16),
            column_tokens,
            preferred_element_type=jnp.float32,
        )
        packed = packed.astype(jnp.bfloat16).reshape(experts, slot_count * groups, model_width)
        exchanged = lax.all_to_all(packed, "ep", split_axis=0, concat_axis=0, tiled=True)
        flat_rows = exchanged.reshape(-1, exchanged.shape[-1])
        partial_out = expert_rows(flat_rows, w_gate[0], w_up[0], w_down[0]).reshape(exchanged.shape)
        returned = lax.all_to_all(partial_out, "ep", split_axis=0, concat_axis=0, tiled=True)
        returned = returned.reshape(experts * slot_count, groups, model_width).astype(jnp.float32)
        token_terms = jnp.einsum(
            "gjs,sgd->gjd", combine_all, returned, precision=lax.Precision.HIGHEST
        )
        summed = lax.psum_scatter(
            token_terms.astype(jnp.bfloat16), "grp", scatter_dimension=0, tiled=True
        ).astype(jnp.float32)
        moe_list.append(summed[0].astype(jnp.bfloat16))
    return jnp.stack(moe_list)


def body(
    queries,
    cache,
    new_entries,
    lengths,
    moe_input,
    expert_ids,
    route_gains,
    w_gate,
    w_up,
    w_down,
    plan,
):
    queries, cache = jnp.swapaxes(queries, 2, 3), jnp.swapaxes(cache, 1, 2)
    plan, group = plan.reshape(-1), lax.axis_index("grp").reshape(1)
    leaving = outgoing(cache, new_entries, lengths, plan, group)
    received = [across(leaving[flip - 1], flip, 0) for flip in range(1, lax.axis_size("grp"))]
    contexts, migrated_cache = attention(
        queries, cache, new_entries, lengths, plan, group, received
    )
    migrated_cache = jnp.swapaxes(migrated_cache, 1, 2)
    every_expert = expert_ids.shape[3] == lax.axis_size("ep")
    experts_of = dense_experts if every_expert else routed_experts
    moe_output = experts_of(moe_input, expert_ids, route_gains, w_gate, w_up, w_down)
    return (contexts, migrated_cache, moe_output)


def solution(mesh):
    return jax.shard_map(
        body,
        mesh=mesh,
        in_specs=(
            P(None, ("grp", "ep"), None, None),
            P(("grp", "ep"), None, None),
            P(None, ("grp", "ep"), None),
            P(("grp", "ep")),
            P(None, ("grp", "ep"), None),
            P(None, None, "ep", None),
            P(None, None, "ep", None),
            P("ep", None, "grp"),
            P("ep", None, "grp"),
            P("ep", "grp", None),
            P(None, "ep", None, None),
        ),
        out_specs=(
            P(None, ("grp", "ep"), None, None),
            P(("grp", "ep"), None, None),
            P(None, ("grp", "ep"), None),
        ),
        check_vma=False,
    )
```

```python
from functools import partial

import jax
import jax.numpy as jnp
from jax import lax
from jax.experimental import pallas as pl
from jax.experimental.pallas import tpu as pltpu
from jax.sharding import PartitionSpec as P

ROPE = 64


SCORE_SCALE = 192.0 ** (-0.5)


BOTH = ("grp", "ep")


GAIN_LANES = 128


PLANE_GROUPS = ((1, 2, 3), (0,))


SMALL_COST = pl.CostEstimate(flops=1, bytes_accessed=1, transcendentals=0)


LARGE_COST = pl.CostEstimate(flops=1, bytes_accessed=100_000_000, transcendentals=0)


KERNEL_PARAMS = pltpu.CompilerParams(vmem_limit_bytes=12 * 1024 * 1024)


def across(values, grp_flip, ep_flip):
    groups, columns = lax.axis_size("grp"), lax.axis_size("ep")
    pairs = [
        (g * columns + e, (g ^ grp_flip) * columns + (e ^ ep_flip))
        for g in range(groups)
        for e in range(columns)
    ]
    return lax.ppermute(values, BOTH, pairs)


DONE = jax.ShapeDtypeStruct((8, 128), jnp.int32)


ANYWHERE = pl.BlockSpec(memory_space=pl.ANY)


def ignoring(kernel, first, count):
    return lambda *refs: kernel(*refs[:first], *refs[first + count :])


def gate_kernel(count, *refs):
    pass


def gate(arrays, others):
    count = len(arrays)
    return pl.pallas_call(
        partial(gate_kernel, count),
        in_specs=[ANYWHERE] * (count + len(others)),
        out_specs=[ANYWHERE] * count,
        out_shape=[jax.ShapeDtypeStruct(array.shape, array.dtype) for array in arrays],
        input_output_aliases={number: number for number in range(count)},
        compiler_params=KERNEL_PARAMS,
        cost_estimate=SMALL_COST,
        name="gate",
    )(*arrays, *others)


def plan_entry(plan_ref, group, entry, field):
    return plan_ref[entry, field, group]


def insert_entries(keys, entries, filled, trace, steps, traces):
    rows, capacity = entries.shape[0], keys.shape[1]
    row_index = lax.broadcasted_iota(jnp.int32, (rows, capacity), 0)
    column_index = lax.broadcasted_iota(jnp.int32, (rows, capacity), 1)
    place = ((column_index - filled) * traces + trace == row_index) & (column_index >= filled)
    spread = lax.dot_general(
        entries,
        place.astype(jnp.bfloat16),
        (((0,), (0,)), ((), ())),
        preferred_element_type=jnp.float32,
    )
    column_index = lax.broadcasted_iota(jnp.int32, keys.shape, 1)
    new = (column_index >= filled) & (column_index < filled + steps)
    return jnp.where(new, spread, keys.astype(jnp.float32)).astype(jnp.bfloat16)


def outgoing_slot(number, plan_ref, group_ref):
    group = group_ref[0]
    partner = group ^ (number + 1)
    slot = jnp.int32(0)
    for entry in range(2):
        goes = plan_entry(plan_ref, group, entry, 1) == partner
        slot = jnp.where(goes, plan_entry(plan_ref, group, entry, 0), slot)
    return slot


def gain_lanes(ids, gains):
    lane = lax.broadcasted_iota(jnp.int32, (ids.shape[0], GAIN_LANES), 1)
    dense = jnp.zeros(lane.shape, jnp.float32)
    for choice in range(ids.shape[1]):
        place = ids[:, choice : choice + 1]
        named = (lane >= 3 * place) & (lane < 3 * place + 3)
        dense = dense + jnp.where(named, gains[:, choice : choice + 1], 0.0)
    high = dense.astype(jnp.bfloat16).astype(jnp.float32)
    rest = dense - high
    middle = rest.astype(jnp.bfloat16).astype(jnp.float32)
    part = lane % 3
    parts = jnp.where(part == 0, high, jnp.where(part == 1, middle, rest - middle))
    return parts.astype(jnp.bfloat16)


def prepare_kernel(others, lengths_ref, plan_ref, group_ref, *refs):
    cache_hbm, sources, refs = refs[0], refs[1:5], refs[5:]
    rows_ref, entries_ref, out_refs = refs[0], refs[1], refs[2 : 2 + others]
    slots_ref, targets, stack_ref, semaphores = refs[2 + others], refs[3 + others : -2], refs[-2], refs[-1]
    copies = [
        pltpu.make_async_copy(source, target, semaphores.at[others + number])
        for number, (source, target) in enumerate(zip(sources, targets))
    ]
    slots = [outgoing_slot(number, plan_ref, group_ref) for number in range(others)]
    for number, slot in enumerate(slots):
        copies.append(
            pltpu.make_async_copy(
                cache_hbm.at[slot], slots_ref.at[number], semaphores.at[number]
            )
        )
    for copy in copies:
        copy.start()
    for copy in copies:
        copy.wait()
    ids_ref, gains_ref, tokens_ref, new_entries_ref = targets
    steps, traces, width = tokens_ref.shape
    group = group_ref[0]
    for step in range(steps):
        rows_ref[step, :, :width] = tokens_ref[step]
        rows_ref[step, :, width:] = gain_lanes(ids_ref[step, group], gains_ref[step, group])
    stack_ref[...] = jnp.zeros_like(stack_ref)
    for step in range(steps):
        stack_ref[step * traces : (step + 1) * traces, :] = new_entries_ref[step].astype(jnp.float32)
    entries = stack_ref[...].astype(jnp.bfloat16)
    entries_ref[...] = entries
    for number, slot in enumerate(slots):
        out_refs[number][...] = insert_entries(
            slots_ref[number], entries, lengths_ref[slot], slot, steps, traces
        )


def prepare(cache, new_entries, lengths, plan, group, moe_input, expert_ids, route_gains):
    traces, width, capacity = cache.shape
    steps, _, model_width = moe_input.shape
    others = lax.axis_size("grp") - 1
    entry_rows = -(-steps * traces // 16) * 16
    smem, vmem = pl.BlockSpec(memory_space=pltpu.SMEM), pl.BlockSpec(memory_space=pltpu.VMEM)
    sources = [cache, expert_ids, route_gains, moe_input, new_entries]
    rows, entries, *leaving = pl.pallas_call(
        partial(prepare_kernel, others),
        in_specs=[smem] * 3 + [pl.BlockSpec(memory_space=pltpu.HBM)] * len(sources),
        out_specs=[vmem] * (others + 2),
        out_shape=[
            jax.ShapeDtypeStruct((steps, traces, model_width + GAIN_LANES), moe_input.dtype),
            jax.ShapeDtypeStruct((entry_rows, width), cache.dtype),
        ]
        + [jax.ShapeDtypeStruct((width, capacity), cache.dtype)] * others,
        scratch_shapes=[pltpu.VMEM((others, width, capacity), cache.dtype)]
        + [pltpu.VMEM(source.shape, source.dtype) for source in sources[1:]]
        + [
            pltpu.VMEM((entry_rows, width), jnp.float32),
            pltpu.SemaphoreType.DMA((others + len(sources) - 1,)),
        ],
        compiler_params=KERNEL_PARAMS,
        cost_estimate=LARGE_COST,
        name="prepare",
    )(
        pltpu.with_memory_space_constraint(lengths, pltpu.HBM),
        pltpu.with_memory_space_constraint(plan, pltpu.HBM),
        group,
        *(pltpu.with_memory_space_constraint(source, pltpu.HBM) for source in sources),
    )
    return rows, entries, leaving


def line_kernel(*refs):
    pieces, out_ref = refs[:-1], refs[-1]
    rows = [piece[step].astype(jnp.float32) for piece in pieces for step in range(piece.shape[0])]
    out_ref[...] = jnp.concatenate(rows, axis=0).astype(out_ref.dtype)


def line_rows(pieces, others):
    steps, traces, lanes = pieces[0].shape
    vmem = pl.BlockSpec(memory_space=pltpu.VMEM)
    return pl.pallas_call(
        ignoring(line_kernel, 0, len(others)),
        in_specs=[ANYWHERE] * len(others) + [vmem] * len(pieces),
        out_specs=vmem,
        out_shape=jax.ShapeDtypeStruct((len(pieces) * steps * traces, lanes), pieces[0].dtype),
        cost_estimate=LARGE_COST,
        compiler_params=KERNEL_PARAMS,
        name="line_rows",
    )(*others, *pieces)


def line_sums_kernel(*refs):
    steps, traces, _ = refs[-1].shape
    count = len(refs) - refs[0].shape[0] // (steps * traces)
    total = refs[0][...].astype(jnp.float32)
    for term_ref in refs[1:count]:
        total = total + term_ref[...].astype(jnp.float32)
    for number, out_ref in enumerate(refs[count:]):
        for step in range(steps):
            first = (number * steps + step) * traces
            out_ref[step] = total[first : first + traces].astype(out_ref.dtype)


def line_sums(terms, steps, traces, pieces, others):
    lanes = terms[0].shape[1]
    vmem = pl.BlockSpec(memory_space=pltpu.VMEM)
    return pl.pallas_call(
        ignoring(line_sums_kernel, 0, len(others)),
        in_specs=[ANYWHERE] * len(others) + [vmem] * len(terms),
        out_specs=[vmem] * pieces,
        out_shape=[jax.ShapeDtypeStruct((steps, traces, lanes), terms[0].dtype)] * pieces,
        cost_estimate=LARGE_COST,
        compiler_params=KERNEL_PARAMS,
        name="line_sums",
    )(*others, *terms)


def attention_kernel(
    block, lengths_ref, plan_ref, group_ref, queries_ref, cache_ref, entries_ref, *rest
):
    received_refs, (contexts_ref, migrated_ref, done_ref) = rest[:-3], rest[-3:]
    done_ref[...] = jnp.zeros_like(done_ref)
    grid_index = pl.program_id(0)
    step_count, _, width, heads = queries_ref.shape
    latent = contexts_ref.shape[3]
    traces = block * pl.num_programs(0)
    group = group_ref[0]
    for member in range(block):
        trace = grid_index * block + member
        filled = lengths_ref[trace]
        keys = insert_entries(
            cache_ref[member], entries_ref[...], filled, trace, step_count, traces
        )
        migrated = keys
        for number, received_ref in enumerate(received_refs):
            partner = group ^ (number + 1)
            for entry in range(2):
                lands = (plan_entry(plan_ref, partner, entry, 1) == group) & (
                    plan_entry(plan_ref, group, entry, 0) == trace
                )
                migrated = jnp.where(lands, received_ref[...], migrated)
        migrated_ref[member] = migrated
        key_rows = jnp.transpose(keys)
        flat_queries = jnp.concatenate(
            [queries_ref[s, member] for s in range(step_count)], axis=1
        )
        scores = jnp.dot(key_rows, flat_queries, preferred_element_type=jnp.float32) * SCORE_SCALE
        position = lax.broadcasted_iota(jnp.int32, scores.shape, 0)
        step_of_column = lax.broadcasted_iota(jnp.int32, scores.shape, 1) // heads
        scores = jnp.where(position <= filled + step_of_column, scores, -jnp.inf)
        exp_scores = jnp.exp(scores - jnp.max(scores, axis=0, keepdims=True))
        weights = (exp_scores / jnp.sum(exp_scores, axis=0, keepdims=True)).astype(jnp.bfloat16)
        context = lax.dot_general(
            weights,
            key_rows[:, :latent],
            (((0,), (0,)), ((), ())),
            preferred_element_type=jnp.float32,
        )
        contexts_ref[:, member] = context.astype(jnp.bfloat16).reshape(step_count, heads, latent)


def fetch_kernel(*refs):
    refs, done_ref, refs_semaphores = refs[:-2], refs[-2], refs[-1]
    done_ref[...] = jnp.zeros_like(done_ref)
    refs = (*refs, refs_semaphores)
    count = (len(refs) - 1) // 2
    copies = [
        pltpu.make_async_copy(source.at[0], target, refs[-1].at[number])
        for number, (source, target) in enumerate(zip(refs[:count], refs[count:-1]))
    ]
    for copy in copies:
        copy.start()
    for copy in copies:
        copy.wait()


def fetch(weights, others):
    weights = [pltpu.with_memory_space_constraint(weight, pltpu.HBM) for weight in weights]
    return pl.pallas_call(
        ignoring(fetch_kernel, 0, len(others)),
        in_specs=[ANYWHERE] * len(others)
        + [pl.BlockSpec(memory_space=pltpu.HBM)] * len(weights),
        out_specs=[pl.BlockSpec(memory_space=pltpu.VMEM)] * (len(weights) + 1),
        out_shape=[pltpu.VMEM(weight.shape[1:], weight.dtype) for weight in weights] + [DONE],
        scratch_shapes=[pltpu.SemaphoreType.DMA((len(weights),))],
        cost_estimate=LARGE_COST,
        compiler_params=KERNEL_PARAMS,
        name="fetch",
    )(*others, *weights)


def attention(queries, cache, entries, lengths, plan, group, received, others=(), block=2):
    step_count, traces, width, heads = queries.shape
    capacity = cache.shape[2]
    latent = width - ROPE
    whole = lambda shape: pl.BlockSpec(shape, lambda t, *_: (0,) * len(shape))
    return pl.pallas_call(
        ignoring(partial(attention_kernel, block), 3, len(others)),
        grid_spec=pltpu.PrefetchScalarGridSpec(
            num_scalar_prefetch=3,
            grid=(traces // block,),
            in_specs=[ANYWHERE] * len(others)
            + [
                pl.BlockSpec((step_count, block, width, heads), lambda t, *_: (0, t, 0, 0)),
                pl.BlockSpec((block, width, capacity), lambda t, *_: (t, 0, 0)),
                whole(entries.shape),
            ]
            + [whole((width, capacity))] * len(received),
            out_specs=[
                pl.BlockSpec((step_count, block, heads, latent), lambda t, *_: (0, t, 0, 0)),
                pl.BlockSpec((block, width, capacity), lambda t, *_: (t, 0, 0)),
                whole(DONE.shape),
            ],
        ),
        out_shape=[
            jax.ShapeDtypeStruct((step_count, traces, heads, latent), jnp.bfloat16),
            jax.ShapeDtypeStruct(cache.shape, jnp.bfloat16),
            DONE,
        ],
        cost_estimate=LARGE_COST,
        compiler_params=KERNEL_PARAMS,
        name="attention",
    )(lengths, plan, group, *others, queries, cache, entries, *received)


def expert_kernel(column_ref, *refs):
    count = (len(refs) - 4) // 2
    pieces, (gate_ref, up_ref, down_ref) = refs[:count], refs[count : count + 3]
    out_refs, hidden_ref = refs[count + 3 : -1], refs[-1]
    width, hidden_width = gate_ref.shape
    rows = pieces[0].shape[0]
    gain_parts = jnp.concatenate([piece[:, width:] for piece in pieces], axis=0).astype(jnp.float32)
    lane = lax.broadcasted_iota(jnp.int32, gain_parts.shape, 1)
    first_lane = column_ref[0] * 3
    gain = jnp.sum(
        jnp.where((lane >= first_lane) & (lane < first_lane + 3), gain_parts, 0.0),
        axis=1,
        keepdims=True,
    )
    tokens = jnp.concatenate([piece[:, :width] for piece in pieces], axis=0)
    gate_out = jnp.dot(tokens, gate_ref[...], preferred_element_type=jnp.float32)
    up_out = jnp.dot(tokens, up_ref[...], preferred_element_type=jnp.float32)
    hidden = gate_out / (1.0 + jnp.exp(-gate_out)) * up_out * gain
    hidden_ref[...] = hidden.astype(jnp.bfloat16)
    tile = 512 if width % 512 == 0 else width
    for first in range(0, width, tile):
        columns = slice(first, first + tile)
        products = jnp.dot(
            hidden_ref[...], down_ref[:, columns], preferred_element_type=jnp.float32
        ).astype(jnp.bfloat16)
        for number, out_ref in enumerate(out_refs):
            out_ref[:, columns] = products[number * rows : (number + 1) * rows]


def expert(pieces, weights, others=()):
    width, hidden_width = weights[0].shape
    rows = pieces[0].shape[0]
    vmem = pl.BlockSpec(memory_space=pltpu.VMEM)
    column = lax.axis_index("ep").astype(jnp.int32).reshape(1)
    return pl.pallas_call(
        ignoring(expert_kernel, 0, len(others)),
        in_specs=[ANYWHERE] * len(others)
        + [pl.BlockSpec(memory_space=pltpu.SMEM)]
        + [vmem] * (len(pieces) + 3),
        out_specs=[vmem] * len(pieces),
        out_shape=[jax.ShapeDtypeStruct((rows, width), jnp.bfloat16)] * len(pieces),
        scratch_shapes=[pltpu.VMEM((len(pieces) * rows, hidden_width), jnp.bfloat16)],
        cost_estimate=LARGE_COST,
        compiler_params=pltpu.CompilerParams(vmem_limit_bytes=28 * 1024 * 1024),
        name="expert",
    )(*others, column, *pieces, *weights)


def add_up(terms):
    total = terms[0].astype(jnp.float32)
    for term in terms[1:]:
        total = total + term.astype(jnp.float32)
    return total.astype(jnp.bfloat16)


def dense_layer(
    queries, cache, new_entries, lengths, moe_input, expert_ids, route_gains, weights, plan, group
):
    groups, experts = lax.axis_size("grp"), lax.axis_size("ep")
    far_flips = [(0, 2 * z) for z in range(1, experts // 2)][::-1]
    near_flips = [(2 * x, y) for x in range(groups // 2) for y in range(2)][1:]
    steps, trace_count, width = moe_input.shape
    rows, entries, leaving = prepare(
        cache, new_entries, lengths, plan, group, moe_input, expert_ids, route_gains
    )
    received = [across(leaving[flip - 1], flip, 0) for flip in range(1, groups)]
    line = [rows] + [across(rows, *flip) for flip in far_flips]
    own_line = line_rows(line, received)
    plane = [across(own_line, *flip) for flip in near_flips]
    *weights, fetched = fetch(weights, [own_line])
    plane = [own_line] + list(lax.optimization_barrier((plane, fetched))[0])
    other_plane = [across(piece, 1, 0) for piece in plane]
    terms, sums = [None] * len(plane), []
    for members in PLANE_GROUPS:
        pieces = [half[member] for half in (plane, other_plane) for member in members]
        outputs = expert(pieces, weights, sums)
        for member, own, other in zip(members, outputs, outputs[len(members) :]):
            term = add_up([own, across(other, 1, 0)])
            terms[member] = across(term, *near_flips[member - 1]) if member else term
            sums = sums + [term]
    contexts, migrated_cache, attended = attention(
        queries, cache, entries, lengths, plan, group, received, sums
    )
    parts = line_sums(terms, steps, trace_count, len(line), [attended])
    moe_output = add_up(
        [parts[0]] + [across(part, *flip) for part, flip in zip(parts[1:], far_flips)]
    )
    return contexts, migrated_cache, moe_output


def routed_layer(
    queries, cache, new_entries, lengths, moe_input, expert_ids, route_gains, weights, plan, group
):
    _, entries, leaving = prepare(
        cache, new_entries, lengths, plan, group, moe_input, expert_ids, route_gains
    )
    received = [across(leaving[flip - 1], flip, 0) for flip in range(1, lax.axis_size("grp"))]
    contexts, migrated_cache, _ = attention(
        queries, cache, entries, lengths, plan, group, received
    )
    moe_output = routed_experts(moe_input, expert_ids, route_gains, *weights)
    return contexts, migrated_cache, moe_output


def slot_tables(route_ids, route_gains, expert_count, slot_count):
    token_count, top_count = route_ids.shape
    flat_ids = route_ids.reshape(-1)
    row_list = jnp.arange(flat_ids.shape[0], dtype=jnp.int32)
    same_expert = flat_ids[:, None] == flat_ids[None, :]
    earlier = row_list[None, :] < row_list[:, None]
    slot_rank = jnp.sum(jnp.where(same_expert & earlier, 1, 0), axis=1).astype(jnp.int32)
    slot_index = flat_ids * slot_count + slot_rank
    slot_hot = (
        slot_index[:, None] == jnp.arange(expert_count * slot_count, dtype=jnp.int32)[None, :]
    ).astype(jnp.float32)
    token_hot = (
        (row_list // top_count)[:, None] == jnp.arange(token_count, dtype=jnp.int32)[None, :]
    ).astype(jnp.float32)
    dispatch = jnp.dot(slot_hot.T, token_hot, precision=lax.Precision.HIGHEST)
    combine = jnp.dot(
        token_hot.T, slot_hot * route_gains.reshape(-1)[:, None], precision=lax.Precision.HIGHEST
    )
    return (dispatch, combine)


def expert_rows(token_rows, gate_slice, up_slice, down_slice):
    gate_out = jnp.dot(token_rows, gate_slice, preferred_element_type=jnp.float32)
    up_out = jnp.dot(token_rows, up_slice, preferred_element_type=jnp.float32)
    hidden = (jax.nn.silu(gate_out) * up_out).astype(jnp.bfloat16)
    return jnp.dot(hidden, down_slice, preferred_element_type=jnp.float32).astype(jnp.bfloat16)


def routed_experts(moe_input, expert_ids, route_gains, w_gate, w_up, w_down):
    groups, experts = lax.axis_size("grp"), lax.axis_size("ep")
    trace_count, model_width = moe_input.shape[1:]
    top_count = expert_ids.shape[3]
    slot_count = max(2, trace_count * top_count // experts)
    tables = partial(slot_tables, expert_count=experts, slot_count=slot_count)
    moe_list = []
    for step_index in range(moe_input.shape[0]):
        column_ids = expert_ids[step_index]
        column_gains = route_gains[step_index]
        dispatch_all, combine_all = jax.vmap(tables)(column_ids, column_gains)
        column_tokens = lax.all_gather(moe_input[step_index][None], "grp", axis=0, tiled=True)
        packed = jnp.einsum(
            "gsj,gjd->sgd",
            dispatch_all.astype(jnp.bfloat16),
            column_tokens,
            preferred_element_type=jnp.float32,
        )
        packed = packed.astype(jnp.bfloat16).reshape(experts, slot_count * groups, model_width)
        exchanged = lax.all_to_all(packed, "ep", split_axis=0, concat_axis=0, tiled=True)
        flat_rows = exchanged.reshape(-1, exchanged.shape[-1])
        partial_out = expert_rows(flat_rows, w_gate[0], w_up[0], w_down[0]).reshape(exchanged.shape)
        returned = lax.all_to_all(partial_out, "ep", split_axis=0, concat_axis=0, tiled=True)
        returned = returned.reshape(experts * slot_count, groups, model_width).astype(jnp.float32)
        token_terms = jnp.einsum(
            "gjs,sgd->gjd", combine_all, returned, precision=lax.Precision.HIGHEST
        )
        summed = lax.psum_scatter(
            token_terms.astype(jnp.bfloat16), "grp", scatter_dimension=0, tiled=True
        ).astype(jnp.float32)
        moe_list.append(summed[0].astype(jnp.bfloat16))
    return jnp.stack(moe_list)


def body(
    queries,
    cache,
    new_entries,
    lengths,
    moe_input,
    expert_ids,
    route_gains,
    w_gate,
    w_up,
    w_down,
    plan,
):
    queries, cache = jnp.swapaxes(queries, 2, 3), jnp.swapaxes(cache, 1, 2)
    plan, group = jnp.transpose(plan[:, 0], (1, 2, 0)), lax.axis_index("grp").reshape(1)
    every_expert = expert_ids.shape[3] == lax.axis_size("ep")
    layer = dense_layer if every_expert else routed_layer
    contexts, migrated_cache, moe_output = layer(
        queries,
        cache,
        new_entries,
        lengths,
        moe_input,
        expert_ids,
        route_gains,
        (w_gate, w_up, w_down),
        plan,
        group,
    )
    return contexts, jnp.swapaxes(migrated_cache, 1, 2), moe_output


def solution(mesh):
    return jax.shard_map(
        body,
        mesh=mesh,
        in_specs=(
            P(None, ("grp", "ep"), None, None),
            P(("grp", "ep"), None, None),
            P(None, ("grp", "ep"), None),
            P(("grp", "ep")),
            P(None, ("grp", "ep"), None),
            P(None, None, "ep", None),
            P(None, None, "ep", None),
            P("ep", None, "grp"),
            P("ep", None, "grp"),
            P("ep", "grp", None),
            P(None, "ep", None, None),
        ),
        out_specs=(
            P(None, ("grp", "ep"), None, None),
            P(("grp", "ep"), None, None),
            P(None, ("grp", "ep"), None),
        ),
        check_vma=False,
    )
```

```python
from functools import partial

import jax
import jax.numpy as jnp
from jax import lax
from jax.experimental import pallas as pl
from jax.experimental.pallas import tpu as pltpu
from jax.sharding import PartitionSpec as P

ROPE = 64


SCORE_SCALE = 192.0 ** (-0.5)


BOTH = ("grp", "ep")


GAIN_LANES = 128


PLANE_GROUPS = ((1, 2, 3), (0,))


SMALL_COST = pl.CostEstimate(flops=1, bytes_accessed=1, transcendentals=0)


LARGE_COST = pl.CostEstimate(flops=1, bytes_accessed=100_000_000, transcendentals=0)


KERNEL_PARAMS = pltpu.CompilerParams(vmem_limit_bytes=12 * 1024 * 1024)


def across(values, even_flip, odd_flip=None):
    groups, columns = lax.axis_size("grp"), lax.axis_size("ep")
    flips = (even_flip, odd_flip or even_flip)
    pairs = []
    for g in range(groups):
        for e in range(columns):
            grp_flip, ep_flip = flips[g % 2]
            pairs.append((g * columns + e, (g ^ grp_flip) * columns + (e ^ ep_flip)))
    return lax.ppermute(values, BOTH, pairs)


DONE = jax.ShapeDtypeStruct((8, 128), jnp.int32)


ANYWHERE = pl.BlockSpec(memory_space=pl.ANY)


def ignoring(kernel, first, count):
    return lambda *refs: kernel(*refs[:first], *refs[first + count :])


def gate_kernel(count, *refs):
    pass


def gate(arrays, others):
    count = len(arrays)
    return pl.pallas_call(
        partial(gate_kernel, count),
        in_specs=[ANYWHERE] * (count + len(others)),
        out_specs=[ANYWHERE] * count,
        out_shape=[jax.ShapeDtypeStruct(array.shape, array.dtype) for array in arrays],
        input_output_aliases={number: number for number in range(count)},
        compiler_params=KERNEL_PARAMS,
        cost_estimate=SMALL_COST,
        name="gate",
    )(*arrays, *others)


def plan_entry(plan_ref, group, entry, field):
    return plan_ref[entry, field, group]


def insert_entries(keys, entries, filled, trace, steps, traces):
    rows, capacity = entries.shape[0], keys.shape[1]
    row_index = lax.broadcasted_iota(jnp.int32, (rows, capacity), 0)
    column_index = lax.broadcasted_iota(jnp.int32, (rows, capacity), 1)
    place = ((column_index - filled) * traces + trace == row_index) & (column_index >= filled)
    spread = lax.dot_general(
        entries,
        place.astype(jnp.bfloat16),
        (((0,), (0,)), ((), ())),
        preferred_element_type=jnp.float32,
    )
    column_index = lax.broadcasted_iota(jnp.int32, keys.shape, 1)
    new = (column_index >= filled) & (column_index < filled + steps)
    return jnp.where(new, spread, keys.astype(jnp.float32)).astype(jnp.bfloat16)


def outgoing_slot(number, plan_ref, group_ref):
    group = group_ref[0]
    partner = group ^ (number + 1)
    slot = jnp.int32(0)
    for entry in range(2):
        goes = plan_entry(plan_ref, group, entry, 1) == partner
        slot = jnp.where(goes, plan_entry(plan_ref, group, entry, 0), slot)
    return slot


def gain_lanes(ids, gains):
    lane = lax.broadcasted_iota(jnp.int32, (ids.shape[0], GAIN_LANES), 1)
    dense = jnp.zeros(lane.shape, jnp.float32)
    for choice in range(ids.shape[1]):
        place = ids[:, choice : choice + 1]
        named = (lane >= 3 * place) & (lane < 3 * place + 3)
        dense = dense + jnp.where(named, gains[:, choice : choice + 1], 0.0)
    high = dense.astype(jnp.bfloat16).astype(jnp.float32)
    rest = dense - high
    middle = rest.astype(jnp.bfloat16).astype(jnp.float32)
    part = lane % 3
    parts = jnp.where(part == 0, high, jnp.where(part == 1, middle, rest - middle))
    return parts.astype(jnp.bfloat16)


def token_rows_kernel(group_ref, *refs):
    sources, rows_ref, targets, semaphores = refs[:3], refs[3], refs[4:7], refs[7]
    copies = [
        pltpu.make_async_copy(source, target, semaphores.at[number])
        for number, (source, target) in enumerate(zip(sources, targets))
    ]
    for copy in copies:
        copy.start()
    for copy in copies:
        copy.wait()
    ids_ref, gains_ref, tokens_ref = targets
    steps, _, width = tokens_ref.shape
    group = group_ref[0]
    for step in range(steps):
        rows_ref[step, :, :width] = tokens_ref[step]
        rows_ref[step, :, width:] = gain_lanes(ids_ref[step, group], gains_ref[step, group])


def token_rows(group, expert_ids, route_gains, moe_input):
    steps, traces, width = moe_input.shape
    sources = [expert_ids, route_gains, moe_input]
    return pl.pallas_call(
        token_rows_kernel,
        in_specs=[pl.BlockSpec(memory_space=pltpu.SMEM)]
        + [pl.BlockSpec(memory_space=pltpu.HBM)] * len(sources),
        out_specs=pl.BlockSpec(memory_space=pltpu.VMEM),
        out_shape=jax.ShapeDtypeStruct((steps, traces, width + GAIN_LANES), moe_input.dtype),
        scratch_shapes=[pltpu.VMEM(source.shape, source.dtype) for source in sources]
        + [pltpu.SemaphoreType.DMA((len(sources),))],
        compiler_params=KERNEL_PARAMS,
        cost_estimate=LARGE_COST,
        name="token_rows",
    )(group, *(pltpu.with_memory_space_constraint(source, pltpu.HBM) for source in sources))


def outgoing_kernel(others, lengths_ref, plan_ref, group_ref, cache_hbm, entries_hbm, *refs):
    entries_ref, out_refs = refs[0], refs[1 : 1 + others]
    slots_ref, new_entries_ref, stack_ref, semaphores = refs[1 + others :]
    slots = [outgoing_slot(number, plan_ref, group_ref) for number in range(others)]
    copies = [pltpu.make_async_copy(entries_hbm, new_entries_ref, semaphores.at[others])]
    for number, slot in enumerate(slots):
        copies.append(
            pltpu.make_async_copy(cache_hbm.at[slot], slots_ref.at[number], semaphores.at[number])
        )
    for copy in copies:
        copy.start()
    for copy in copies:
        copy.wait()
    steps, traces, _ = new_entries_ref.shape
    stack_ref[...] = jnp.zeros_like(stack_ref)
    for step in range(steps):
        stack_ref[step * traces : (step + 1) * traces, :] = new_entries_ref[step].astype(jnp.float32)
    entries = stack_ref[...].astype(jnp.bfloat16)
    entries_ref[...] = entries
    for number, slot in enumerate(slots):
        out_refs[number][...] = insert_entries(
            slots_ref[number], entries, lengths_ref[slot], slot, steps, traces
        )


def outgoing(cache, new_entries, lengths, plan, group, behind=()):
    traces, width, capacity = cache.shape
    others = lax.axis_size("grp") - 1
    entry_rows = -(-new_entries.shape[0] * traces // 16) * 16
    smem, vmem = pl.BlockSpec(memory_space=pltpu.SMEM), pl.BlockSpec(memory_space=pltpu.VMEM)
    hbm = pl.BlockSpec(memory_space=pltpu.HBM)
    entries, *leaving = pl.pallas_call(
        ignoring(partial(outgoing_kernel, others), 0, len(behind)),
        in_specs=[ANYWHERE] * len(behind) + [smem, smem, smem, hbm, hbm],
        out_specs=[vmem] * (others + 1),
        out_shape=[jax.ShapeDtypeStruct((entry_rows, width), cache.dtype)]
        + [jax.ShapeDtypeStruct((width, capacity), cache.dtype)] * others,
        scratch_shapes=[
            pltpu.VMEM((others, width, capacity), cache.dtype),
            pltpu.VMEM(new_entries.shape, new_entries.dtype),
            pltpu.VMEM((entry_rows, width), jnp.float32),
            pltpu.SemaphoreType.DMA((others + 1,)),
        ],
        compiler_params=KERNEL_PARAMS,
        cost_estimate=LARGE_COST,
        name="outgoing",
    )(
        *behind,
        pltpu.with_memory_space_constraint(lengths, pltpu.HBM),
        pltpu.with_memory_space_constraint(plan, pltpu.HBM),
        group,
        pltpu.with_memory_space_constraint(cache, pltpu.HBM),
        pltpu.with_memory_space_constraint(new_entries, pltpu.HBM),
    )
    return entries, leaving


def line_kernel(*refs):
    pieces, out_ref = refs[:-1], refs[-1]
    rows = [piece[step].astype(jnp.float32) for piece in pieces for step in range(piece.shape[0])]
    out_ref[...] = jnp.concatenate(rows, axis=0).astype(out_ref.dtype)


def line_rows(pieces, others):
    steps, traces, lanes = pieces[0].shape
    vmem = pl.BlockSpec(memory_space=pltpu.VMEM)
    return pl.pallas_call(
        ignoring(line_kernel, 0, len(others)),
        in_specs=[ANYWHERE] * len(others) + [vmem] * len(pieces),
        out_specs=vmem,
        out_shape=jax.ShapeDtypeStruct((len(pieces) * steps * traces, lanes), pieces[0].dtype),
        cost_estimate=LARGE_COST,
        compiler_params=KERNEL_PARAMS,
        name="line_rows",
    )(*others, *pieces)


def line_sums_kernel(*refs):
    steps, traces, _ = refs[-1].shape
    count = len(refs) - refs[0].shape[0] // (steps * traces)
    total = refs[0][...].astype(jnp.float32)
    for term_ref in refs[1:count]:
        total = total + term_ref[...].astype(jnp.float32)
    for number, out_ref in enumerate(refs[count:]):
        for step in range(steps):
            first = (number * steps + step) * traces
            out_ref[step] = total[first : first + traces].astype(out_ref.dtype)


def line_sums(terms, steps, traces, pieces, others):
    lanes = terms[0].shape[1]
    vmem = pl.BlockSpec(memory_space=pltpu.VMEM)
    return pl.pallas_call(
        ignoring(line_sums_kernel, 0, len(others)),
        in_specs=[ANYWHERE] * len(others) + [vmem] * len(terms),
        out_specs=[vmem] * pieces,
        out_shape=[jax.ShapeDtypeStruct((steps, traces, lanes), terms[0].dtype)] * pieces,
        cost_estimate=LARGE_COST,
        compiler_params=KERNEL_PARAMS,
        name="line_sums",
    )(*others, *terms)


def attention_kernel(
    block, lengths_ref, plan_ref, group_ref, queries_ref, cache_ref, entries_ref, *rest
):
    received_refs, (contexts_ref, migrated_ref, done_ref) = rest[:-3], rest[-3:]
    done_ref[...] = jnp.zeros_like(done_ref)
    grid_index = pl.program_id(0)
    step_count, _, width, heads = queries_ref.shape
    latent = contexts_ref.shape[3]
    traces = block * pl.num_programs(0)
    group = group_ref[0]
    for member in range(block):
        trace = grid_index * block + member
        filled = lengths_ref[trace]
        keys = insert_entries(
            cache_ref[member], entries_ref[...], filled, trace, step_count, traces
        )
        migrated = keys
        for number, received_ref in enumerate(received_refs):
            partner = group ^ (number + 1)
            for entry in range(2):
                lands = (plan_entry(plan_ref, partner, entry, 1) == group) & (
                    plan_entry(plan_ref, group, entry, 0) == trace
                )
                migrated = jnp.where(lands, received_ref[...], migrated)
        migrated_ref[member] = migrated
        key_rows = jnp.transpose(keys)
        flat_queries = jnp.concatenate(
            [queries_ref[s, member] for s in range(step_count)], axis=1
        )
        scores = jnp.dot(key_rows, flat_queries, preferred_element_type=jnp.float32) * SCORE_SCALE
        position = lax.broadcasted_iota(jnp.int32, scores.shape, 0)
        step_of_column = lax.broadcasted_iota(jnp.int32, scores.shape, 1) // heads
        scores = jnp.where(position <= filled + step_of_column, scores, -jnp.inf)
        exp_scores = jnp.exp(scores - jnp.max(scores, axis=0, keepdims=True))
        weights = (exp_scores / jnp.sum(exp_scores, axis=0, keepdims=True)).astype(jnp.bfloat16)
        context = lax.dot_general(
            weights,
            key_rows[:, :latent],
            (((0,), (0,)), ((), ())),
            preferred_element_type=jnp.float32,
        )
        contexts_ref[:, member] = context.astype(jnp.bfloat16).reshape(step_count, heads, latent)


def fetch_kernel(*refs):
    refs, done_ref, refs_semaphores = refs[:-2], refs[-2], refs[-1]
    done_ref[...] = jnp.zeros_like(done_ref)
    refs = (*refs, refs_semaphores)
    count = (len(refs) - 1) // 2
    copies = [
        pltpu.make_async_copy(source.at[0], target, refs[-1].at[number])
        for number, (source, target) in enumerate(zip(refs[:count], refs[count:-1]))
    ]
    for copy in copies:
        copy.start()
    for copy in copies:
        copy.wait()


def fetch(weights, others):
    weights = [pltpu.with_memory_space_constraint(weight, pltpu.HBM) for weight in weights]
    return pl.pallas_call(
        ignoring(fetch_kernel, 0, len(others)),
        in_specs=[ANYWHERE] * len(others)
        + [pl.BlockSpec(memory_space=pltpu.HBM)] * len(weights),
        out_specs=[pl.BlockSpec(memory_space=pltpu.VMEM)] * (len(weights) + 1),
        out_shape=[pltpu.VMEM(weight.shape[1:], weight.dtype) for weight in weights] + [DONE],
        scratch_shapes=[pltpu.SemaphoreType.DMA((len(weights),))],
        cost_estimate=LARGE_COST,
        compiler_params=KERNEL_PARAMS,
        name="fetch",
    )(*others, *weights)


def attention(queries, cache, entries, lengths, plan, group, received, others=(), block=2):
    step_count, traces, width, heads = queries.shape
    capacity = cache.shape[2]
    latent = width - ROPE
    whole = lambda shape: pl.BlockSpec(shape, lambda t, *_: (0,) * len(shape))
    return pl.pallas_call(
        ignoring(partial(attention_kernel, block), 3, len(others)),
        grid_spec=pltpu.PrefetchScalarGridSpec(
            num_scalar_prefetch=3,
            grid=(traces // block,),
            in_specs=[ANYWHERE] * len(others)
            + [
                pl.BlockSpec((step_count, block, width, heads), lambda t, *_: (0, t, 0, 0)),
                pl.BlockSpec((block, width, capacity), lambda t, *_: (t, 0, 0)),
                whole(entries.shape),
            ]
            + [whole((width, capacity))] * len(received),
            out_specs=[
                pl.BlockSpec((step_count, block, heads, latent), lambda t, *_: (0, t, 0, 0)),
                pl.BlockSpec((block, width, capacity), lambda t, *_: (t, 0, 0)),
                whole(DONE.shape),
            ],
        ),
        out_shape=[
            jax.ShapeDtypeStruct((step_count, traces, heads, latent), jnp.bfloat16),
            jax.ShapeDtypeStruct(cache.shape, jnp.bfloat16),
            DONE,
        ],
        cost_estimate=LARGE_COST,
        compiler_params=KERNEL_PARAMS,
        name="attention",
    )(lengths, plan, group, *others, queries, cache, entries, *received)


def expert_kernel(column_ref, *refs):
    count = (len(refs) - 4) // 2
    pieces, (gate_ref, up_ref, down_ref) = refs[:count], refs[count : count + 3]
    out_refs, hidden_ref = refs[count + 3 : -1], refs[-1]
    width, hidden_width = gate_ref.shape
    rows = pieces[0].shape[0]
    gain_parts = jnp.concatenate([piece[:, width:] for piece in pieces], axis=0).astype(jnp.float32)
    lane = lax.broadcasted_iota(jnp.int32, gain_parts.shape, 1)
    first_lane = column_ref[0] * 3
    gain = jnp.sum(
        jnp.where((lane >= first_lane) & (lane < first_lane + 3), gain_parts, 0.0),
        axis=1,
        keepdims=True,
    )
    tokens = jnp.concatenate([piece[:, :width] for piece in pieces], axis=0)
    gate_out = jnp.dot(tokens, gate_ref[...], preferred_element_type=jnp.float32)
    up_out = jnp.dot(tokens, up_ref[...], preferred_element_type=jnp.float32)
    hidden = gate_out / (1.0 + jnp.exp(-gate_out)) * up_out * gain
    hidden_ref[...] = hidden.astype(jnp.bfloat16)
    tile = 512 if width % 512 == 0 else width
    for first in range(0, width, tile):
        columns = slice(first, first + tile)
        products = jnp.dot(
            hidden_ref[...], down_ref[:, columns], preferred_element_type=jnp.float32
        ).astype(jnp.bfloat16)
        for number, out_ref in enumerate(out_refs):
            out_ref[:, columns] = products[number * rows : (number + 1) * rows]


def expert(pieces, weights, others=()):
    width, hidden_width = weights[0].shape
    rows = pieces[0].shape[0]
    vmem = pl.BlockSpec(memory_space=pltpu.VMEM)
    column = lax.axis_index("ep").astype(jnp.int32).reshape(1)
    return pl.pallas_call(
        ignoring(expert_kernel, 0, len(others)),
        in_specs=[ANYWHERE] * len(others)
        + [pl.BlockSpec(memory_space=pltpu.SMEM)]
        + [vmem] * (len(pieces) + 3),
        out_specs=[vmem] * len(pieces),
        out_shape=[jax.ShapeDtypeStruct((rows, width), jnp.bfloat16)] * len(pieces),
        scratch_shapes=[pltpu.VMEM((len(pieces) * rows, hidden_width), jnp.bfloat16)],
        cost_estimate=LARGE_COST,
        compiler_params=pltpu.CompilerParams(vmem_limit_bytes=28 * 1024 * 1024),
        name="expert",
    )(*others, column, *pieces, *weights)


def add_up(terms):
    total = terms[0].astype(jnp.float32)
    for term in terms[1:]:
        total = total + term.astype(jnp.float32)
    return total.astype(jnp.bfloat16)


def dense_layer(
    queries, cache, new_entries, lengths, moe_input, expert_ids, route_gains, weights, plan, group
):
    groups, experts = lax.axis_size("grp"), lax.axis_size("ep")
    far_flips = [(0, 2 * z) for z in range(1, experts // 2)][::-1]
    near_flips = [(2 * x, y) for x in range(groups // 2) for y in range(2)][1:]
    steps, trace_count, width = moe_input.shape
    rows = token_rows(group, expert_ids, route_gains, moe_input)
    first_flips = list(zip(far_flips, near_flips))
    last_flips = list(zip(near_flips, far_flips))
    line = [rows] + [across(rows, *flips) for flips in first_flips]
    own_line = line_rows(line, [])
    plane = [across(own_line, *flips) for flips in last_flips]
    entries, leaving = outgoing(cache, new_entries, lengths, plan, group, [own_line])
    received = [across(leaving[flip - 1], (flip, 0)) for flip in range(1, groups)]
    *weights, _ = fetch(weights, [own_line])
    own_sums, other_sums = expert([own_line, across(own_line, (1, 0))], weights)
    plane = gate(plane, [*received, own_sums])
    other_plane = [across(piece, (1, 0)) for piece in plane]
    own = expert(plane, weights)
    other = expert(other_plane, weights, own[:1])
    sums = [add_up([mine, across(theirs, (1, 0))]) for mine, theirs in zip(own, other)]
    terms = [across(term, *flips) for term, flips in zip(sums, last_flips)]
    contexts, migrated_cache, attended = attention(
        queries, cache, entries, lengths, plan, group, received, sums
    )
    own_term = add_up([own_sums, across(other_sums, (1, 0))])
    parts = line_sums([*terms, own_term], steps, trace_count, len(line), [attended])
    moe_output = add_up(
        [parts[0]] + [across(part, *flips) for part, flips in zip(parts[1:], first_flips)]
    )
    return contexts, migrated_cache, moe_output


def routed_layer(
    queries, cache, new_entries, lengths, moe_input, expert_ids, route_gains, weights, plan, group
):
    entries, leaving = outgoing(cache, new_entries, lengths, plan, group)
    received = [across(leaving[flip - 1], (flip, 0)) for flip in range(1, lax.axis_size("grp"))]
    contexts, migrated_cache, _ = attention(
        queries, cache, entries, lengths, plan, group, received
    )
    moe_output = routed_experts(moe_input, expert_ids, route_gains, *weights)
    return contexts, migrated_cache, moe_output


def slot_tables(route_ids, route_gains, expert_count, slot_count):
    token_count, top_count = route_ids.shape
    flat_ids = route_ids.reshape(-1)
    row_list = jnp.arange(flat_ids.shape[0], dtype=jnp.int32)
    same_expert = flat_ids[:, None] == flat_ids[None, :]
    earlier = row_list[None, :] < row_list[:, None]
    slot_rank = jnp.sum(jnp.where(same_expert & earlier, 1, 0), axis=1).astype(jnp.int32)
    slot_index = flat_ids * slot_count + slot_rank
    slot_hot = (
        slot_index[:, None] == jnp.arange(expert_count * slot_count, dtype=jnp.int32)[None, :]
    ).astype(jnp.float32)
    token_hot = (
        (row_list // top_count)[:, None] == jnp.arange(token_count, dtype=jnp.int32)[None, :]
    ).astype(jnp.float32)
    dispatch = jnp.dot(slot_hot.T, token_hot, precision=lax.Precision.HIGHEST)
    combine = jnp.dot(
        token_hot.T, slot_hot * route_gains.reshape(-1)[:, None], precision=lax.Precision.HIGHEST
    )
    return (dispatch, combine)


def expert_rows(token_rows, gate_slice, up_slice, down_slice):
    gate_out = jnp.dot(token_rows, gate_slice, preferred_element_type=jnp.float32)
    up_out = jnp.dot(token_rows, up_slice, preferred_element_type=jnp.float32)
    hidden = (jax.nn.silu(gate_out) * up_out).astype(jnp.bfloat16)
    return jnp.dot(hidden, down_slice, preferred_element_type=jnp.float32).astype(jnp.bfloat16)


def routed_experts(moe_input, expert_ids, route_gains, w_gate, w_up, w_down):
    groups, experts = lax.axis_size("grp"), lax.axis_size("ep")
    trace_count, model_width = moe_input.shape[1:]
    top_count = expert_ids.shape[3]
    slot_count = max(2, trace_count * top_count // experts)
    tables = partial(slot_tables, expert_count=experts, slot_count=slot_count)
    moe_list = []
    for step_index in range(moe_input.shape[0]):
        column_ids = expert_ids[step_index]
        column_gains = route_gains[step_index]
        dispatch_all, combine_all = jax.vmap(tables)(column_ids, column_gains)
        column_tokens = lax.all_gather(moe_input[step_index][None], "grp", axis=0, tiled=True)
        packed = jnp.einsum(
            "gsj,gjd->sgd",
            dispatch_all.astype(jnp.bfloat16),
            column_tokens,
            preferred_element_type=jnp.float32,
        )
        packed = packed.astype(jnp.bfloat16).reshape(experts, slot_count * groups, model_width)
        exchanged = lax.all_to_all(packed, "ep", split_axis=0, concat_axis=0, tiled=True)
        flat_rows = exchanged.reshape(-1, exchanged.shape[-1])
        partial_out = expert_rows(flat_rows, w_gate[0], w_up[0], w_down[0]).reshape(exchanged.shape)
        returned = lax.all_to_all(partial_out, "ep", split_axis=0, concat_axis=0, tiled=True)
        returned = returned.reshape(experts * slot_count, groups, model_width).astype(jnp.float32)
        token_terms = jnp.einsum(
            "gjs,sgd->gjd", combine_all, returned, precision=lax.Precision.HIGHEST
        )
        summed = lax.psum_scatter(
            token_terms.astype(jnp.bfloat16), "grp", scatter_dimension=0, tiled=True
        ).astype(jnp.float32)
        moe_list.append(summed[0].astype(jnp.bfloat16))
    return jnp.stack(moe_list)


def body(
    queries,
    cache,
    new_entries,
    lengths,
    moe_input,
    expert_ids,
    route_gains,
    w_gate,
    w_up,
    w_down,
    plan,
):
    queries, cache = jnp.swapaxes(queries, 2, 3), jnp.swapaxes(cache, 1, 2)
    plan, group = jnp.transpose(plan[:, 0], (1, 2, 0)), lax.axis_index("grp").reshape(1)
    every_expert = expert_ids.shape[3] == lax.axis_size("ep")
    layer = dense_layer if every_expert else routed_layer
    contexts, migrated_cache, moe_output = layer(
        queries,
        cache,
        new_entries,
        lengths,
        moe_input,
        expert_ids,
        route_gains,
        (w_gate, w_up, w_down),
        plan,
        group,
    )
    return contexts, jnp.swapaxes(migrated_cache, 1, 2), moe_output


def solution(mesh):
    return jax.shard_map(
        body,
        mesh=mesh,
        in_specs=(
            P(None, ("grp", "ep"), None, None),
            P(("grp", "ep"), None, None),
            P(None, ("grp", "ep"), None),
            P(("grp", "ep")),
            P(None, ("grp", "ep"), None),
            P(None, None, "ep", None),
            P(None, None, "ep", None),
            P("ep", None, "grp"),
            P("ep", None, "grp"),
            P("ep", "grp", None),
            P(None, "ep", None, None),
        ),
        out_specs=(
            P(None, ("grp", "ep"), None, None),
            P(("grp", "ep"), None, None),
            P(None, ("grp", "ep"), None),
        ),
        check_vma=False,
    )
```

```python
from functools import partial

import jax
import jax.numpy as jnp
from jax import lax
from jax.experimental import pallas as pl
from jax.experimental.pallas import tpu as pltpu
from jax.sharding import PartitionSpec as P

ROPE = 64


SCORE_SCALE = 192.0 ** (-0.5)


BOTH = ("grp", "ep")


GAIN_LANES = 128


PLANE_GROUPS = ((1, 2, 3), (0,))


SMALL_COST = pl.CostEstimate(flops=1, bytes_accessed=1, transcendentals=0)


LARGE_COST = pl.CostEstimate(flops=1, bytes_accessed=100_000_000, transcendentals=0)


KERNEL_PARAMS = pltpu.CompilerParams(vmem_limit_bytes=12 * 1024 * 1024)


def across(values, even_flip, odd_flip=None):
    groups, columns = lax.axis_size("grp"), lax.axis_size("ep")
    flips = (even_flip, odd_flip or even_flip)
    pairs = []
    for g in range(groups):
        for e in range(columns):
            grp_flip, ep_flip = flips[g % 2]
            pairs.append((g * columns + e, (g ^ grp_flip) * columns + (e ^ ep_flip)))
    return lax.ppermute(values, BOTH, pairs)


DONE = jax.ShapeDtypeStruct((8, 128), jnp.int32)


ANYWHERE = pl.BlockSpec(memory_space=pl.ANY)


def ignoring(kernel, first, count):
    return lambda *refs: kernel(*refs[:first], *refs[first + count :])


def gate_kernel(count, *refs):
    pass


def gate(arrays, others):
    count = len(arrays)
    return pl.pallas_call(
        partial(gate_kernel, count),
        in_specs=[ANYWHERE] * (count + len(others)),
        out_specs=[ANYWHERE] * count,
        out_shape=[jax.ShapeDtypeStruct(array.shape, array.dtype) for array in arrays],
        input_output_aliases={number: number for number in range(count)},
        compiler_params=KERNEL_PARAMS,
        cost_estimate=SMALL_COST,
        name="gate",
    )(*arrays, *others)


def choose_kernel(odd_ref, even_rows_ref, odd_rows_ref, out_ref):
    odd = odd_ref[0] == 1

    @pl.when(odd)
    def _():
        out_ref[...] = odd_rows_ref[...]

    @pl.when(jnp.logical_not(odd))
    def _():
        out_ref[...] = even_rows_ref[...]


def choose(odd, even_rows, odd_rows, others):
    vmem = pl.BlockSpec(memory_space=pltpu.VMEM)
    return pl.pallas_call(
        ignoring(choose_kernel, 0, len(others)),
        in_specs=[ANYWHERE] * len(others) + [pl.BlockSpec(memory_space=pltpu.SMEM), vmem, vmem],
        out_specs=vmem,
        out_shape=jax.ShapeDtypeStruct(even_rows.shape, even_rows.dtype),
        compiler_params=KERNEL_PARAMS,
        cost_estimate=SMALL_COST,
        name="choose",
    )(*others, odd, even_rows, odd_rows)


def add_if_odd_kernel(odd_ref, rows_ref, more_ref, out_ref):
    more = jnp.where(odd_ref[0] == 1, more_ref[...].astype(jnp.float32), 0.0)
    out_ref[...] = (rows_ref[...].astype(jnp.float32) + more).astype(out_ref.dtype)


def add_if_odd(odd, rows, more):
    vmem = pl.BlockSpec(memory_space=pltpu.VMEM)
    return pl.pallas_call(
        add_if_odd_kernel,
        in_specs=[pl.BlockSpec(memory_space=pltpu.SMEM), vmem, vmem],
        out_specs=vmem,
        out_shape=jax.ShapeDtypeStruct(rows.shape, rows.dtype),
        compiler_params=KERNEL_PARAMS,
        cost_estimate=SMALL_COST,
        name="add_if_odd",
    )(odd, rows, more)


def plan_entry(plan_ref, group, entry, field):
    return plan_ref[entry, field, group]


def stack_entries(new_entries_ref, stack_ref):
    steps, traces = new_entries_ref.shape[:2]
    stack_ref[...] = jnp.zeros_like(stack_ref)
    for step in range(steps):
        stack_ref[step * traces : (step + 1) * traces, :] = new_entries_ref[step].astype(jnp.float32)
    return stack_ref[...].astype(jnp.bfloat16)


def insert_entries(keys, entries, filled, trace, steps, traces):
    rows, capacity = entries.shape[0], keys.shape[1]
    row_index = lax.broadcasted_iota(jnp.int32, (rows, capacity), 0)
    column_index = lax.broadcasted_iota(jnp.int32, (rows, capacity), 1)
    place = ((column_index - filled) * traces + trace == row_index) & (column_index >= filled)
    spread = lax.dot_general(
        entries,
        place.astype(jnp.bfloat16),
        (((0,), (0,)), ((), ())),
        preferred_element_type=jnp.float32,
    )
    column_index = lax.broadcasted_iota(jnp.int32, keys.shape, 1)
    new = (column_index >= filled) & (column_index < filled + steps)
    return jnp.where(new, spread, keys.astype(jnp.float32)).astype(jnp.bfloat16)


def outgoing_slot(number, plan_ref, group_ref):
    group = group_ref[0]
    partner = group ^ (number + 1)
    slot = jnp.int32(0)
    for entry in range(2):
        goes = plan_entry(plan_ref, group, entry, 1) == partner
        slot = jnp.where(goes, plan_entry(plan_ref, group, entry, 0), slot)
    return slot


def gain_lanes(ids, gains):
    lane = lax.broadcasted_iota(jnp.int32, (ids.shape[0], GAIN_LANES), 1)
    dense = jnp.zeros(lane.shape, jnp.float32)
    for choice in range(ids.shape[1]):
        place = ids[:, choice : choice + 1]
        named = (lane >= 3 * place) & (lane < 3 * place + 3)
        dense = dense + jnp.where(named, gains[:, choice : choice + 1], 0.0)
    high = dense.astype(jnp.bfloat16).astype(jnp.float32)
    rest = dense - high
    middle = rest.astype(jnp.bfloat16).astype(jnp.float32)
    part = lane % 3
    parts = jnp.where(part == 0, high, jnp.where(part == 1, middle, rest - middle))
    return parts.astype(jnp.bfloat16)


def token_rows_kernel(group_ref, *refs):
    sources, rows_ref, targets, semaphores = refs[:3], refs[3], refs[4:7], refs[7]
    copies = [
        pltpu.make_async_copy(source, target, semaphores.at[number])
        for number, (source, target) in enumerate(zip(sources, targets))
    ]
    for copy in copies:
        copy.start()
    for copy in copies:
        copy.wait()
    ids_ref, gains_ref, tokens_ref = targets
    steps, _, width = tokens_ref.shape
    group = group_ref[0]
    for step in range(steps):
        rows_ref[step, :, :width] = tokens_ref[step]
        rows_ref[step, :, width:] = gain_lanes(ids_ref[step, group], gains_ref[step, group])


def token_rows(group, expert_ids, route_gains, moe_input):
    steps, traces, width = moe_input.shape
    sources = [expert_ids, route_gains, moe_input]
    return pl.pallas_call(
        token_rows_kernel,
        in_specs=[pl.BlockSpec(memory_space=pltpu.SMEM)]
        + [pl.BlockSpec(memory_space=pltpu.HBM)] * len(sources),
        out_specs=pl.BlockSpec(memory_space=pltpu.VMEM),
        out_shape=jax.ShapeDtypeStruct((steps, traces, width + GAIN_LANES), moe_input.dtype),
        scratch_shapes=[pltpu.VMEM(source.shape, source.dtype) for source in sources]
        + [pltpu.SemaphoreType.DMA((len(sources),))],
        compiler_params=KERNEL_PARAMS,
        cost_estimate=LARGE_COST,
        name="token_rows",
    )(group, *(pltpu.with_memory_space_constraint(source, pltpu.HBM) for source in sources))


def outgoing_kernel(others, lengths_ref, plan_ref, group_ref, cache_hbm, entries_hbm, *refs):
    out_refs = refs[:others]
    slots_ref, new_entries_ref, stack_ref, semaphores = refs[others:]
    slots = [outgoing_slot(number, plan_ref, group_ref) for number in range(others)]
    copies = [pltpu.make_async_copy(entries_hbm, new_entries_ref, semaphores.at[others])]
    for number, slot in enumerate(slots):
        copies.append(
            pltpu.make_async_copy(cache_hbm.at[slot], slots_ref.at[number], semaphores.at[number])
        )
    for copy in copies:
        copy.start()
    for copy in copies:
        copy.wait()
    steps, traces, _ = new_entries_ref.shape
    entries = stack_entries(new_entries_ref, stack_ref)
    for number, slot in enumerate(slots):
        out_refs[number][...] = insert_entries(
            slots_ref[number], entries, lengths_ref[slot], slot, steps, traces
        )


def outgoing(cache, new_entries, lengths, plan, group, behind=()):
    traces, width, capacity = cache.shape
    others = lax.axis_size("grp") - 1
    entry_rows = -(-new_entries.shape[0] * traces // 16) * 16
    smem, vmem = pl.BlockSpec(memory_space=pltpu.SMEM), pl.BlockSpec(memory_space=pltpu.VMEM)
    hbm = pl.BlockSpec(memory_space=pltpu.HBM)
    return pl.pallas_call(
        ignoring(partial(outgoing_kernel, others), 0, len(behind)),
        in_specs=[ANYWHERE] * len(behind) + [smem, smem, smem, hbm, hbm],
        out_specs=[vmem] * others,
        out_shape=[jax.ShapeDtypeStruct((width, capacity), cache.dtype)] * others,
        scratch_shapes=[
            pltpu.VMEM((others, width, capacity), cache.dtype),
            pltpu.VMEM(new_entries.shape, new_entries.dtype),
            pltpu.VMEM((entry_rows, width), jnp.float32),
            pltpu.SemaphoreType.DMA((others + 1,)),
        ],
        compiler_params=KERNEL_PARAMS,
        cost_estimate=LARGE_COST,
        name="outgoing",
    )(
        *behind,
        pltpu.with_memory_space_constraint(lengths, pltpu.HBM),
        pltpu.with_memory_space_constraint(plan, pltpu.HBM),
        group,
        pltpu.with_memory_space_constraint(cache, pltpu.HBM),
        pltpu.with_memory_space_constraint(new_entries, pltpu.HBM),
    )


def line_kernel(*refs):
    pieces, out_ref = refs[:-1], refs[-1]
    rows = [piece[step].astype(jnp.float32) for piece in pieces for step in range(piece.shape[0])]
    out_ref[...] = jnp.concatenate(rows, axis=0).astype(out_ref.dtype)


def line_rows(pieces, others):
    steps, traces, lanes = pieces[0].shape
    vmem = pl.BlockSpec(memory_space=pltpu.VMEM)
    return pl.pallas_call(
        ignoring(line_kernel, 0, len(others)),
        in_specs=[ANYWHERE] * len(others) + [vmem] * len(pieces),
        out_specs=vmem,
        out_shape=jax.ShapeDtypeStruct((len(pieces) * steps * traces, lanes), pieces[0].dtype),
        cost_estimate=LARGE_COST,
        compiler_params=KERNEL_PARAMS,
        name="line_rows",
    )(*others, *pieces)


def line_sums_kernel(odd_ref, *refs):
    steps, traces, _ = refs[-1].shape
    count = len(refs) - refs[0].shape[0] // (steps * traces)
    total = jnp.where(odd_ref[0] == 1, 0.0, refs[0][...].astype(jnp.float32))
    for term_ref in refs[1:count]:
        total = total + term_ref[...].astype(jnp.float32)
    for number, out_ref in enumerate(refs[count:]):
        for step in range(steps):
            first = (number * steps + step) * traces
            out_ref[step] = total[first : first + traces].astype(out_ref.dtype)


def line_sums(odd, terms, steps, traces, pieces, others):
    lanes = terms[0].shape[1]
    vmem = pl.BlockSpec(memory_space=pltpu.VMEM)
    return pl.pallas_call(
        ignoring(line_sums_kernel, 0, len(others)),
        in_specs=[ANYWHERE] * len(others)
        + [pl.BlockSpec(memory_space=pltpu.SMEM)]
        + [vmem] * len(terms),
        out_specs=[vmem] * pieces,
        out_shape=[jax.ShapeDtypeStruct((steps, traces, lanes), terms[0].dtype)] * pieces,
        compiler_params=KERNEL_PARAMS,
        cost_estimate=LARGE_COST,
        name="line_sums",
    )(*others, odd, *terms)


def attention_kernel(
    block, lengths_ref, queries_ref, cache_ref, entries_ref, contexts_ref, grown_ref, done_ref, stack_ref
):
    done_ref[...] = jnp.zeros_like(done_ref)
    grid_index = pl.program_id(0)
    step_count, _, width, heads = queries_ref.shape
    latent = contexts_ref.shape[3]
    traces = block * pl.num_programs(0)
    entries = stack_entries(entries_ref, stack_ref)
    for member in range(block):
        trace = grid_index * block + member
        filled = lengths_ref[trace]
        keys = insert_entries(
            cache_ref[member], entries, filled, trace, step_count, traces
        )
        grown_ref[member] = keys
        key_rows = jnp.transpose(keys)
        flat_queries = jnp.concatenate(
            [queries_ref[s, member] for s in range(step_count)], axis=1
        )
        scores = jnp.dot(key_rows, flat_queries, preferred_element_type=jnp.float32) * SCORE_SCALE
        position = lax.broadcasted_iota(jnp.int32, scores.shape, 0)
        step_of_column = lax.broadcasted_iota(jnp.int32, scores.shape, 1) // heads
        scores = jnp.where(position <= filled + step_of_column, scores, -jnp.inf)
        exp_scores = jnp.exp(scores - jnp.max(scores, axis=0, keepdims=True))
        weights = (exp_scores / jnp.sum(exp_scores, axis=0, keepdims=True)).astype(jnp.bfloat16)
        context = lax.dot_general(
            weights,
            key_rows[:, :latent],
            (((0,), (0,)), ((), ())),
            preferred_element_type=jnp.float32,
        )
        contexts_ref[:, member] = context.astype(jnp.bfloat16).reshape(step_count, heads, latent)


def place_kernel(plan_ref, group_ref, *refs):
    received_refs, (_, migrated_ref, semaphores) = refs[:-3], refs[-3:]
    group = group_ref[0]
    copies = []
    for number, received_ref in enumerate(received_refs):
        partner = group ^ (number + 1)
        lands, slot = jnp.bool_(False), jnp.int32(0)
        for entry in range(2):
            here = plan_entry(plan_ref, partner, entry, 1) == group
            lands = lands | here
            slot = jnp.where(here, plan_entry(plan_ref, group, entry, 0), slot)
        copies.append(
            (
                lands,
                pltpu.make_async_copy(received_ref, migrated_ref.at[slot], semaphores.at[number]),
            )
        )
    for lands, copy in copies:
        pl.when(lands)(copy.start)
    for lands, copy in copies:
        pl.when(lands)(copy.wait)


def place(grown, received, plan, group):
    smem = pl.BlockSpec(memory_space=pltpu.SMEM)
    return pl.pallas_call(
        place_kernel,
        in_specs=[smem, smem] + [ANYWHERE] * (len(received) + 1),
        out_specs=ANYWHERE,
        out_shape=jax.ShapeDtypeStruct(grown.shape, grown.dtype),
        input_output_aliases={len(received) + 2: 0},
        scratch_shapes=[pltpu.SemaphoreType.DMA((len(received),))],
        compiler_params=KERNEL_PARAMS,
        cost_estimate=LARGE_COST,
        name="place",
    )(plan, group, *received, grown)


def fetch_kernel(*refs):
    refs, done_ref, refs_semaphores = refs[:-2], refs[-2], refs[-1]
    done_ref[...] = jnp.zeros_like(done_ref)
    refs = (*refs, refs_semaphores)
    count = (len(refs) - 1) // 2
    copies = [
        pltpu.make_async_copy(source.at[0], target, refs[-1].at[number])
        for number, (source, target) in enumerate(zip(refs[:count], refs[count:-1]))
    ]
    for copy in copies:
        copy.start()
    for copy in copies:
        copy.wait()


def fetch(weights, others):
    weights = [pltpu.with_memory_space_constraint(weight, pltpu.HBM) for weight in weights]
    return pl.pallas_call(
        ignoring(fetch_kernel, 0, len(others)),
        in_specs=[ANYWHERE] * len(others)
        + [pl.BlockSpec(memory_space=pltpu.HBM)] * len(weights),
        out_specs=[pl.BlockSpec(memory_space=pltpu.VMEM)] * (len(weights) + 1),
        out_shape=[pltpu.VMEM(weight.shape[1:], weight.dtype) for weight in weights] + [DONE],
        scratch_shapes=[pltpu.SemaphoreType.DMA((len(weights),))],
        cost_estimate=LARGE_COST,
        compiler_params=KERNEL_PARAMS,
        name="fetch",
    )(*others, *weights)


def attention(queries, cache, new_entries, lengths, others=(), block=2):
    step_count, traces, width, heads = queries.shape
    capacity = cache.shape[2]
    latent = width - ROPE
    entry_rows = -(-step_count * traces // 16) * 16
    whole = lambda shape: pl.BlockSpec(shape, lambda t, *_: (0,) * len(shape))
    return pl.pallas_call(
        ignoring(partial(attention_kernel, block), 1, len(others)),
        grid_spec=pltpu.PrefetchScalarGridSpec(
            num_scalar_prefetch=1,
            grid=(traces // block,),
            in_specs=[ANYWHERE] * len(others)
            + [
                pl.BlockSpec((step_count, block, width, heads), lambda t, *_: (0, t, 0, 0)),
                pl.BlockSpec((block, width, capacity), lambda t, *_: (t, 0, 0)),
                whole(new_entries.shape),
            ],
            out_specs=[
                pl.BlockSpec((step_count, block, heads, latent), lambda t, *_: (0, t, 0, 0)),
                pl.BlockSpec((block, width, capacity), lambda t, *_: (t, 0, 0)),
                whole(DONE.shape),
            ],
            scratch_shapes=[pltpu.VMEM((entry_rows, width), jnp.float32)],
        ),
        out_shape=[
            jax.ShapeDtypeStruct((step_count, traces, heads, latent), jnp.bfloat16),
            jax.ShapeDtypeStruct(cache.shape, jnp.bfloat16),
            DONE,
        ],
        cost_estimate=LARGE_COST,
        compiler_params=KERNEL_PARAMS,
        name="attention",
    )(
        lengths,
        *others,
        pltpu.with_memory_space_constraint(queries, pltpu.HBM),
        pltpu.with_memory_space_constraint(cache, pltpu.HBM),
        new_entries,
    )


def expert_kernel(column_ref, *refs):
    count = (len(refs) - 4) // 2
    pieces, (gate_ref, up_ref, down_ref) = refs[:count], refs[count : count + 3]
    out_refs, hidden_ref = refs[count + 3 : -1], refs[-1]
    width, hidden_width = gate_ref.shape
    rows = pieces[0].shape[0]
    gain_parts = jnp.concatenate([piece[:, width:] for piece in pieces], axis=0).astype(jnp.float32)
    lane = lax.broadcasted_iota(jnp.int32, gain_parts.shape, 1)
    first_lane = column_ref[0] * 3
    gain = jnp.sum(
        jnp.where((lane >= first_lane) & (lane < first_lane + 3), gain_parts, 0.0),
        axis=1,
        keepdims=True,
    )
    tokens = jnp.concatenate([piece[:, :width] for piece in pieces], axis=0)
    gate_out = jnp.dot(tokens, gate_ref[...], preferred_element_type=jnp.float32)
    up_out = jnp.dot(tokens, up_ref[...], preferred_element_type=jnp.float32)
    hidden = gate_out / (1.0 + jnp.exp(-gate_out)) * up_out * gain
    hidden_ref[...] = hidden.astype(jnp.bfloat16)
    tile = 512 if width % 512 == 0 else width
    for first in range(0, width, tile):
        columns = slice(first, first + tile)
        products = jnp.dot(
            hidden_ref[...], down_ref[:, columns], preferred_element_type=jnp.float32
        ).astype(jnp.bfloat16)
        for number, out_ref in enumerate(out_refs):
            out_ref[:, columns] = products[number * rows : (number + 1) * rows]


def expert(pieces, weights, others=()):
    width, hidden_width = weights[0].shape
    rows = pieces[0].shape[0]
    vmem = pl.BlockSpec(memory_space=pltpu.VMEM)
    column = lax.axis_index("ep").astype(jnp.int32).reshape(1)
    return pl.pallas_call(
        ignoring(expert_kernel, 0, len(others)),
        in_specs=[ANYWHERE] * len(others)
        + [pl.BlockSpec(memory_space=pltpu.SMEM)]
        + [vmem] * (len(pieces) + 3),
        out_specs=[vmem] * len(pieces),
        out_shape=[jax.ShapeDtypeStruct((rows, width), jnp.bfloat16)] * len(pieces),
        scratch_shapes=[pltpu.VMEM((len(pieces) * rows, hidden_width), jnp.bfloat16)],
        cost_estimate=LARGE_COST,
        compiler_params=pltpu.CompilerParams(vmem_limit_bytes=28 * 1024 * 1024),
        name="expert",
    )(*others, column, *pieces, *weights)


def add_up(terms):
    total = terms[0].astype(jnp.float32)
    for term in terms[1:]:
        total = total + term.astype(jnp.float32)
    return total.astype(jnp.bfloat16)


def dense_layer(
    queries, cache, new_entries, lengths, moe_input, expert_ids, route_gains, weights, plan, group
):
    groups = lax.axis_size("grp")
    steps, trace_count, _ = moe_input.shape
    core, neighbour, skip, opposite = (1, 0), (0, 2), (0, 4), (0, 6)
    beside, above, diagonal = (0, 1), (2, 0), (2, 1)
    first_flips = [(opposite, beside), (skip, above), (neighbour, diagonal)]
    odd = (lax.axis_index("grp") % 2).reshape(1)
    rows = token_rows(group, expert_ids, route_gains, moe_input)
    line = [rows] + [across(rows, *flips) for flips in first_flips]
    own = line_rows(line, [])

    pieces = [
        across(own, *flips)
        for flips in ((beside, skip), (above, neighbour), (diagonal, opposite))
    ]
    *weights, _ = fetch(weights, [own])
    own_sums, other_sums = expert([own, across(own, core)], weights)
    pieces = gate(pieces, [own_sums])
    other_pieces = [across(piece, core) for piece in pieces]
    mine = expert(pieces, weights)
    theirs = expert(other_pieces, weights, mine[:1])
    sums_3, sums_2, sums_1 = [
        add_up([own_part, across(part, core)]) for own_part, part in zip(mine[::-1], theirs[::-1])
    ]

    term_3 = across(sums_3, diagonal, neighbour)
    contexts, grown, attended = attention(queries, cache, new_entries, lengths, [sums_3])
    (sums_2,) = gate([sums_2], [term_3, attended])
    term_2 = across(sums_2, above, neighbour)
    term_1 = across(add_if_odd(odd, sums_1, term_3), beside, skip)
    leaving = outgoing(cache, new_entries, lengths, plan, group, [sums_2])
    received = [across(leaving[flip - 1], (flip, 0)) for flip in range(1, groups)]
    own_term = add_up([own_sums, across(other_sums, core)])
    parts = line_sums(
        odd, [term_3, term_1, term_2, own_term], steps, trace_count, len(line), leaving[:1]
    )
    moe_output = add_up(
        [parts[0]] + [across(part, *flips) for part, flips in zip(parts[1:], first_flips)]
    )
    return contexts, place(grown, received, plan, group), moe_output


def routed_layer(
    queries, cache, new_entries, lengths, moe_input, expert_ids, route_gains, weights, plan, group
):
    leaving = outgoing(cache, new_entries, lengths, plan, group)
    received = [across(leaving[flip - 1], (flip, 0)) for flip in range(1, lax.axis_size("grp"))]
    contexts, grown, _ = attention(queries, cache, new_entries, lengths)
    migrated_cache = place(grown, received, plan, group)
    moe_output = routed_experts(moe_input, expert_ids, route_gains, *weights)
    return contexts, migrated_cache, moe_output


def slot_tables(route_ids, route_gains, expert_count, slot_count):
    token_count, top_count = route_ids.shape
    flat_ids = route_ids.reshape(-1)
    row_list = jnp.arange(flat_ids.shape[0], dtype=jnp.int32)
    same_expert = flat_ids[:, None] == flat_ids[None, :]
    earlier = row_list[None, :] < row_list[:, None]
    slot_rank = jnp.sum(jnp.where(same_expert & earlier, 1, 0), axis=1).astype(jnp.int32)
    slot_index = flat_ids * slot_count + slot_rank
    slot_hot = (
        slot_index[:, None] == jnp.arange(expert_count * slot_count, dtype=jnp.int32)[None, :]
    ).astype(jnp.float32)
    token_hot = (
        (row_list // top_count)[:, None] == jnp.arange(token_count, dtype=jnp.int32)[None, :]
    ).astype(jnp.float32)
    dispatch = jnp.dot(slot_hot.T, token_hot, precision=lax.Precision.HIGHEST)
    combine = jnp.dot(
        token_hot.T, slot_hot * route_gains.reshape(-1)[:, None], precision=lax.Precision.HIGHEST
    )
    return (dispatch, combine)


def expert_rows(token_rows, gate_slice, up_slice, down_slice):
    gate_out = jnp.dot(token_rows, gate_slice, preferred_element_type=jnp.float32)
    up_out = jnp.dot(token_rows, up_slice, preferred_element_type=jnp.float32)
    hidden = (jax.nn.silu(gate_out) * up_out).astype(jnp.bfloat16)
    return jnp.dot(hidden, down_slice, preferred_element_type=jnp.float32).astype(jnp.bfloat16)


def routed_experts(moe_input, expert_ids, route_gains, w_gate, w_up, w_down):
    groups, experts = lax.axis_size("grp"), lax.axis_size("ep")
    trace_count, model_width = moe_input.shape[1:]
    top_count = expert_ids.shape[3]
    slot_count = max(2, trace_count * top_count // experts)
    tables = partial(slot_tables, expert_count=experts, slot_count=slot_count)
    moe_list = []
    for step_index in range(moe_input.shape[0]):
        column_ids = expert_ids[step_index]
        column_gains = route_gains[step_index]
        dispatch_all, combine_all = jax.vmap(tables)(column_ids, column_gains)
        column_tokens = lax.all_gather(moe_input[step_index][None], "grp", axis=0, tiled=True)
        packed = jnp.einsum(
            "gsj,gjd->sgd",
            dispatch_all.astype(jnp.bfloat16),
            column_tokens,
            preferred_element_type=jnp.float32,
        )
        packed = packed.astype(jnp.bfloat16).reshape(experts, slot_count * groups, model_width)
        exchanged = lax.all_to_all(packed, "ep", split_axis=0, concat_axis=0, tiled=True)
        flat_rows = exchanged.reshape(-1, exchanged.shape[-1])
        partial_out = expert_rows(flat_rows, w_gate[0], w_up[0], w_down[0]).reshape(exchanged.shape)
        returned = lax.all_to_all(partial_out, "ep", split_axis=0, concat_axis=0, tiled=True)
        returned = returned.reshape(experts * slot_count, groups, model_width).astype(jnp.float32)
        token_terms = jnp.einsum(
            "gjs,sgd->gjd", combine_all, returned, precision=lax.Precision.HIGHEST
        )
        summed = lax.psum_scatter(
            token_terms.astype(jnp.bfloat16), "grp", scatter_dimension=0, tiled=True
        ).astype(jnp.float32)
        moe_list.append(summed[0].astype(jnp.bfloat16))
    return jnp.stack(moe_list)


def body(
    queries,
    cache,
    new_entries,
    lengths,
    moe_input,
    expert_ids,
    route_gains,
    w_gate,
    w_up,
    w_down,
    plan,
):
    queries, cache = jnp.swapaxes(queries, 2, 3), jnp.swapaxes(cache, 1, 2)
    plan, group = jnp.transpose(plan[:, 0], (1, 2, 0)), lax.axis_index("grp").reshape(1)
    every_expert = expert_ids.shape[3] == lax.axis_size("ep")
    every_expert = every_expert and (lax.axis_size("grp"), lax.axis_size("ep")) == (4, 8)
    layer = dense_layer if every_expert else routed_layer
    contexts, migrated_cache, moe_output = layer(
        queries,
        cache,
        new_entries,
        lengths,
        moe_input,
        expert_ids,
        route_gains,
        (w_gate, w_up, w_down),
        plan,
        group,
    )
    return contexts, jnp.swapaxes(migrated_cache, 1, 2), moe_output


def solution(mesh):
    return jax.shard_map(
        body,
        mesh=mesh,
        in_specs=(
            P(None, ("grp", "ep"), None, None),
            P(("grp", "ep"), None, None),
            P(None, ("grp", "ep"), None),
            P(("grp", "ep")),
            P(None, ("grp", "ep"), None),
            P(None, None, "ep", None),
            P(None, None, "ep", None),
            P("ep", None, "grp"),
            P("ep", None, "grp"),
            P("ep", "grp", None),
            P(None, "ep", None, None),
        ),
        out_specs=(
            P(None, ("grp", "ep"), None, None),
            P(("grp", "ep"), None, None),
            P(None, ("grp", "ep"), None),
        ),
        check_vma=False,
    )
```

```python
from functools import partial

import jax
import jax.numpy as jnp
from jax import lax
from jax.experimental import pallas as pl
from jax.experimental.pallas import tpu as pltpu
from jax.sharding import PartitionSpec as P

ROPE = 64


SCORE_SCALE = 192.0 ** (-0.5)


BOTH = ("grp", "ep")


GAIN_LANES = 128


PLANE_GROUPS = ((1, 2, 3), (0,))


SMALL_COST = pl.CostEstimate(flops=1, bytes_accessed=1, transcendentals=0)


LARGE_COST = pl.CostEstimate(flops=1, bytes_accessed=100_000_000, transcendentals=0)


KERNEL_PARAMS = pltpu.CompilerParams(vmem_limit_bytes=12 * 1024 * 1024)


def across(values, even_flip, odd_flip=None):
    groups, columns = lax.axis_size("grp"), lax.axis_size("ep")
    flips = (even_flip, odd_flip or even_flip)
    pairs = []
    for g in range(groups):
        for e in range(columns):
            grp_flip, ep_flip = flips[g % 2]
            pairs.append((g * columns + e, (g ^ grp_flip) * columns + (e ^ ep_flip)))
    return lax.ppermute(values, BOTH, pairs)


DONE = jax.ShapeDtypeStruct((8, 128), jnp.int32)


ANYWHERE = pl.BlockSpec(memory_space=pl.ANY)


def ignoring(kernel, first, count):
    return lambda *refs: kernel(*refs[:first], *refs[first + count :])


def gate_kernel(count, *refs):
    pass


def gate(arrays, others):
    count = len(arrays)
    return pl.pallas_call(
        partial(gate_kernel, count),
        in_specs=[ANYWHERE] * (count + len(others)),
        out_specs=[ANYWHERE] * count,
        out_shape=[jax.ShapeDtypeStruct(array.shape, array.dtype) for array in arrays],
        input_output_aliases={number: number for number in range(count)},
        compiler_params=KERNEL_PARAMS,
        cost_estimate=SMALL_COST,
        name="gate",
    )(*arrays, *others)


def choose_kernel(odd_ref, even_rows_ref, odd_rows_ref, out_ref):
    odd = odd_ref[0] == 1

    @pl.when(odd)
    def _():
        out_ref[...] = odd_rows_ref[...]

    @pl.when(jnp.logical_not(odd))
    def _():
        out_ref[...] = even_rows_ref[...]


def choose(odd, even_rows, odd_rows, others):
    vmem = pl.BlockSpec(memory_space=pltpu.VMEM)
    return pl.pallas_call(
        ignoring(choose_kernel, 0, len(others)),
        in_specs=[ANYWHERE] * len(others) + [pl.BlockSpec(memory_space=pltpu.SMEM), vmem, vmem],
        out_specs=vmem,
        out_shape=jax.ShapeDtypeStruct(even_rows.shape, even_rows.dtype),
        compiler_params=KERNEL_PARAMS,
        cost_estimate=SMALL_COST,
        name="choose",
    )(*others, odd, even_rows, odd_rows)


def add_if_odd_kernel(odd_ref, rows_ref, more_ref, out_ref):
    more = jnp.where(odd_ref[0] == 1, more_ref[...].astype(jnp.float32), 0.0)
    out_ref[...] = (rows_ref[...].astype(jnp.float32) + more).astype(out_ref.dtype)


def add_if_odd(odd, rows, more):
    vmem = pl.BlockSpec(memory_space=pltpu.VMEM)
    return pl.pallas_call(
        add_if_odd_kernel,
        in_specs=[pl.BlockSpec(memory_space=pltpu.SMEM), vmem, vmem],
        out_specs=vmem,
        out_shape=jax.ShapeDtypeStruct(rows.shape, rows.dtype),
        compiler_params=KERNEL_PARAMS,
        cost_estimate=SMALL_COST,
        name="add_if_odd",
    )(odd, rows, more)


def plan_entry(plan_ref, group, entry, field):
    return plan_ref[entry, field, group]


def stack_entries(new_entries_ref, stack_ref):
    steps, traces = new_entries_ref.shape[:2]
    stack_ref[...] = jnp.zeros_like(stack_ref)
    for step in range(steps):
        stack_ref[step * traces : (step + 1) * traces, :] = new_entries_ref[step].astype(jnp.float32)
    return stack_ref[...].astype(jnp.bfloat16)


def insert_entries(keys, entries, filled, trace, steps, traces):
    rows, capacity = entries.shape[0], keys.shape[1]
    row_index = lax.broadcasted_iota(jnp.int32, (rows, capacity), 0)
    column_index = lax.broadcasted_iota(jnp.int32, (rows, capacity), 1)
    place = ((column_index - filled) * traces + trace == row_index) & (column_index >= filled)
    spread = lax.dot_general(
        entries,
        place.astype(jnp.bfloat16),
        (((0,), (0,)), ((), ())),
        preferred_element_type=jnp.float32,
    )
    column_index = lax.broadcasted_iota(jnp.int32, keys.shape, 1)
    new = (column_index >= filled) & (column_index < filled + steps)
    return jnp.where(new, spread, keys.astype(jnp.float32)).astype(jnp.bfloat16)


def outgoing_slot(number, plan_ref, group_ref):
    group = group_ref[0]
    partner = group ^ (number + 1)
    slot = jnp.int32(0)
    for entry in range(2):
        goes = plan_entry(plan_ref, group, entry, 1) == partner
        slot = jnp.where(goes, plan_entry(plan_ref, group, entry, 0), slot)
    return slot


def gain_lanes(ids, gains):
    lane = lax.broadcasted_iota(jnp.int32, (ids.shape[0], GAIN_LANES), 1)
    dense = jnp.zeros(lane.shape, jnp.float32)
    for choice in range(ids.shape[1]):
        place = ids[:, choice : choice + 1]
        named = (lane >= 3 * place) & (lane < 3 * place + 3)
        dense = dense + jnp.where(named, gains[:, choice : choice + 1], 0.0)
    high = dense.astype(jnp.bfloat16).astype(jnp.float32)
    rest = dense - high
    middle = rest.astype(jnp.bfloat16).astype(jnp.float32)
    part = lane % 3
    parts = jnp.where(part == 0, high, jnp.where(part == 1, middle, rest - middle))
    return parts.astype(jnp.bfloat16)


def token_rows_kernel(group_ref, *refs):
    sources, rows_ref, targets, semaphores = refs[:3], refs[3], refs[4:7], refs[7]
    copies = [
        pltpu.make_async_copy(source, target, semaphores.at[number])
        for number, (source, target) in enumerate(zip(sources, targets))
    ]
    for copy in copies:
        copy.start()
    for copy in copies:
        copy.wait()
    ids_ref, gains_ref, tokens_ref = targets
    steps, _, width = tokens_ref.shape
    group = group_ref[0]
    for step in range(steps):
        rows_ref[step, :, :width] = tokens_ref[step]
        rows_ref[step, :, width:] = gain_lanes(ids_ref[step, group], gains_ref[step, group])


def token_rows(group, expert_ids, route_gains, moe_input):
    steps, traces, width = moe_input.shape
    sources = [expert_ids, route_gains, moe_input]
    return pl.pallas_call(
        token_rows_kernel,
        in_specs=[pl.BlockSpec(memory_space=pltpu.SMEM)]
        + [pl.BlockSpec(memory_space=pltpu.HBM)] * len(sources),
        out_specs=pl.BlockSpec(memory_space=pltpu.VMEM),
        out_shape=jax.ShapeDtypeStruct((steps, traces, width + GAIN_LANES), moe_input.dtype),
        scratch_shapes=[pltpu.VMEM(source.shape, source.dtype) for source in sources]
        + [pltpu.SemaphoreType.DMA((len(sources),))],
        compiler_params=KERNEL_PARAMS,
        cost_estimate=LARGE_COST,
        name="token_rows",
    )(group, *(pltpu.with_memory_space_constraint(source, pltpu.HBM) for source in sources))


def outgoing_kernel(others, lengths_ref, plan_ref, group_ref, cache_hbm, entries_hbm, *refs):
    out_refs = refs[:others]
    slots_ref, new_entries_ref, stack_ref, semaphores = refs[others:]
    slots = [outgoing_slot(number, plan_ref, group_ref) for number in range(others)]
    copies = [pltpu.make_async_copy(entries_hbm, new_entries_ref, semaphores.at[others])]
    for number, slot in enumerate(slots):
        copies.append(
            pltpu.make_async_copy(cache_hbm.at[slot], slots_ref.at[number], semaphores.at[number])
        )
    for copy in copies:
        copy.start()
    for copy in copies:
        copy.wait()
    steps, traces, _ = new_entries_ref.shape
    entries = stack_entries(new_entries_ref, stack_ref)
    for number, slot in enumerate(slots):
        out_refs[number][...] = insert_entries(
            slots_ref[number], entries, lengths_ref[slot], slot, steps, traces
        )


def outgoing(cache, new_entries, lengths, plan, group, behind=()):
    traces, width, capacity = cache.shape
    others = lax.axis_size("grp") - 1
    entry_rows = -(-new_entries.shape[0] * traces // 16) * 16
    smem, vmem = pl.BlockSpec(memory_space=pltpu.SMEM), pl.BlockSpec(memory_space=pltpu.VMEM)
    hbm = pl.BlockSpec(memory_space=pltpu.HBM)
    return pl.pallas_call(
        ignoring(partial(outgoing_kernel, others), 0, len(behind)),
        in_specs=[ANYWHERE] * len(behind) + [smem, smem, smem, hbm, hbm],
        out_specs=[vmem] * others,
        out_shape=[jax.ShapeDtypeStruct((width, capacity), cache.dtype)] * others,
        scratch_shapes=[
            pltpu.VMEM((others, width, capacity), cache.dtype),
            pltpu.VMEM(new_entries.shape, new_entries.dtype),
            pltpu.VMEM((entry_rows, width), jnp.float32),
            pltpu.SemaphoreType.DMA((others + 1,)),
        ],
        compiler_params=KERNEL_PARAMS,
        cost_estimate=LARGE_COST,
        name="outgoing",
    )(
        *behind,
        pltpu.with_memory_space_constraint(lengths, pltpu.HBM),
        pltpu.with_memory_space_constraint(plan, pltpu.HBM),
        group,
        pltpu.with_memory_space_constraint(cache, pltpu.HBM),
        pltpu.with_memory_space_constraint(new_entries, pltpu.HBM),
    )


def line_kernel(*refs):
    pieces, out_ref = refs[:-1], refs[-1]
    rows = [piece[step].astype(jnp.float32) for piece in pieces for step in range(piece.shape[0])]
    out_ref[...] = jnp.concatenate(rows, axis=0).astype(out_ref.dtype)


def line_rows(pieces, others):
    steps, traces, lanes = pieces[0].shape
    vmem = pl.BlockSpec(memory_space=pltpu.VMEM)
    return pl.pallas_call(
        ignoring(line_kernel, 0, len(others)),
        in_specs=[ANYWHERE] * len(others) + [vmem] * len(pieces),
        out_specs=vmem,
        out_shape=jax.ShapeDtypeStruct((len(pieces) * steps * traces, lanes), pieces[0].dtype),
        cost_estimate=LARGE_COST,
        compiler_params=KERNEL_PARAMS,
        name="line_rows",
    )(*others, *pieces)


def line_sums_kernel(odd_ref, *refs):
    steps, traces, _ = refs[-1].shape
    count = len(refs) - refs[0].shape[0] // (steps * traces)
    total = jnp.where(odd_ref[0] == 1, 0.0, refs[0][...].astype(jnp.float32))
    for term_ref in refs[1:count]:
        total = total + term_ref[...].astype(jnp.float32)
    for number, out_ref in enumerate(refs[count:]):
        for step in range(steps):
            first = (number * steps + step) * traces
            out_ref[step] = total[first : first + traces].astype(out_ref.dtype)


def line_sums(odd, terms, steps, traces, pieces, others):
    lanes = terms[0].shape[1]
    vmem = pl.BlockSpec(memory_space=pltpu.VMEM)
    return pl.pallas_call(
        ignoring(line_sums_kernel, 0, len(others)),
        in_specs=[ANYWHERE] * len(others)
        + [pl.BlockSpec(memory_space=pltpu.SMEM)]
        + [vmem] * len(terms),
        out_specs=[vmem] * pieces,
        out_shape=[jax.ShapeDtypeStruct((steps, traces, lanes), terms[0].dtype)] * pieces,
        compiler_params=KERNEL_PARAMS,
        cost_estimate=LARGE_COST,
        name="line_sums",
    )(*others, odd, *terms)


def attention_kernel(
    block, lengths_ref, queries_ref, cache_ref, entries_ref, contexts_ref, grown_ref, done_ref, stack_ref
):
    done_ref[...] = jnp.zeros_like(done_ref)
    grid_index = pl.program_id(0)
    step_count, _, width, heads = queries_ref.shape
    latent = contexts_ref.shape[3]
    traces = block * pl.num_programs(0)
    entries = stack_entries(entries_ref, stack_ref)
    for member in range(block):
        trace = grid_index * block + member
        filled = lengths_ref[trace]
        keys = insert_entries(
            cache_ref[member], entries, filled, trace, step_count, traces
        )
        grown_ref[member] = keys
        key_rows = jnp.transpose(keys)
        flat_queries = jnp.concatenate(
            [queries_ref[s, member] for s in range(step_count)], axis=1
        )
        scores = jnp.dot(key_rows, flat_queries, preferred_element_type=jnp.float32) * SCORE_SCALE
        position = lax.broadcasted_iota(jnp.int32, scores.shape, 0)
        step_of_column = lax.broadcasted_iota(jnp.int32, scores.shape, 1) // heads
        scores = jnp.where(position <= filled + step_of_column, scores, -jnp.inf)
        exp_scores = jnp.exp(scores - jnp.max(scores, axis=0, keepdims=True))
        weights = (exp_scores / jnp.sum(exp_scores, axis=0, keepdims=True)).astype(jnp.bfloat16)
        context = lax.dot_general(
            weights,
            key_rows[:, :latent],
            (((0,), (0,)), ((), ())),
            preferred_element_type=jnp.float32,
        )
        contexts_ref[:, member] = context.astype(jnp.bfloat16).reshape(step_count, heads, latent)


def place_kernel(plan_ref, group_ref, *refs):
    received_refs, (_, migrated_ref, semaphores) = refs[:-3], refs[-3:]
    group = group_ref[0]
    copies = []
    for number, received_ref in enumerate(received_refs):
        partner = group ^ (number + 1)
        lands, slot = jnp.bool_(False), jnp.int32(0)
        for entry in range(2):
            here = plan_entry(plan_ref, partner, entry, 1) == group
            lands = lands | here
            slot = jnp.where(here, plan_entry(plan_ref, group, entry, 0), slot)
        copies.append(
            (
                lands,
                pltpu.make_async_copy(received_ref, migrated_ref.at[slot], semaphores.at[number]),
            )
        )
    for lands, copy in copies:
        pl.when(lands)(copy.start)
    for lands, copy in copies:
        pl.when(lands)(copy.wait)


def place(grown, received, plan, group):
    smem = pl.BlockSpec(memory_space=pltpu.SMEM)
    return pl.pallas_call(
        place_kernel,
        in_specs=[smem, smem] + [ANYWHERE] * (len(received) + 1),
        out_specs=ANYWHERE,
        out_shape=jax.ShapeDtypeStruct(grown.shape, grown.dtype),
        input_output_aliases={len(received) + 2: 0},
        scratch_shapes=[pltpu.SemaphoreType.DMA((len(received),))],
        compiler_params=KERNEL_PARAMS,
        cost_estimate=LARGE_COST,
        name="place",
    )(plan, group, *received, grown)


def fetch_kernel(*refs):
    refs, done_ref, refs_semaphores = refs[:-2], refs[-2], refs[-1]
    done_ref[...] = jnp.zeros_like(done_ref)
    refs = (*refs, refs_semaphores)
    count = (len(refs) - 1) // 2
    copies = [
        pltpu.make_async_copy(source.at[0], target, refs[-1].at[number])
        for number, (source, target) in enumerate(zip(refs[:count], refs[count:-1]))
    ]
    for copy in copies:
        copy.start()
    for copy in copies:
        copy.wait()


def fetch(weights, others):
    weights = [pltpu.with_memory_space_constraint(weight, pltpu.HBM) for weight in weights]
    return pl.pallas_call(
        ignoring(fetch_kernel, 0, len(others)),
        in_specs=[ANYWHERE] * len(others)
        + [pl.BlockSpec(memory_space=pltpu.HBM)] * len(weights),
        out_specs=[pl.BlockSpec(memory_space=pltpu.VMEM)] * (len(weights) + 1),
        out_shape=[pltpu.VMEM(weight.shape[1:], weight.dtype) for weight in weights] + [DONE],
        scratch_shapes=[pltpu.SemaphoreType.DMA((len(weights),))],
        cost_estimate=LARGE_COST,
        compiler_params=KERNEL_PARAMS,
        name="fetch",
    )(*others, *weights)


def attention(queries, cache, new_entries, lengths, others=(), block=2):
    step_count, traces, width, heads = queries.shape
    capacity = cache.shape[2]
    latent = width - ROPE
    entry_rows = -(-step_count * traces // 16) * 16
    whole = lambda shape: pl.BlockSpec(shape, lambda t, *_: (0,) * len(shape))
    return pl.pallas_call(
        ignoring(partial(attention_kernel, block), 1, len(others)),
        grid_spec=pltpu.PrefetchScalarGridSpec(
            num_scalar_prefetch=1,
            grid=(traces // block,),
            in_specs=[ANYWHERE] * len(others)
            + [
                pl.BlockSpec((step_count, block, width, heads), lambda t, *_: (0, t, 0, 0)),
                pl.BlockSpec((block, width, capacity), lambda t, *_: (t, 0, 0)),
                whole(new_entries.shape),
            ],
            out_specs=[
                pl.BlockSpec((step_count, block, heads, latent), lambda t, *_: (0, t, 0, 0)),
                pl.BlockSpec((block, width, capacity), lambda t, *_: (t, 0, 0)),
                whole(DONE.shape),
            ],
            scratch_shapes=[pltpu.VMEM((entry_rows, width), jnp.float32)],
        ),
        out_shape=[
            jax.ShapeDtypeStruct((step_count, traces, heads, latent), jnp.bfloat16),
            jax.ShapeDtypeStruct(cache.shape, jnp.bfloat16),
            DONE,
        ],
        cost_estimate=LARGE_COST,
        compiler_params=KERNEL_PARAMS,
        name="attention",
    )(
        lengths,
        *others,
        pltpu.with_memory_space_constraint(queries, pltpu.HBM),
        pltpu.with_memory_space_constraint(cache, pltpu.HBM),
        new_entries,
    )


def expert_kernel(column_ref, *refs):
    count = (len(refs) - 4) // 2
    pieces, (gate_ref, up_ref, down_ref) = refs[:count], refs[count : count + 3]
    out_refs, hidden_ref = refs[count + 3 : -1], refs[-1]
    width, hidden_width = gate_ref.shape
    rows = pieces[0].shape[0]
    gain_parts = jnp.concatenate([piece[:, width:] for piece in pieces], axis=0).astype(jnp.float32)
    lane = lax.broadcasted_iota(jnp.int32, gain_parts.shape, 1)
    first_lane = column_ref[0] * 3
    gain = jnp.sum(
        jnp.where((lane >= first_lane) & (lane < first_lane + 3), gain_parts, 0.0),
        axis=1,
        keepdims=True,
    )
    tokens = jnp.concatenate([piece[:, :width] for piece in pieces], axis=0)
    gate_out = jnp.dot(tokens, gate_ref[...], preferred_element_type=jnp.float32)
    up_out = jnp.dot(tokens, up_ref[...], preferred_element_type=jnp.float32)
    hidden = gate_out / (1.0 + jnp.exp(-gate_out)) * up_out * gain
    hidden_ref[...] = hidden.astype(jnp.bfloat16)
    tile = 512 if width % 512 == 0 else width
    for first in range(0, width, tile):
        columns = slice(first, first + tile)
        products = jnp.dot(
            hidden_ref[...], down_ref[:, columns], preferred_element_type=jnp.float32
        ).astype(jnp.bfloat16)
        for number, out_ref in enumerate(out_refs):
            out_ref[:, columns] = products[number * rows : (number + 1) * rows]


def expert(pieces, weights, others=()):
    width, hidden_width = weights[0].shape
    rows = pieces[0].shape[0]
    vmem = pl.BlockSpec(memory_space=pltpu.VMEM)
    column = lax.axis_index("ep").astype(jnp.int32).reshape(1)
    return pl.pallas_call(
        ignoring(expert_kernel, 0, len(others)),
        in_specs=[ANYWHERE] * len(others)
        + [pl.BlockSpec(memory_space=pltpu.SMEM)]
        + [vmem] * (len(pieces) + 3),
        out_specs=[vmem] * len(pieces),
        out_shape=[jax.ShapeDtypeStruct((rows, width), jnp.bfloat16)] * len(pieces),
        scratch_shapes=[pltpu.VMEM((len(pieces) * rows, hidden_width), jnp.bfloat16)],
        cost_estimate=LARGE_COST,
        compiler_params=pltpu.CompilerParams(vmem_limit_bytes=28 * 1024 * 1024),
        name="expert",
    )(*others, column, *pieces, *weights)


def add_up(terms):
    total = terms[0].astype(jnp.float32)
    for term in terms[1:]:
        total = total + term.astype(jnp.float32)
    return total.astype(jnp.bfloat16)


def dense_layer(
    queries, cache, new_entries, lengths, moe_input, expert_ids, route_gains, weights, plan, group
):
    groups = lax.axis_size("grp")
    steps, trace_count, _ = moe_input.shape
    core, neighbour, skip, opposite = (1, 0), (0, 2), (0, 4), (0, 6)
    beside, above, diagonal = (0, 1), (2, 0), (2, 1)
    first_flips = [(opposite, beside), (skip, above), (neighbour, diagonal)]
    odd = (lax.axis_index("grp") % 2).reshape(1)
    rows = token_rows(group, expert_ids, route_gains, moe_input)
    line = [rows] + [across(rows, *flips) for flips in first_flips]
    own = line_rows(line, [])

    pieces = [
        across(own, *flips)
        for flips in ((beside, skip), (above, neighbour), (diagonal, opposite))
    ]
    *weights, _ = fetch(weights, [own])
    (own_sums,) = expert([own], weights)
    pieces = gate(pieces, [own_sums])
    other_pieces = [across(piece, core) for piece in [*pieces, own]]
    mine = expert(pieces, weights)
    *theirs, other_sums = expert(other_pieces, weights, mine[:1])
    sums_3, sums_2, sums_1 = [
        add_up([own_part, across(part, core)]) for own_part, part in zip(mine[::-1], theirs[::-1])
    ]

    term_3 = across(sums_3, diagonal, neighbour)
    contexts, grown, attended = attention(queries, cache, new_entries, lengths, [sums_3])
    (sums_2,) = gate([sums_2], [term_3, attended])
    term_2 = across(sums_2, above, neighbour)
    term_1 = across(add_if_odd(odd, sums_1, term_3), beside, skip)
    leaving = outgoing(cache, new_entries, lengths, plan, group, [sums_2])
    received = [across(leaving[flip - 1], (flip, 0)) for flip in range(1, groups)]
    own_term = add_up([own_sums, across(other_sums, core)])
    parts = line_sums(
        odd, [term_3, term_1, term_2, own_term], steps, trace_count, len(line), leaving[:1]
    )
    moe_output = add_up(
        [parts[0]] + [across(part, *flips) for part, flips in zip(parts[1:], first_flips)]
    )
    return contexts, place(grown, received, plan, group), moe_output


def routed_layer(
    queries, cache, new_entries, lengths, moe_input, expert_ids, route_gains, weights, plan, group
):
    leaving = outgoing(cache, new_entries, lengths, plan, group)
    received = [across(leaving[flip - 1], (flip, 0)) for flip in range(1, lax.axis_size("grp"))]
    contexts, grown, _ = attention(queries, cache, new_entries, lengths)
    migrated_cache = place(grown, received, plan, group)
    moe_output = routed_experts(moe_input, expert_ids, route_gains, *weights)
    return contexts, migrated_cache, moe_output


def slot_tables(route_ids, route_gains, expert_count, slot_count):
    token_count, top_count = route_ids.shape
    flat_ids = route_ids.reshape(-1)
    row_list = jnp.arange(flat_ids.shape[0], dtype=jnp.int32)
    same_expert = flat_ids[:, None] == flat_ids[None, :]
    earlier = row_list[None, :] < row_list[:, None]
    slot_rank = jnp.sum(jnp.where(same_expert & earlier, 1, 0), axis=1).astype(jnp.int32)
    slot_index = flat_ids * slot_count + slot_rank
    slot_hot = (
        slot_index[:, None] == jnp.arange(expert_count * slot_count, dtype=jnp.int32)[None, :]
    ).astype(jnp.float32)
    token_hot = (
        (row_list // top_count)[:, None] == jnp.arange(token_count, dtype=jnp.int32)[None, :]
    ).astype(jnp.float32)
    dispatch = jnp.dot(slot_hot.T, token_hot, precision=lax.Precision.HIGHEST)
    combine = jnp.dot(
        token_hot.T, slot_hot * route_gains.reshape(-1)[:, None], precision=lax.Precision.HIGHEST
    )
    return (dispatch, combine)


def expert_rows(token_rows, gate_slice, up_slice, down_slice):
    gate_out = jnp.dot(token_rows, gate_slice, preferred_element_type=jnp.float32)
    up_out = jnp.dot(token_rows, up_slice, preferred_element_type=jnp.float32)
    hidden = (jax.nn.silu(gate_out) * up_out).astype(jnp.bfloat16)
    return jnp.dot(hidden, down_slice, preferred_element_type=jnp.float32).astype(jnp.bfloat16)


def routed_experts(moe_input, expert_ids, route_gains, w_gate, w_up, w_down):
    groups, experts = lax.axis_size("grp"), lax.axis_size("ep")
    trace_count, model_width = moe_input.shape[1:]
    top_count = expert_ids.shape[3]
    slot_count = max(2, trace_count * top_count // experts)
    tables = partial(slot_tables, expert_count=experts, slot_count=slot_count)
    moe_list = []
    for step_index in range(moe_input.shape[0]):
        column_ids = expert_ids[step_index]
        column_gains = route_gains[step_index]
        dispatch_all, combine_all = jax.vmap(tables)(column_ids, column_gains)
        column_tokens = lax.all_gather(moe_input[step_index][None], "grp", axis=0, tiled=True)
        packed = jnp.einsum(
            "gsj,gjd->sgd",
            dispatch_all.astype(jnp.bfloat16),
            column_tokens,
            preferred_element_type=jnp.float32,
        )
        packed = packed.astype(jnp.bfloat16).reshape(experts, slot_count * groups, model_width)
        exchanged = lax.all_to_all(packed, "ep", split_axis=0, concat_axis=0, tiled=True)
        flat_rows = exchanged.reshape(-1, exchanged.shape[-1])
        partial_out = expert_rows(flat_rows, w_gate[0], w_up[0], w_down[0]).reshape(exchanged.shape)
        returned = lax.all_to_all(partial_out, "ep", split_axis=0, concat_axis=0, tiled=True)
        returned = returned.reshape(experts * slot_count, groups, model_width).astype(jnp.float32)
        token_terms = jnp.einsum(
            "gjs,sgd->gjd", combine_all, returned, precision=lax.Precision.HIGHEST
        )
        summed = lax.psum_scatter(
            token_terms.astype(jnp.bfloat16), "grp", scatter_dimension=0, tiled=True
        ).astype(jnp.float32)
        moe_list.append(summed[0].astype(jnp.bfloat16))
    return jnp.stack(moe_list)


def body(
    queries,
    cache,
    new_entries,
    lengths,
    moe_input,
    expert_ids,
    route_gains,
    w_gate,
    w_up,
    w_down,
    plan,
):
    queries, cache = jnp.swapaxes(queries, 2, 3), jnp.swapaxes(cache, 1, 2)
    plan, group = jnp.transpose(plan[:, 0], (1, 2, 0)), lax.axis_index("grp").reshape(1)
    every_expert = expert_ids.shape[3] == lax.axis_size("ep")
    every_expert = every_expert and (lax.axis_size("grp"), lax.axis_size("ep")) == (4, 8)
    layer = dense_layer if every_expert else routed_layer
    contexts, migrated_cache, moe_output = layer(
        queries,
        cache,
        new_entries,
        lengths,
        moe_input,
        expert_ids,
        route_gains,
        (w_gate, w_up, w_down),
        plan,
        group,
    )
    return contexts, jnp.swapaxes(migrated_cache, 1, 2), moe_output


def solution(mesh):
    return jax.shard_map(
        body,
        mesh=mesh,
        in_specs=(
            P(None, ("grp", "ep"), None, None),
            P(("grp", "ep"), None, None),
            P(None, ("grp", "ep"), None),
            P(("grp", "ep")),
            P(None, ("grp", "ep"), None),
            P(None, None, "ep", None),
            P(None, None, "ep", None),
            P("ep", None, "grp"),
            P("ep", None, "grp"),
            P("ep", "grp", None),
            P(None, "ep", None, None),
        ),
        out_specs=(
            P(None, ("grp", "ep"), None, None),
            P(("grp", "ep"), None, None),
            P(None, ("grp", "ep"), None),
        ),
        check_vma=False,
    )
```

```python
from functools import partial

import jax
import jax.numpy as jnp
from jax import lax
from jax.experimental import pallas as pl
from jax.experimental.pallas import tpu as pltpu
from jax.sharding import PartitionSpec as P

ROPE = 64


SCORE_SCALE = 192.0 ** (-0.5)


BOTH = ("grp", "ep")


GAIN_LANES = 128


PLANE_GROUPS = ((1, 2, 3), (0,))


SMALL_COST = pl.CostEstimate(flops=1, bytes_accessed=1, transcendentals=0)


LARGE_COST = pl.CostEstimate(flops=1, bytes_accessed=100_000_000, transcendentals=0)


KERNEL_PARAMS = pltpu.CompilerParams(vmem_limit_bytes=12 * 1024 * 1024)


def across(values, even_flip, odd_flip=None):
    groups, columns = lax.axis_size("grp"), lax.axis_size("ep")
    flips = (even_flip, odd_flip or even_flip)
    pairs = []
    for g in range(groups):
        for e in range(columns):
            grp_flip, ep_flip = flips[g % 2]
            pairs.append((g * columns + e, (g ^ grp_flip) * columns + (e ^ ep_flip)))
    return lax.ppermute(values, BOTH, pairs)


DONE = jax.ShapeDtypeStruct((8, 128), jnp.int32)


ANYWHERE = pl.BlockSpec(memory_space=pl.ANY)


def ignoring(kernel, first, count):
    return lambda *refs: kernel(*refs[:first], *refs[first + count :])


def gate_kernel(count, *refs):
    pass


def gate(arrays, others):
    count = len(arrays)
    return pl.pallas_call(
        partial(gate_kernel, count),
        in_specs=[ANYWHERE] * (count + len(others)),
        out_specs=[ANYWHERE] * count,
        out_shape=[jax.ShapeDtypeStruct(array.shape, array.dtype) for array in arrays],
        input_output_aliases={number: number for number in range(count)},
        compiler_params=KERNEL_PARAMS,
        cost_estimate=SMALL_COST,
        name="gate",
    )(*arrays, *others)


def choose_kernel(odd_ref, even_rows_ref, odd_rows_ref, out_ref):
    odd = odd_ref[0] == 1

    @pl.when(odd)
    def _():
        out_ref[...] = odd_rows_ref[...]

    @pl.when(jnp.logical_not(odd))
    def _():
        out_ref[...] = even_rows_ref[...]


def choose(odd, even_rows, odd_rows, others):
    vmem = pl.BlockSpec(memory_space=pltpu.VMEM)
    return pl.pallas_call(
        ignoring(choose_kernel, 0, len(others)),
        in_specs=[ANYWHERE] * len(others) + [pl.BlockSpec(memory_space=pltpu.SMEM), vmem, vmem],
        out_specs=vmem,
        out_shape=jax.ShapeDtypeStruct(even_rows.shape, even_rows.dtype),
        compiler_params=KERNEL_PARAMS,
        cost_estimate=SMALL_COST,
        name="choose",
    )(*others, odd, even_rows, odd_rows)


def add_if_odd_kernel(odd_ref, rows_ref, more_ref, out_ref):
    more = jnp.where(odd_ref[0] == 1, more_ref[...].astype(jnp.float32), 0.0)
    out_ref[...] = (rows_ref[...].astype(jnp.float32) + more).astype(out_ref.dtype)


def add_if_odd(odd, rows, more):
    vmem = pl.BlockSpec(memory_space=pltpu.VMEM)
    return pl.pallas_call(
        add_if_odd_kernel,
        in_specs=[pl.BlockSpec(memory_space=pltpu.SMEM), vmem, vmem],
        out_specs=vmem,
        out_shape=jax.ShapeDtypeStruct(rows.shape, rows.dtype),
        compiler_params=KERNEL_PARAMS,
        cost_estimate=SMALL_COST,
        name="add_if_odd",
    )(odd, rows, more)


def plan_entry(plan_ref, group, entry, field):
    return plan_ref[entry, field, group]


def stack_entries(new_entries_ref, stack_ref):
    steps, traces = new_entries_ref.shape[:2]
    stack_ref[...] = jnp.zeros_like(stack_ref)
    for step in range(steps):
        stack_ref[step * traces : (step + 1) * traces, :] = new_entries_ref[step].astype(jnp.float32)
    return stack_ref[...].astype(jnp.bfloat16)


def insert_entries(keys, entries, filled, trace, steps, traces):
    rows, capacity = entries.shape[0], keys.shape[1]
    row_index = lax.broadcasted_iota(jnp.int32, (rows, capacity), 0)
    column_index = lax.broadcasted_iota(jnp.int32, (rows, capacity), 1)
    place = ((column_index - filled) * traces + trace == row_index) & (column_index >= filled)
    spread = lax.dot_general(
        entries,
        place.astype(jnp.bfloat16),
        (((0,), (0,)), ((), ())),
        preferred_element_type=jnp.float32,
    )
    column_index = lax.broadcasted_iota(jnp.int32, keys.shape, 1)
    new = (column_index >= filled) & (column_index < filled + steps)
    return jnp.where(new, spread, keys.astype(jnp.float32)).astype(jnp.bfloat16)


def outgoing_slot(number, plan_ref, group_ref):
    group = group_ref[0]
    partner = group ^ (number + 1)
    slot = jnp.int32(0)
    for entry in range(2):
        goes = plan_entry(plan_ref, group, entry, 1) == partner
        slot = jnp.where(goes, plan_entry(plan_ref, group, entry, 0), slot)
    return slot


def gain_lanes(ids, gains):
    lane = lax.broadcasted_iota(jnp.int32, (ids.shape[0], GAIN_LANES), 1)
    dense = jnp.zeros(lane.shape, jnp.float32)
    for choice in range(ids.shape[1]):
        place = ids[:, choice : choice + 1]
        named = (lane >= 3 * place) & (lane < 3 * place + 3)
        dense = dense + jnp.where(named, gains[:, choice : choice + 1], 0.0)
    high = dense.astype(jnp.bfloat16).astype(jnp.float32)
    rest = dense - high
    middle = rest.astype(jnp.bfloat16).astype(jnp.float32)
    part = lane % 3
    parts = jnp.where(part == 0, high, jnp.where(part == 1, middle, rest - middle))
    return parts.astype(jnp.bfloat16)


def token_rows_kernel(group_ref, *refs):
    sources, rows_ref, targets, semaphores = refs[:3], refs[3], refs[4:7], refs[7]
    copies = [
        pltpu.make_async_copy(source, target, semaphores.at[number])
        for number, (source, target) in enumerate(zip(sources, targets))
    ]
    for copy in copies:
        copy.start()
    for copy in copies:
        copy.wait()
    ids_ref, gains_ref, tokens_ref = targets
    steps, _, width = tokens_ref.shape
    group = group_ref[0]
    for step in range(steps):
        rows_ref[step, :, :width] = tokens_ref[step]
        rows_ref[step, :, width:] = gain_lanes(ids_ref[step, group], gains_ref[step, group])


def token_rows(group, expert_ids, route_gains, moe_input):
    steps, traces, width = moe_input.shape
    sources = [expert_ids, route_gains, moe_input]
    return pl.pallas_call(
        token_rows_kernel,
        in_specs=[pl.BlockSpec(memory_space=pltpu.SMEM)]
        + [pl.BlockSpec(memory_space=pltpu.HBM)] * len(sources),
        out_specs=pl.BlockSpec(memory_space=pltpu.VMEM),
        out_shape=jax.ShapeDtypeStruct((steps, traces, width + GAIN_LANES), moe_input.dtype),
        scratch_shapes=[pltpu.VMEM(source.shape, source.dtype) for source in sources]
        + [pltpu.SemaphoreType.DMA((len(sources),))],
        compiler_params=KERNEL_PARAMS,
        cost_estimate=LARGE_COST,
        name="token_rows",
    )(group, *(pltpu.with_memory_space_constraint(source, pltpu.HBM) for source in sources))


def outgoing_kernel(others, lengths_ref, plan_ref, group_ref, cache_hbm, entries_hbm, *refs):
    out_refs = refs[:others]
    slots_ref, new_entries_ref, stack_ref, semaphores = refs[others:]
    slots = [outgoing_slot(number, plan_ref, group_ref) for number in range(others)]
    copies = [pltpu.make_async_copy(entries_hbm, new_entries_ref, semaphores.at[others])]
    for number, slot in enumerate(slots):
        copies.append(
            pltpu.make_async_copy(cache_hbm.at[slot], slots_ref.at[number], semaphores.at[number])
        )
    for copy in copies:
        copy.start()
    for copy in copies:
        copy.wait()
    steps, traces, _ = new_entries_ref.shape
    entries = stack_entries(new_entries_ref, stack_ref)
    for number, slot in enumerate(slots):
        out_refs[number][...] = insert_entries(
            slots_ref[number], entries, lengths_ref[slot], slot, steps, traces
        )


def outgoing(cache, new_entries, lengths, plan, group, behind=()):
    traces, width, capacity = cache.shape
    others = lax.axis_size("grp") - 1
    entry_rows = -(-new_entries.shape[0] * traces // 16) * 16
    smem, vmem = pl.BlockSpec(memory_space=pltpu.SMEM), pl.BlockSpec(memory_space=pltpu.VMEM)
    hbm = pl.BlockSpec(memory_space=pltpu.HBM)
    return pl.pallas_call(
        ignoring(partial(outgoing_kernel, others), 0, len(behind)),
        in_specs=[ANYWHERE] * len(behind) + [smem, smem, smem, hbm, hbm],
        out_specs=[vmem] * others,
        out_shape=[jax.ShapeDtypeStruct((width, capacity), cache.dtype)] * others,
        scratch_shapes=[
            pltpu.VMEM((others, width, capacity), cache.dtype),
            pltpu.VMEM(new_entries.shape, new_entries.dtype),
            pltpu.VMEM((entry_rows, width), jnp.float32),
            pltpu.SemaphoreType.DMA((others + 1,)),
        ],
        compiler_params=KERNEL_PARAMS,
        cost_estimate=LARGE_COST,
        name="outgoing",
    )(
        *behind,
        pltpu.with_memory_space_constraint(lengths, pltpu.HBM),
        pltpu.with_memory_space_constraint(plan, pltpu.HBM),
        group,
        pltpu.with_memory_space_constraint(cache, pltpu.HBM),
        pltpu.with_memory_space_constraint(new_entries, pltpu.HBM),
    )


def line_kernel(*refs):
    pieces, out_ref = refs[:-1], refs[-1]
    rows = [piece[step].astype(jnp.float32) for piece in pieces for step in range(piece.shape[0])]
    out_ref[...] = jnp.concatenate(rows, axis=0).astype(out_ref.dtype)


def line_rows(pieces, others):
    steps, traces, lanes = pieces[0].shape
    vmem = pl.BlockSpec(memory_space=pltpu.VMEM)
    return pl.pallas_call(
        ignoring(line_kernel, 0, len(others)),
        in_specs=[ANYWHERE] * len(others) + [vmem] * len(pieces),
        out_specs=vmem,
        out_shape=jax.ShapeDtypeStruct((len(pieces) * steps * traces, lanes), pieces[0].dtype),
        cost_estimate=LARGE_COST,
        compiler_params=KERNEL_PARAMS,
        name="line_rows",
    )(*others, *pieces)


def line_sums_kernel(odd_ref, *refs):
    steps, traces, _ = refs[-1].shape
    count = len(refs) - refs[0].shape[0] // (steps * traces)
    total = jnp.where(odd_ref[0] == 1, 0.0, refs[0][...].astype(jnp.float32))
    for term_ref in refs[1:count]:
        total = total + term_ref[...].astype(jnp.float32)
    for number, out_ref in enumerate(refs[count:]):
        for step in range(steps):
            first = (number * steps + step) * traces
            out_ref[step] = total[first : first + traces].astype(out_ref.dtype)


def line_sums(odd, terms, steps, traces, pieces, others):
    lanes = terms[0].shape[1]
    vmem = pl.BlockSpec(memory_space=pltpu.VMEM)
    return pl.pallas_call(
        ignoring(line_sums_kernel, 0, len(others)),
        in_specs=[ANYWHERE] * len(others)
        + [pl.BlockSpec(memory_space=pltpu.SMEM)]
        + [vmem] * len(terms),
        out_specs=[vmem] * pieces,
        out_shape=[jax.ShapeDtypeStruct((steps, traces, lanes), terms[0].dtype)] * pieces,
        compiler_params=KERNEL_PARAMS,
        cost_estimate=LARGE_COST,
        name="line_sums",
    )(*others, odd, *terms)


def attention_kernel(
    block, lengths_ref, queries_ref, cache_ref, entries_ref, contexts_ref, grown_ref, done_ref, stack_ref
):
    done_ref[...] = jnp.zeros_like(done_ref)
    grid_index = pl.program_id(0)
    step_count, _, width, heads = queries_ref.shape
    latent = contexts_ref.shape[3]
    traces = block * pl.num_programs(0)
    entries = stack_entries(entries_ref, stack_ref)
    for member in range(block):
        trace = grid_index * block + member
        filled = lengths_ref[trace]
        keys = insert_entries(
            cache_ref[member], entries, filled, trace, step_count, traces
        )
        grown_ref[member] = keys
        key_rows = jnp.transpose(keys)
        flat_queries = jnp.concatenate(
            [queries_ref[s, member] for s in range(step_count)], axis=1
        )
        scores = jnp.dot(key_rows, flat_queries, preferred_element_type=jnp.float32) * SCORE_SCALE
        position = lax.broadcasted_iota(jnp.int32, scores.shape, 0)
        step_of_column = lax.broadcasted_iota(jnp.int32, scores.shape, 1) // heads
        scores = jnp.where(position <= filled + step_of_column, scores, -jnp.inf)
        exp_scores = jnp.exp(scores - jnp.max(scores, axis=0, keepdims=True))
        weights = (exp_scores / jnp.sum(exp_scores, axis=0, keepdims=True)).astype(jnp.bfloat16)
        context = lax.dot_general(
            weights,
            key_rows[:, :latent],
            (((0,), (0,)), ((), ())),
            preferred_element_type=jnp.float32,
        )
        contexts_ref[:, member] = context.astype(jnp.bfloat16).reshape(step_count, heads, latent)


def place_kernel(plan_ref, group_ref, *refs):
    received_refs, (_, migrated_ref, semaphores) = refs[:-3], refs[-3:]
    group = group_ref[0]
    copies = []
    for number, received_ref in enumerate(received_refs):
        partner = group ^ (number + 1)
        lands, slot = jnp.bool_(False), jnp.int32(0)
        for entry in range(2):
            here = plan_entry(plan_ref, partner, entry, 1) == group
            lands = lands | here
            slot = jnp.where(here, plan_entry(plan_ref, group, entry, 0), slot)
        copies.append(
            (
                lands,
                pltpu.make_async_copy(received_ref, migrated_ref.at[slot], semaphores.at[number]),
            )
        )
    for lands, copy in copies:
        pl.when(lands)(copy.start)
    for lands, copy in copies:
        pl.when(lands)(copy.wait)


def place(grown, received, plan, group):
    smem = pl.BlockSpec(memory_space=pltpu.SMEM)
    return pl.pallas_call(
        place_kernel,
        in_specs=[smem, smem] + [ANYWHERE] * (len(received) + 1),
        out_specs=ANYWHERE,
        out_shape=jax.ShapeDtypeStruct(grown.shape, grown.dtype),
        input_output_aliases={len(received) + 2: 0},
        scratch_shapes=[pltpu.SemaphoreType.DMA((len(received),))],
        compiler_params=KERNEL_PARAMS,
        cost_estimate=LARGE_COST,
        name="place",
    )(plan, group, *received, grown)


def fetch_kernel(*refs):
    refs, done_ref, refs_semaphores = refs[:-2], refs[-2], refs[-1]
    done_ref[...] = jnp.zeros_like(done_ref)
    refs = (*refs, refs_semaphores)
    count = (len(refs) - 1) // 2
    copies = [
        pltpu.make_async_copy(source.at[0], target, refs[-1].at[number])
        for number, (source, target) in enumerate(zip(refs[:count], refs[count:-1]))
    ]
    for copy in copies:
        copy.start()
    for copy in copies:
        copy.wait()


def fetch(weights, others):
    weights = [pltpu.with_memory_space_constraint(weight, pltpu.HBM) for weight in weights]
    return pl.pallas_call(
        ignoring(fetch_kernel, 0, len(others)),
        in_specs=[ANYWHERE] * len(others)
        + [pl.BlockSpec(memory_space=pltpu.HBM)] * len(weights),
        out_specs=[pl.BlockSpec(memory_space=pltpu.VMEM)] * (len(weights) + 1),
        out_shape=[pltpu.VMEM(weight.shape[1:], weight.dtype) for weight in weights] + [DONE],
        scratch_shapes=[pltpu.SemaphoreType.DMA((len(weights),))],
        cost_estimate=LARGE_COST,
        compiler_params=KERNEL_PARAMS,
        name="fetch",
    )(*others, *weights)


def attention(queries, cache, new_entries, lengths, others=(), block=2):
    step_count, traces, width, heads = queries.shape
    capacity = cache.shape[2]
    latent = width - ROPE
    entry_rows = -(-step_count * traces // 16) * 16
    whole = lambda shape: pl.BlockSpec(shape, lambda t, *_: (0,) * len(shape))
    return pl.pallas_call(
        ignoring(partial(attention_kernel, block), 1, len(others)),
        grid_spec=pltpu.PrefetchScalarGridSpec(
            num_scalar_prefetch=1,
            grid=(traces // block,),
            in_specs=[ANYWHERE] * len(others)
            + [
                pl.BlockSpec((step_count, block, width, heads), lambda t, *_: (0, t, 0, 0)),
                pl.BlockSpec((block, width, capacity), lambda t, *_: (t, 0, 0)),
                whole(new_entries.shape),
            ],
            out_specs=[
                pl.BlockSpec((step_count, block, heads, latent), lambda t, *_: (0, t, 0, 0)),
                pl.BlockSpec((block, width, capacity), lambda t, *_: (t, 0, 0)),
                whole(DONE.shape),
            ],
            scratch_shapes=[pltpu.VMEM((entry_rows, width), jnp.float32)],
        ),
        out_shape=[
            jax.ShapeDtypeStruct((step_count, traces, heads, latent), jnp.bfloat16),
            jax.ShapeDtypeStruct(cache.shape, jnp.bfloat16),
            DONE,
        ],
        cost_estimate=LARGE_COST,
        compiler_params=KERNEL_PARAMS,
        name="attention",
    )(
        lengths,
        *others,
        pltpu.with_memory_space_constraint(queries, pltpu.HBM),
        pltpu.with_memory_space_constraint(cache, pltpu.HBM),
        new_entries,
    )


def expert_kernel(column_ref, *refs):
    count = (len(refs) - 4) // 2
    pieces, (gate_ref, up_ref, down_ref) = refs[:count], refs[count : count + 3]
    out_refs, hidden_ref = refs[count + 3 : -1], refs[-1]
    width, hidden_width = gate_ref.shape
    rows = pieces[0].shape[0]
    gain_parts = jnp.concatenate([piece[:, width:] for piece in pieces], axis=0).astype(jnp.float32)
    lane = lax.broadcasted_iota(jnp.int32, gain_parts.shape, 1)
    first_lane = column_ref[0] * 3
    gain = jnp.sum(
        jnp.where((lane >= first_lane) & (lane < first_lane + 3), gain_parts, 0.0),
        axis=1,
        keepdims=True,
    )
    tokens = jnp.concatenate([piece[:, :width] for piece in pieces], axis=0)
    gate_out = jnp.dot(tokens, gate_ref[...], preferred_element_type=jnp.float32)
    up_out = jnp.dot(tokens, up_ref[...], preferred_element_type=jnp.float32)
    hidden = gate_out / (1.0 + jnp.exp(-gate_out)) * up_out * gain
    hidden_ref[...] = hidden.astype(jnp.bfloat16)
    tile = 512 if width % 512 == 0 else width
    for first in range(0, width, tile):
        columns = slice(first, first + tile)
        products = jnp.dot(
            hidden_ref[...], down_ref[:, columns], preferred_element_type=jnp.float32
        ).astype(jnp.bfloat16)
        for number, out_ref in enumerate(out_refs):
            out_ref[:, columns] = products[number * rows : (number + 1) * rows]


def expert(pieces, weights, others=()):
    width, hidden_width = weights[0].shape
    rows = pieces[0].shape[0]
    vmem = pl.BlockSpec(memory_space=pltpu.VMEM)
    column = lax.axis_index("ep").astype(jnp.int32).reshape(1)
    return pl.pallas_call(
        ignoring(expert_kernel, 0, len(others)),
        in_specs=[ANYWHERE] * len(others)
        + [pl.BlockSpec(memory_space=pltpu.SMEM)]
        + [vmem] * (len(pieces) + 3),
        out_specs=[vmem] * len(pieces),
        out_shape=[jax.ShapeDtypeStruct((rows, width), jnp.bfloat16)] * len(pieces),
        scratch_shapes=[pltpu.VMEM((len(pieces) * rows, hidden_width), jnp.bfloat16)],
        cost_estimate=LARGE_COST,
        compiler_params=pltpu.CompilerParams(vmem_limit_bytes=28 * 1024 * 1024),
        name="expert",
    )(*others, column, *pieces, *weights)


def add_up(terms):
    total = terms[0].astype(jnp.float32)
    for term in terms[1:]:
        total = total + term.astype(jnp.float32)
    return total.astype(jnp.bfloat16)


def dense_layer(
    queries, cache, new_entries, lengths, moe_input, expert_ids, route_gains, weights, plan, group
):
    groups = lax.axis_size("grp")
    steps, trace_count, _ = moe_input.shape
    core, neighbour, skip, opposite = (1, 0), (0, 2), (0, 4), (0, 6)
    beside, above, diagonal = (0, 1), (2, 0), (2, 1)
    first_flips = [(opposite, beside), (skip, above), (neighbour, diagonal)]
    odd = (lax.axis_index("grp") % 2).reshape(1)
    rows = token_rows(group, expert_ids, route_gains, moe_input)
    line = [rows] + [across(rows, *flips) for flips in first_flips]
    own = line_rows(line, [])

    pieces = [
        across(own, *flips)
        for flips in ((beside, skip), (above, neighbour), (diagonal, opposite))
    ]
    *weights, _ = fetch(weights, [own])
    (own_sums,) = expert([own], weights)
    pieces = gate(pieces, [own_sums])
    other_pieces = [across(piece, core) for piece in [*pieces, own]]
    mine = expert(pieces, weights)
    *theirs, other_sums = expert(other_pieces, weights, mine[:1])
    sums_3 = add_up([mine[2], across(theirs[2], core)])

    term_3 = across(sums_3, diagonal, neighbour)
    contexts, grown, attended = attention(queries, cache, new_entries, lengths, [sums_3])
    theirs_1, theirs_2 = gate([across(part, core) for part in theirs[:2]], [attended])
    sums_1, sums_2 = add_up([mine[0], theirs_1]), add_up([mine[1], theirs_2])
    (sums_2,) = gate([sums_2], [term_3, attended])
    term_2 = across(sums_2, above, neighbour)
    term_1 = across(add_if_odd(odd, sums_1, term_3), beside, skip)
    leaving = outgoing(cache, new_entries, lengths, plan, group, [sums_2])
    received = [across(leaving[flip - 1], (flip, 0)) for flip in range(1, groups)]
    own_term = add_up([own_sums, across(other_sums, core)])
    parts = line_sums(
        odd, [term_3, term_1, term_2, own_term], steps, trace_count, len(line), leaving[:1]
    )
    moe_output = add_up(
        [parts[0]] + [across(part, *flips) for part, flips in zip(parts[1:], first_flips)]
    )
    return contexts, place(grown, received, plan, group), moe_output


def routed_layer(
    queries, cache, new_entries, lengths, moe_input, expert_ids, route_gains, weights, plan, group
):
    leaving = outgoing(cache, new_entries, lengths, plan, group)
    received = [across(leaving[flip - 1], (flip, 0)) for flip in range(1, lax.axis_size("grp"))]
    contexts, grown, _ = attention(queries, cache, new_entries, lengths)
    migrated_cache = place(grown, received, plan, group)
    moe_output = routed_experts(moe_input, expert_ids, route_gains, *weights)
    return contexts, migrated_cache, moe_output


def slot_tables(route_ids, route_gains, expert_count, slot_count):
    token_count, top_count = route_ids.shape
    flat_ids = route_ids.reshape(-1)
    row_list = jnp.arange(flat_ids.shape[0], dtype=jnp.int32)
    same_expert = flat_ids[:, None] == flat_ids[None, :]
    earlier = row_list[None, :] < row_list[:, None]
    slot_rank = jnp.sum(jnp.where(same_expert & earlier, 1, 0), axis=1).astype(jnp.int32)
    slot_index = flat_ids * slot_count + slot_rank
    slot_hot = (
        slot_index[:, None] == jnp.arange(expert_count * slot_count, dtype=jnp.int32)[None, :]
    ).astype(jnp.float32)
    token_hot = (
        (row_list // top_count)[:, None] == jnp.arange(token_count, dtype=jnp.int32)[None, :]
    ).astype(jnp.float32)
    dispatch = jnp.dot(slot_hot.T, token_hot, precision=lax.Precision.HIGHEST)
    combine = jnp.dot(
        token_hot.T, slot_hot * route_gains.reshape(-1)[:, None], precision=lax.Precision.HIGHEST
    )
    return (dispatch, combine)


def expert_rows(token_rows, gate_slice, up_slice, down_slice):
    gate_out = jnp.dot(token_rows, gate_slice, preferred_element_type=jnp.float32)
    up_out = jnp.dot(token_rows, up_slice, preferred_element_type=jnp.float32)
    hidden = (jax.nn.silu(gate_out) * up_out).astype(jnp.bfloat16)
    return jnp.dot(hidden, down_slice, preferred_element_type=jnp.float32).astype(jnp.bfloat16)


def routed_experts(moe_input, expert_ids, route_gains, w_gate, w_up, w_down):
    groups, experts = lax.axis_size("grp"), lax.axis_size("ep")
    trace_count, model_width = moe_input.shape[1:]
    top_count = expert_ids.shape[3]
    slot_count = max(2, trace_count * top_count // experts)
    tables = partial(slot_tables, expert_count=experts, slot_count=slot_count)
    moe_list = []
    for step_index in range(moe_input.shape[0]):
        column_ids = expert_ids[step_index]
        column_gains = route_gains[step_index]
        dispatch_all, combine_all = jax.vmap(tables)(column_ids, column_gains)
        column_tokens = lax.all_gather(moe_input[step_index][None], "grp", axis=0, tiled=True)
        packed = jnp.einsum(
            "gsj,gjd->sgd",
            dispatch_all.astype(jnp.bfloat16),
            column_tokens,
            preferred_element_type=jnp.float32,
        )
        packed = packed.astype(jnp.bfloat16).reshape(experts, slot_count * groups, model_width)
        exchanged = lax.all_to_all(packed, "ep", split_axis=0, concat_axis=0, tiled=True)
        flat_rows = exchanged.reshape(-1, exchanged.shape[-1])
        partial_out = expert_rows(flat_rows, w_gate[0], w_up[0], w_down[0]).reshape(exchanged.shape)
        returned = lax.all_to_all(partial_out, "ep", split_axis=0, concat_axis=0, tiled=True)
        returned = returned.reshape(experts * slot_count, groups, model_width).astype(jnp.float32)
        token_terms = jnp.einsum(
            "gjs,sgd->gjd", combine_all, returned, precision=lax.Precision.HIGHEST
        )
        summed = lax.psum_scatter(
            token_terms.astype(jnp.bfloat16), "grp", scatter_dimension=0, tiled=True
        ).astype(jnp.float32)
        moe_list.append(summed[0].astype(jnp.bfloat16))
    return jnp.stack(moe_list)


def body(
    queries,
    cache,
    new_entries,
    lengths,
    moe_input,
    expert_ids,
    route_gains,
    w_gate,
    w_up,
    w_down,
    plan,
):
    queries, cache = jnp.swapaxes(queries, 2, 3), jnp.swapaxes(cache, 1, 2)
    plan, group = jnp.transpose(plan[:, 0], (1, 2, 0)), lax.axis_index("grp").reshape(1)
    every_expert = expert_ids.shape[3] == lax.axis_size("ep")
    every_expert = every_expert and (lax.axis_size("grp"), lax.axis_size("ep")) == (4, 8)
    layer = dense_layer if every_expert else routed_layer
    contexts, migrated_cache, moe_output = layer(
        queries,
        cache,
        new_entries,
        lengths,
        moe_input,
        expert_ids,
        route_gains,
        (w_gate, w_up, w_down),
        plan,
        group,
    )
    return contexts, jnp.swapaxes(migrated_cache, 1, 2), moe_output


def solution(mesh):
    return jax.shard_map(
        body,
        mesh=mesh,
        in_specs=(
            P(None, ("grp", "ep"), None, None),
            P(("grp", "ep"), None, None),
            P(None, ("grp", "ep"), None),
            P(("grp", "ep")),
            P(None, ("grp", "ep"), None),
            P(None, None, "ep", None),
            P(None, None, "ep", None),
            P("ep", None, "grp"),
            P("ep", None, "grp"),
            P("ep", "grp", None),
            P(None, "ep", None, None),
        ),
        out_specs=(
            P(None, ("grp", "ep"), None, None),
            P(("grp", "ep"), None, None),
            P(None, ("grp", "ep"), None),
        ),
        check_vma=False,
    )
```

```python
from functools import partial

import jax
import jax.numpy as jnp
from jax import lax
from jax.experimental import pallas as pl
from jax.experimental.pallas import tpu as pltpu
from jax.sharding import PartitionSpec as P

ROPE = 64


SCORE_SCALE = 192.0 ** (-0.5)


BOTH = ("grp", "ep")


GAIN_LANES = 128


PLANE_GROUPS = ((1, 2, 3), (0,))


SMALL_COST = pl.CostEstimate(flops=1, bytes_accessed=1, transcendentals=0)


LARGE_COST = pl.CostEstimate(flops=1, bytes_accessed=100_000_000, transcendentals=0)


KERNEL_PARAMS = pltpu.CompilerParams(vmem_limit_bytes=12 * 1024 * 1024)


def across(values, even_flip, odd_flip=None):
    groups, columns = lax.axis_size("grp"), lax.axis_size("ep")
    flips = (even_flip, odd_flip or even_flip)
    pairs = []
    for g in range(groups):
        for e in range(columns):
            grp_flip, ep_flip = flips[g % 2]
            pairs.append((g * columns + e, (g ^ grp_flip) * columns + (e ^ ep_flip)))
    return lax.ppermute(values, BOTH, pairs)


DONE = jax.ShapeDtypeStruct((8, 128), jnp.int32)


ANYWHERE = pl.BlockSpec(memory_space=pl.ANY)


def ignoring(kernel, first, count):
    return lambda *refs: kernel(*refs[:first], *refs[first + count :])


def gate_kernel(count, *refs):
    pass


def gate(arrays, others):
    count = len(arrays)
    return pl.pallas_call(
        partial(gate_kernel, count),
        in_specs=[ANYWHERE] * (count + len(others)),
        out_specs=[ANYWHERE] * count,
        out_shape=[jax.ShapeDtypeStruct(array.shape, array.dtype) for array in arrays],
        input_output_aliases={number: number for number in range(count)},
        compiler_params=KERNEL_PARAMS,
        cost_estimate=SMALL_COST,
        name="gate",
    )(*arrays, *others)


def choose_kernel(odd_ref, even_rows_ref, odd_rows_ref, out_ref):
    odd = odd_ref[0] == 1

    @pl.when(odd)
    def _():
        out_ref[...] = odd_rows_ref[...]

    @pl.when(jnp.logical_not(odd))
    def _():
        out_ref[...] = even_rows_ref[...]


def choose(odd, even_rows, odd_rows, others):
    vmem = pl.BlockSpec(memory_space=pltpu.VMEM)
    return pl.pallas_call(
        ignoring(choose_kernel, 0, len(others)),
        in_specs=[ANYWHERE] * len(others) + [pl.BlockSpec(memory_space=pltpu.SMEM), vmem, vmem],
        out_specs=vmem,
        out_shape=jax.ShapeDtypeStruct(even_rows.shape, even_rows.dtype),
        compiler_params=KERNEL_PARAMS,
        cost_estimate=SMALL_COST,
        name="choose",
    )(*others, odd, even_rows, odd_rows)


def add_if_odd_kernel(odd_ref, rows_ref, more_ref, out_ref):
    more = jnp.where(odd_ref[0] == 1, more_ref[...].astype(jnp.float32), 0.0)
    out_ref[...] = (rows_ref[...].astype(jnp.float32) + more).astype(out_ref.dtype)


def add_if_odd(odd, rows, more):
    vmem = pl.BlockSpec(memory_space=pltpu.VMEM)
    return pl.pallas_call(
        add_if_odd_kernel,
        in_specs=[pl.BlockSpec(memory_space=pltpu.SMEM), vmem, vmem],
        out_specs=vmem,
        out_shape=jax.ShapeDtypeStruct(rows.shape, rows.dtype),
        compiler_params=KERNEL_PARAMS,
        cost_estimate=SMALL_COST,
        name="add_if_odd",
    )(odd, rows, more)


def plan_entry(plan_ref, group, entry, field):
    return plan_ref[entry, field, group]


def stack_entries(new_entries_ref, stack_ref):
    steps, traces = new_entries_ref.shape[:2]
    stack_ref[...] = jnp.zeros_like(stack_ref)
    for step in range(steps):
        stack_ref[step * traces : (step + 1) * traces, :] = new_entries_ref[step].astype(jnp.float32)
    return stack_ref[...].astype(jnp.bfloat16)


def insert_entries(keys, entries, filled, trace, steps, traces):
    rows, capacity = entries.shape[0], keys.shape[1]
    row_index = lax.broadcasted_iota(jnp.int32, (rows, capacity), 0)
    column_index = lax.broadcasted_iota(jnp.int32, (rows, capacity), 1)
    place = ((column_index - filled) * traces + trace == row_index) & (column_index >= filled)
    spread = lax.dot_general(
        entries,
        place.astype(jnp.bfloat16),
        (((0,), (0,)), ((), ())),
        preferred_element_type=jnp.float32,
    )
    column_index = lax.broadcasted_iota(jnp.int32, keys.shape, 1)
    new = (column_index >= filled) & (column_index < filled + steps)
    return jnp.where(new, spread, keys.astype(jnp.float32)).astype(jnp.bfloat16)


def outgoing_slot(number, plan_ref, group_ref):
    group = group_ref[0]
    partner = group ^ (number + 1)
    slot = jnp.int32(0)
    for entry in range(2):
        goes = plan_entry(plan_ref, group, entry, 1) == partner
        slot = jnp.where(goes, plan_entry(plan_ref, group, entry, 0), slot)
    return slot


def gain_lanes(ids, gains):
    lane = lax.broadcasted_iota(jnp.int32, (ids.shape[0], GAIN_LANES), 1)
    dense = jnp.zeros(lane.shape, jnp.float32)
    for choice in range(ids.shape[1]):
        place = ids[:, choice : choice + 1]
        named = (lane >= 3 * place) & (lane < 3 * place + 3)
        dense = dense + jnp.where(named, gains[:, choice : choice + 1], 0.0)
    high = dense.astype(jnp.bfloat16).astype(jnp.float32)
    rest = dense - high
    middle = rest.astype(jnp.bfloat16).astype(jnp.float32)
    part = lane % 3
    parts = jnp.where(part == 0, high, jnp.where(part == 1, middle, rest - middle))
    return parts.astype(jnp.bfloat16)


def token_rows_kernel(group_ref, *refs):
    sources, rows_ref, targets, semaphores = refs[:3], refs[3], refs[4:7], refs[7]
    copies = [
        pltpu.make_async_copy(source, target, semaphores.at[number])
        for number, (source, target) in enumerate(zip(sources, targets))
    ]
    for copy in copies:
        copy.start()
    for copy in copies:
        copy.wait()
    ids_ref, gains_ref, tokens_ref = targets
    steps, _, width = tokens_ref.shape
    group = group_ref[0]
    for step in range(steps):
        rows_ref[step, :, :width] = tokens_ref[step]
        rows_ref[step, :, width:] = gain_lanes(ids_ref[step, group], gains_ref[step, group])


def token_rows(group, expert_ids, route_gains, moe_input):
    steps, traces, width = moe_input.shape
    sources = [expert_ids, route_gains, moe_input]
    return pl.pallas_call(
        token_rows_kernel,
        in_specs=[pl.BlockSpec(memory_space=pltpu.SMEM)]
        + [pl.BlockSpec(memory_space=pltpu.HBM)] * len(sources),
        out_specs=pl.BlockSpec(memory_space=pltpu.VMEM),
        out_shape=jax.ShapeDtypeStruct((steps, traces, width + GAIN_LANES), moe_input.dtype),
        scratch_shapes=[pltpu.VMEM(source.shape, source.dtype) for source in sources]
        + [pltpu.SemaphoreType.DMA((len(sources),))],
        compiler_params=KERNEL_PARAMS,
        cost_estimate=LARGE_COST,
        name="token_rows",
    )(group, *(pltpu.with_memory_space_constraint(source, pltpu.HBM) for source in sources))


def outgoing_kernel(others, lengths_ref, plan_ref, group_ref, cache_hbm, entries_hbm, *refs):
    out_refs = refs[:others]
    slots_ref, new_entries_ref, stack_ref, semaphores = refs[others:]
    slots = [outgoing_slot(number, plan_ref, group_ref) for number in range(others)]
    copies = [pltpu.make_async_copy(entries_hbm, new_entries_ref, semaphores.at[others])]
    for number, slot in enumerate(slots):
        copies.append(
            pltpu.make_async_copy(cache_hbm.at[slot], slots_ref.at[number], semaphores.at[number])
        )
    for copy in copies:
        copy.start()
    for copy in copies:
        copy.wait()
    steps, traces, _ = new_entries_ref.shape
    entries = stack_entries(new_entries_ref, stack_ref)
    for number, slot in enumerate(slots):
        out_refs[number][...] = insert_entries(
            slots_ref[number], entries, lengths_ref[slot], slot, steps, traces
        )


def outgoing(cache, new_entries, lengths, plan, group, behind=()):
    traces, width, capacity = cache.shape
    others = lax.axis_size("grp") - 1
    entry_rows = -(-new_entries.shape[0] * traces // 16) * 16
    smem, vmem = pl.BlockSpec(memory_space=pltpu.SMEM), pl.BlockSpec(memory_space=pltpu.VMEM)
    hbm = pl.BlockSpec(memory_space=pltpu.HBM)
    return pl.pallas_call(
        ignoring(partial(outgoing_kernel, others), 0, len(behind)),
        in_specs=[ANYWHERE] * len(behind) + [smem, smem, smem, hbm, hbm],
        out_specs=[vmem] * others,
        out_shape=[jax.ShapeDtypeStruct((width, capacity), cache.dtype)] * others,
        scratch_shapes=[
            pltpu.VMEM((others, width, capacity), cache.dtype),
            pltpu.VMEM(new_entries.shape, new_entries.dtype),
            pltpu.VMEM((entry_rows, width), jnp.float32),
            pltpu.SemaphoreType.DMA((others + 1,)),
        ],
        compiler_params=KERNEL_PARAMS,
        cost_estimate=LARGE_COST,
        name="outgoing",
    )(
        *behind,
        pltpu.with_memory_space_constraint(lengths, pltpu.HBM),
        pltpu.with_memory_space_constraint(plan, pltpu.HBM),
        group,
        pltpu.with_memory_space_constraint(cache, pltpu.HBM),
        pltpu.with_memory_space_constraint(new_entries, pltpu.HBM),
    )


def line_kernel(*refs):
    pieces, out_ref = refs[:-1], refs[-1]
    rows = [piece[step].astype(jnp.float32) for piece in pieces for step in range(piece.shape[0])]
    out_ref[...] = jnp.concatenate(rows, axis=0).astype(out_ref.dtype)


def line_rows(pieces, others):
    steps, traces, lanes = pieces[0].shape
    vmem = pl.BlockSpec(memory_space=pltpu.VMEM)
    return pl.pallas_call(
        ignoring(line_kernel, 0, len(others)),
        in_specs=[ANYWHERE] * len(others) + [vmem] * len(pieces),
        out_specs=vmem,
        out_shape=jax.ShapeDtypeStruct((len(pieces) * steps * traces, lanes), pieces[0].dtype),
        cost_estimate=LARGE_COST,
        compiler_params=KERNEL_PARAMS,
        name="line_rows",
    )(*others, *pieces)


def line_sums_kernel(odd_ref, *refs):
    steps, traces, _ = refs[-1].shape
    count = len(refs) - refs[0].shape[0] // (steps * traces)
    total = jnp.where(odd_ref[0] == 1, 0.0, refs[0][...].astype(jnp.float32))
    for term_ref in refs[1:count]:
        total = total + term_ref[...].astype(jnp.float32)
    for number, out_ref in enumerate(refs[count:]):
        for step in range(steps):
            first = (number * steps + step) * traces
            out_ref[step] = total[first : first + traces].astype(out_ref.dtype)


def line_sums(odd, terms, steps, traces, pieces, others):
    lanes = terms[0].shape[1]
    vmem = pl.BlockSpec(memory_space=pltpu.VMEM)
    return pl.pallas_call(
        ignoring(line_sums_kernel, 0, len(others)),
        in_specs=[ANYWHERE] * len(others)
        + [pl.BlockSpec(memory_space=pltpu.SMEM)]
        + [vmem] * len(terms),
        out_specs=[vmem] * pieces,
        out_shape=[jax.ShapeDtypeStruct((steps, traces, lanes), terms[0].dtype)] * pieces,
        compiler_params=KERNEL_PARAMS,
        cost_estimate=LARGE_COST,
        name="line_sums",
    )(*others, odd, *terms)


def attention_kernel(
    block, lengths_ref, queries_ref, cache_ref, entries_ref, contexts_ref, grown_ref, done_ref, stack_ref
):
    done_ref[...] = jnp.zeros_like(done_ref)
    grid_index = pl.program_id(0)
    step_count, _, width, heads = queries_ref.shape
    latent = contexts_ref.shape[3]
    traces = block * pl.num_programs(0)
    entries = stack_entries(entries_ref, stack_ref)
    for member in range(block):
        trace = grid_index * block + member
        filled = lengths_ref[trace]
        keys = insert_entries(
            cache_ref[member], entries, filled, trace, step_count, traces
        )
        grown_ref[member] = keys
        key_rows = jnp.transpose(keys)
        flat_queries = jnp.concatenate(
            [queries_ref[s, member] for s in range(step_count)], axis=1
        )
        scores = jnp.dot(key_rows, flat_queries, preferred_element_type=jnp.float32) * SCORE_SCALE
        position = lax.broadcasted_iota(jnp.int32, scores.shape, 0)
        step_of_column = lax.broadcasted_iota(jnp.int32, scores.shape, 1) // heads
        scores = jnp.where(position <= filled + step_of_column, scores, -jnp.inf)
        exp_scores = jnp.exp(scores - jnp.max(scores, axis=0, keepdims=True))
        weights = (exp_scores / jnp.sum(exp_scores, axis=0, keepdims=True)).astype(jnp.bfloat16)
        context = lax.dot_general(
            weights,
            key_rows[:, :latent],
            (((0,), (0,)), ((), ())),
            preferred_element_type=jnp.float32,
        )
        contexts_ref[:, member] = context.astype(jnp.bfloat16).reshape(step_count, heads, latent)


def place_kernel(plan_ref, group_ref, *refs):
    received_refs, (_, migrated_ref, semaphores) = refs[:-3], refs[-3:]
    group = group_ref[0]
    copies = []
    for number, received_ref in enumerate(received_refs):
        partner = group ^ (number + 1)
        lands, slot = jnp.bool_(False), jnp.int32(0)
        for entry in range(2):
            here = plan_entry(plan_ref, partner, entry, 1) == group
            lands = lands | here
            slot = jnp.where(here, plan_entry(plan_ref, group, entry, 0), slot)
        copies.append(
            (
                lands,
                pltpu.make_async_copy(received_ref, migrated_ref.at[slot], semaphores.at[number]),
            )
        )
    for lands, copy in copies:
        pl.when(lands)(copy.start)
    for lands, copy in copies:
        pl.when(lands)(copy.wait)


def place(grown, received, plan, group):
    smem = pl.BlockSpec(memory_space=pltpu.SMEM)
    return pl.pallas_call(
        place_kernel,
        in_specs=[smem, smem] + [ANYWHERE] * (len(received) + 1),
        out_specs=ANYWHERE,
        out_shape=jax.ShapeDtypeStruct(grown.shape, grown.dtype),
        input_output_aliases={len(received) + 2: 0},
        scratch_shapes=[pltpu.SemaphoreType.DMA((len(received),))],
        compiler_params=KERNEL_PARAMS,
        cost_estimate=LARGE_COST,
        name="place",
    )(plan, group, *received, grown)


def fetch_kernel(*refs):
    refs, done_ref, refs_semaphores = refs[:-2], refs[-2], refs[-1]
    done_ref[...] = jnp.zeros_like(done_ref)
    refs = (*refs, refs_semaphores)
    count = (len(refs) - 1) // 2
    copies = [
        pltpu.make_async_copy(source.at[0], target, refs[-1].at[number])
        for number, (source, target) in enumerate(zip(refs[:count], refs[count:-1]))
    ]
    for copy in copies:
        copy.start()
    for copy in copies:
        copy.wait()


def fetch(weights, others):
    weights = [pltpu.with_memory_space_constraint(weight, pltpu.HBM) for weight in weights]
    return pl.pallas_call(
        ignoring(fetch_kernel, 0, len(others)),
        in_specs=[ANYWHERE] * len(others)
        + [pl.BlockSpec(memory_space=pltpu.HBM)] * len(weights),
        out_specs=[pl.BlockSpec(memory_space=pltpu.VMEM)] * (len(weights) + 1),
        out_shape=[pltpu.VMEM(weight.shape[1:], weight.dtype) for weight in weights] + [DONE],
        scratch_shapes=[pltpu.SemaphoreType.DMA((len(weights),))],
        cost_estimate=LARGE_COST,
        compiler_params=KERNEL_PARAMS,
        name="fetch",
    )(*others, *weights)


def attention(queries, cache, new_entries, lengths, others=(), block=2):
    step_count, traces, width, heads = queries.shape
    capacity = cache.shape[2]
    latent = width - ROPE
    entry_rows = -(-step_count * traces // 16) * 16
    whole = lambda shape: pl.BlockSpec(shape, lambda t, *_: (0,) * len(shape))
    return pl.pallas_call(
        ignoring(partial(attention_kernel, block), 1, len(others)),
        grid_spec=pltpu.PrefetchScalarGridSpec(
            num_scalar_prefetch=1,
            grid=(traces // block,),
            in_specs=[ANYWHERE] * len(others)
            + [
                pl.BlockSpec((step_count, block, width, heads), lambda t, *_: (0, t, 0, 0)),
                pl.BlockSpec((block, width, capacity), lambda t, *_: (t, 0, 0)),
                whole(new_entries.shape),
            ],
            out_specs=[
                pl.BlockSpec((step_count, block, heads, latent), lambda t, *_: (0, t, 0, 0)),
                pl.BlockSpec((block, width, capacity), lambda t, *_: (t, 0, 0)),
                whole(DONE.shape),
            ],
            scratch_shapes=[pltpu.VMEM((entry_rows, width), jnp.float32)],
        ),
        out_shape=[
            jax.ShapeDtypeStruct((step_count, traces, heads, latent), jnp.bfloat16),
            jax.ShapeDtypeStruct(cache.shape, jnp.bfloat16),
            DONE,
        ],
        cost_estimate=LARGE_COST,
        compiler_params=KERNEL_PARAMS,
        name="attention",
    )(
        lengths,
        *others,
        pltpu.with_memory_space_constraint(queries, pltpu.HBM),
        pltpu.with_memory_space_constraint(cache, pltpu.HBM),
        new_entries,
    )


def expert_kernel(column_ref, *refs):
    count = (len(refs) - 4) // 2
    pieces, (gate_ref, up_ref, down_ref) = refs[:count], refs[count : count + 3]
    out_refs, hidden_ref = refs[count + 3 : -1], refs[-1]
    width, hidden_width = gate_ref.shape
    rows = pieces[0].shape[0]
    gain_parts = jnp.concatenate([piece[:, width:] for piece in pieces], axis=0).astype(jnp.float32)
    lane = lax.broadcasted_iota(jnp.int32, gain_parts.shape, 1)
    first_lane = column_ref[0] * 3
    gain = jnp.sum(
        jnp.where((lane >= first_lane) & (lane < first_lane + 3), gain_parts, 0.0),
        axis=1,
        keepdims=True,
    )
    tokens = jnp.concatenate([piece[:, :width] for piece in pieces], axis=0)
    gate_out = jnp.dot(tokens, gate_ref[...], preferred_element_type=jnp.float32)
    up_out = jnp.dot(tokens, up_ref[...], preferred_element_type=jnp.float32)
    hidden = gate_out / (1.0 + jnp.exp(-gate_out)) * up_out * gain
    hidden_ref[...] = hidden.astype(jnp.bfloat16)
    tile = 512 if width % 512 == 0 else width
    for first in range(0, width, tile):
        columns = slice(first, first + tile)
        products = jnp.dot(
            hidden_ref[...], down_ref[:, columns], preferred_element_type=jnp.float32
        ).astype(jnp.bfloat16)
        for number, out_ref in enumerate(out_refs):
            out_ref[:, columns] = products[number * rows : (number + 1) * rows]


def expert(pieces, weights, others=()):
    width, hidden_width = weights[0].shape
    rows = pieces[0].shape[0]
    vmem = pl.BlockSpec(memory_space=pltpu.VMEM)
    column = lax.axis_index("ep").astype(jnp.int32).reshape(1)
    return pl.pallas_call(
        ignoring(expert_kernel, 0, len(others)),
        in_specs=[ANYWHERE] * len(others)
        + [pl.BlockSpec(memory_space=pltpu.SMEM)]
        + [vmem] * (len(pieces) + 3),
        out_specs=[vmem] * len(pieces),
        out_shape=[jax.ShapeDtypeStruct((rows, width), jnp.bfloat16)] * len(pieces),
        scratch_shapes=[pltpu.VMEM((len(pieces) * rows, hidden_width), jnp.bfloat16)],
        cost_estimate=LARGE_COST,
        compiler_params=pltpu.CompilerParams(vmem_limit_bytes=28 * 1024 * 1024),
        name="expert",
    )(*others, column, *pieces, *weights)


def add_up(terms):
    total = terms[0].astype(jnp.float32)
    for term in terms[1:]:
        total = total + term.astype(jnp.float32)
    return total.astype(jnp.bfloat16)


def dense_layer(
    queries, cache, new_entries, lengths, moe_input, expert_ids, route_gains, weights, plan, group
):
    groups = lax.axis_size("grp")
    steps, trace_count, _ = moe_input.shape
    core, neighbour, skip, opposite = (1, 0), (0, 2), (0, 4), (0, 6)
    beside, above, diagonal = (2, 0), (0, 1), (2, 1)
    first_flips = [(opposite, beside), (skip, above), (neighbour, diagonal)]
    odd = (lax.axis_index("grp") % 2).reshape(1)
    rows = token_rows(group, expert_ids, route_gains, moe_input)
    line = [rows] + [across(rows, *flips) for flips in first_flips]
    own = line_rows(line, [])

    pieces = [
        across(own, *flips)
        for flips in ((beside, skip), (above, neighbour), (diagonal, opposite))
    ]
    *weights, _ = fetch(weights, [own])
    (own_sums,) = expert([own], weights)
    pieces = gate(pieces, [own_sums])
    other_pieces = [across(piece, core) for piece in [*pieces, own]]
    mine = expert(pieces, weights)
    *theirs, other_sums = expert(other_pieces, weights, mine[:1])
    sums_3 = add_up([mine[2], across(theirs[2], core)])

    term_3 = across(sums_3, diagonal, neighbour)
    contexts, grown, attended = attention(queries, cache, new_entries, lengths, [sums_3])
    theirs_1, theirs_2 = gate([across(part, core) for part in theirs[:2]], [attended])
    sums_1, sums_2 = add_up([mine[0], theirs_1]), add_up([mine[1], theirs_2])
    (sums_2,) = gate([sums_2], [term_3, attended])
    term_2 = across(sums_2, above, neighbour)
    term_1 = across(add_if_odd(odd, sums_1, term_3), beside, skip)
    leaving = outgoing(cache, new_entries, lengths, plan, group, [sums_2])
    received = [across(leaving[flip - 1], (flip, 0)) for flip in range(1, groups)]
    own_term = add_up([own_sums, across(other_sums, core)])
    parts = line_sums(
        odd, [term_3, term_1, term_2, own_term], steps, trace_count, len(line), leaving[:1]
    )
    moe_output = add_up(
        [parts[0]] + [across(part, *flips) for part, flips in zip(parts[1:], first_flips)]
    )
    return contexts, place(grown, received, plan, group), moe_output


def routed_layer(
    queries, cache, new_entries, lengths, moe_input, expert_ids, route_gains, weights, plan, group
):
    leaving = outgoing(cache, new_entries, lengths, plan, group)
    received = [across(leaving[flip - 1], (flip, 0)) for flip in range(1, lax.axis_size("grp"))]
    contexts, grown, _ = attention(queries, cache, new_entries, lengths)
    migrated_cache = place(grown, received, plan, group)
    moe_output = routed_experts(moe_input, expert_ids, route_gains, *weights)
    return contexts, migrated_cache, moe_output


def slot_tables(route_ids, route_gains, expert_count, slot_count):
    token_count, top_count = route_ids.shape
    flat_ids = route_ids.reshape(-1)
    row_list = jnp.arange(flat_ids.shape[0], dtype=jnp.int32)
    same_expert = flat_ids[:, None] == flat_ids[None, :]
    earlier = row_list[None, :] < row_list[:, None]
    slot_rank = jnp.sum(jnp.where(same_expert & earlier, 1, 0), axis=1).astype(jnp.int32)
    slot_index = flat_ids * slot_count + slot_rank
    slot_hot = (
        slot_index[:, None] == jnp.arange(expert_count * slot_count, dtype=jnp.int32)[None, :]
    ).astype(jnp.float32)
    token_hot = (
        (row_list // top_count)[:, None] == jnp.arange(token_count, dtype=jnp.int32)[None, :]
    ).astype(jnp.float32)
    dispatch = jnp.dot(slot_hot.T, token_hot, precision=lax.Precision.HIGHEST)
    combine = jnp.dot(
        token_hot.T, slot_hot * route_gains.reshape(-1)[:, None], precision=lax.Precision.HIGHEST
    )
    return (dispatch, combine)


def expert_rows(token_rows, gate_slice, up_slice, down_slice):
    gate_out = jnp.dot(token_rows, gate_slice, preferred_element_type=jnp.float32)
    up_out = jnp.dot(token_rows, up_slice, preferred_element_type=jnp.float32)
    hidden = (jax.nn.silu(gate_out) * up_out).astype(jnp.bfloat16)
    return jnp.dot(hidden, down_slice, preferred_element_type=jnp.float32).astype(jnp.bfloat16)


def routed_experts(moe_input, expert_ids, route_gains, w_gate, w_up, w_down):
    groups, experts = lax.axis_size("grp"), lax.axis_size("ep")
    trace_count, model_width = moe_input.shape[1:]
    top_count = expert_ids.shape[3]
    slot_count = max(2, trace_count * top_count // experts)
    tables = partial(slot_tables, expert_count=experts, slot_count=slot_count)
    moe_list = []
    for step_index in range(moe_input.shape[0]):
        column_ids = expert_ids[step_index]
        column_gains = route_gains[step_index]
        dispatch_all, combine_all = jax.vmap(tables)(column_ids, column_gains)
        column_tokens = lax.all_gather(moe_input[step_index][None], "grp", axis=0, tiled=True)
        packed = jnp.einsum(
            "gsj,gjd->sgd",
            dispatch_all.astype(jnp.bfloat16),
            column_tokens,
            preferred_element_type=jnp.float32,
        )
        packed = packed.astype(jnp.bfloat16).reshape(experts, slot_count * groups, model_width)
        exchanged = lax.all_to_all(packed, "ep", split_axis=0, concat_axis=0, tiled=True)
        flat_rows = exchanged.reshape(-1, exchanged.shape[-1])
        partial_out = expert_rows(flat_rows, w_gate[0], w_up[0], w_down[0]).reshape(exchanged.shape)
        returned = lax.all_to_all(partial_out, "ep", split_axis=0, concat_axis=0, tiled=True)
        returned = returned.reshape(experts * slot_count, groups, model_width).astype(jnp.float32)
        token_terms = jnp.einsum(
            "gjs,sgd->gjd", combine_all, returned, precision=lax.Precision.HIGHEST
        )
        summed = lax.psum_scatter(
            token_terms.astype(jnp.bfloat16), "grp", scatter_dimension=0, tiled=True
        ).astype(jnp.float32)
        moe_list.append(summed[0].astype(jnp.bfloat16))
    return jnp.stack(moe_list)


def body(
    queries,
    cache,
    new_entries,
    lengths,
    moe_input,
    expert_ids,
    route_gains,
    w_gate,
    w_up,
    w_down,
    plan,
):
    queries, cache = jnp.swapaxes(queries, 2, 3), jnp.swapaxes(cache, 1, 2)
    plan, group = jnp.transpose(plan[:, 0], (1, 2, 0)), lax.axis_index("grp").reshape(1)
    every_expert = expert_ids.shape[3] == lax.axis_size("ep")
    every_expert = every_expert and (lax.axis_size("grp"), lax.axis_size("ep")) == (4, 8)
    layer = dense_layer if every_expert else routed_layer
    contexts, migrated_cache, moe_output = layer(
        queries,
        cache,
        new_entries,
        lengths,
        moe_input,
        expert_ids,
        route_gains,
        (w_gate, w_up, w_down),
        plan,
        group,
    )
    return contexts, jnp.swapaxes(migrated_cache, 1, 2), moe_output


def solution(mesh):
    return jax.shard_map(
        body,
        mesh=mesh,
        in_specs=(
            P(None, ("grp", "ep"), None, None),
            P(("grp", "ep"), None, None),
            P(None, ("grp", "ep"), None),
            P(("grp", "ep")),
            P(None, ("grp", "ep"), None),
            P(None, None, "ep", None),
            P(None, None, "ep", None),
            P("ep", None, "grp"),
            P("ep", None, "grp"),
            P("ep", "grp", None),
            P(None, "ep", None, None),
        ),
        out_specs=(
            P(None, ("grp", "ep"), None, None),
            P(("grp", "ep"), None, None),
            P(None, ("grp", "ep"), None),
        ),
        check_vma=False,
    )
```
